32 devices in a mesh: clips: 8 (over z, x), tp: 4 (over y, core).
Axes of the slice: x: 2, y: 2, z: 4, core: 2. Of those that a mesh axis runs over, the one named last changes fastest.
Arguments:
- tokens: bfloat16 [64, 256, 768], P('clips', 'tp'), may hold values from -6 to 6
- tubelet_index: int32 [64, 256], P('clips', 'tp'), may hold values from 0 to 2559, as said below
- visible_count: int32 [64], P('clips'), may hold values from 80 to 256, as said below
- norm1_gain: float32 [768], replicated, may hold values from 0.5 to 1.5
- norm1_bias: float32 [768], replicated, may hold values from -1.5 to 1.5
- qkv_weight: bfloat16 [768, 3, 768], P(None, None, 'tp'), may hold values from -0.21875 to 0.21875
- qv_bias: float32 [2, 768], P(None, 'tp'), may hold values from -1 to 1
- proj_weight: bfloat16 [768, 768], P('tp'), may hold values from -1.75 to 1.75
- proj_bias: float32 [768], replicated, may hold values from -1.5 to 1.5
- norm2_gain: float32 [768], replicated, may hold values from 0.5 to 1.5
- norm2_bias: float32 [768], replicated, may hold values from -1.5 to 1.5
- up_weight: bfloat16 [768, 3072], P(None, 'tp'), may hold values from -0.21875 to 0.21875
- up_bias: float32 [3072], P('tp'), may hold values from -1.5 to 1.5
- down_weight: bfloat16 [3072, 768], P('tp'), may hold values from -0.109375 to 0.109375
- down_bias: float32 [768], replicated, may hold values from -1.5 to 1.5
- out_grad: bfloat16 [64, 256, 768], P('clips', 'tp'), may hold values from -6 to 6
Outputs:
- layer_out: float32 [64, 256, 768], P('clips', 'tp')
- in_grad: float32 [64, 256, 768], P('clips', 'tp')
- norm1_gain_grad: float32 [768], replicated
- norm1_bias_grad: float32 [768], replicated
- qkv_weight_grad: float32 [768, 3, 768], P(None, None, 'tp')
- qv_bias_grad: float32 [2, 768], P(None, 'tp')
- proj_weight_grad: float32 [768, 768], P('tp')
- proj_bias_grad: float32 [768], replicated
- norm2_gain_grad: float32 [768], replicated
- norm2_bias_grad: float32 [768], replicated
- up_weight_grad: float32 [768, 3072], P(None, 'tp')
- up_bias_grad: float32 [3072], P('tp')
- down_weight_grad: float32 [3072, 768], P('tp')
- down_bias_grad: float32 [768], replicated
The draws below stay inside these ranges and needn't reach their ends.
Inputs may be any that keep to these rules, and one draw needn't show every extreme that they name: `visible_count`: each clip has 80, 160 or 256 visible tubelets, in its first slots; some clip has 256. `tubelet_index`: slot j of a clip holds an index from 10 * j to 10 * j + 9.
All inputs are finite; a program needn't handle non-finite values.
Results may differ from the reference program's by a relative error of at most 0.019.
Values may be sent and summed in bfloat16 or wider, within the bound.
A program may use at most 128 MiB of HBM per device.

```python
import math
import jax
import jax.numpy as jnp
from jax import lax

D = 768
HD = 64
FF = 3072
CLIPS_DEV = 8
SLOT = 256
CLIPS = 64
N_TP = 4


def draw_visible_count(key, part):
    key = jax.random.fold_in(key, 11)
    first, second = jax.random.split(key)
    level = jax.random.randint(first, (CLIPS,), 0, 3)
    chosen = jax.random.randint(second, (), 0, CLIPS)
    level = jnp.where(jnp.arange(CLIPS) == chosen, 2, level)
    counts = jnp.where(level == 0, SLOT * 5 // 16, jnp.where(level == 1, SLOT * 5 // 8, SLOT))
    return counts.astype(jnp.int32)


def draw_tubelet_index(key, part):
    key = jax.random.fold_in(key, 23)
    offset = jax.random.randint(key, (CLIPS, SLOT), 0, 10)
    return (10 * jnp.arange(SLOT, dtype=jnp.int32)[None, :] + offset).astype(jnp.int32)


def block_levels(stream_key, extent, cuts, least, largest):
    def one(position, blocks):
        heights = jax.random.uniform(jax.random.fold_in(jax.random.fold_in(stream_key, 6), position), (blocks,), jnp.float32, least / len(cuts), largest / len(cuts))
        return jnp.repeat(jnp.exp(heights), extent[position] // blocks).reshape((-1,) + (1,) * (len(extent) - position - 1))

    level = one(*cuts[0])
    for cut in cuts[1:]:
        level = level * one(*cut)
    return level


def bell_draw(key, dims, deviation, reach, cuts=(), held_as=jnp.bfloat16):
    array = deviation * jax.random.normal(key, dims, jnp.float32)
    if cuts:
        array = array * block_levels(key, dims, cuts, -0.22, 0.18)
    return jnp.clip(array, -reach, reach).astype(held_as)


def setup_inputs(seed: int = 0) -> dict:
    streams_of = jax.random.split(jax.random.key(seed), 17)
    return {
        "tokens": bell_draw(streams_of[0], (CLIPS, SLOT, D), 1.0, 6.0, ((0, 8), (1, 4))),
        "tubelet_index": draw_tubelet_index(jax.random.fold_in(streams_of[16], 71), 0),
        "visible_count": draw_visible_count(jax.random.fold_in(streams_of[16], 71), 0),
        "norm1_gain": jnp.clip(1.0 + 0.1 * jax.random.normal(streams_of[3], (D,), jnp.float32), 0.5, 1.5),
        "norm1_bias": bell_draw(streams_of[4], (D,), 0.3, 1.5, (), jnp.float32),
        "qkv_weight": bell_draw(streams_of[5], (D, 3, D), D ** -0.5, 0.21875, ((2, 4),)),
        "qv_bias": bell_draw(streams_of[6], (2, D), 0.2, 1.0, ((1, 4),), jnp.float32),
        "proj_weight": bell_draw(streams_of[7], (D, D), (D // 64) ** -0.5, 1.75, ((0, 4),)),
        "proj_bias": bell_draw(streams_of[8], (D,), 0.3, 1.5, (), jnp.float32),
        "norm2_gain": jnp.clip(1.0 + 0.1 * jax.random.normal(streams_of[9], (D,), jnp.float32), 0.5, 1.5),
        "norm2_bias": bell_draw(streams_of[10], (D,), 0.3, 1.5, (), jnp.float32),
        "up_weight": bell_draw(streams_of[11], (D, FF), D ** -0.5, 0.21875, ((1, 4),)),
        "up_bias": bell_draw(streams_of[12], (FF,), 0.3, 1.5, ((0, 4),), jnp.float32),
        "down_weight": bell_draw(streams_of[13], (FF, D), FF ** -0.5, 0.109375, ((0, 4),)),
        "down_bias": bell_draw(streams_of[14], (D,), 0.3, 1.5, (), jnp.float32),
        "out_grad": bell_draw(streams_of[15], (CLIPS, SLOT, D), 1.0, 6.0, ((0, 8), (1, 4))),
    }


HIGHEST = lax.Precision.HIGHEST
EPSILON = 1e-06
NEGATIVE = -1000000000.0

@jax.custom_vjp
def low(v):
    return lax.optimization_barrier(v.astype(jnp.bfloat16)).astype(jnp.float32)

@jax.custom_vjp
def low_back(v):
    return v

def low_keep(v):
    return (low(v), None)

def low_pass(kept, grad):
    return (grad,)

def back_keep(v):
    return (v, None)

def back_low(kept, grad):
    return (low(grad),)
low.defvjp(low_keep, low_pass)
low_back.defvjp(back_keep, back_low)

def matmul(left, right):
    return jnp.einsum('...i,ij->...j', left, right, precision=HIGHEST)

def positions(index):
    half = D // 2
    freq = jnp.exp(-math.log(10000.0) * jnp.arange(half, dtype=jnp.float32) / half)
    angle = index.astype(jnp.float32)[..., None] * freq
    return jnp.concatenate([jnp.sin(angle), jnp.cos(angle)], axis=-1)

def normalize(stream, gain, bias):
    center = stream - lax.optimization_barrier(jnp.mean(stream, axis=-1, keepdims=True))
    spread = lax.optimization_barrier(jnp.mean(center * center, axis=-1, keepdims=True))
    return center * lax.rsqrt(spread + EPSILON) * gain + bias

def layer(params, stream, keep):
    gain_one, bias_one, qkv_w, qv_b, proj_w, proj_b, gain_two, bias_two, up_w, up_b, down_w, down_b = params
    width = D // N_TP
    hidden = FF // N_TP
    per_group = width // HD
    scale = HD ** (-0.5)
    count = stream.shape[0]
    first_norm = low(normalize(stream, gain_one, bias_one))
    attention = jnp.zeros_like(stream)
    for group in range(N_TP):
        columns = slice(group * width, (group + 1) * width)
        inputs = low_back(first_norm)
        queries = low_back(low(matmul(inputs, qkv_w[:, 0, columns]) + qv_b[0, columns]))
        key_rows = low_back(low(matmul(inputs, qkv_w[:, 1, columns])))
        value_rows = low_back(low(matmul(inputs, qkv_w[:, 2, columns]) + qv_b[1, columns]))
        queries = queries.reshape(count, SLOT, per_group, HD)
        key_rows = key_rows.reshape(count, SLOT, per_group, HD)
        value_rows = value_rows.reshape(count, SLOT, per_group, HD)
        scores = low_back(jnp.einsum('cqhd,ckhd->chqk', queries, key_rows, precision=HIGHEST) * scale)
        scores = jnp.where(keep[:, None, None, :], scores, NEGATIVE)
        row_max = lax.optimization_barrier(jnp.max(scores, axis=-1, keepdims=True))
        raised = jnp.exp(scores - row_max)
        probs = raised / lax.optimization_barrier(jnp.sum(raised, axis=-1, keepdims=True))
        mixed = jnp.einsum('chqk,ckhd->cqhd', low(probs), value_rows, precision=HIGHEST)
        mixed = low_back(low(mixed.reshape(count, SLOT, width)))
        attention = attention + low(matmul(mixed, proj_w[columns, :]))
    attention = low_back(attention + proj_b)
    middle = stream + attention
    second_norm = low(normalize(middle, gain_two, bias_two))
    feedforward = jnp.zeros_like(stream)
    for group in range(N_TP):
        columns = slice(group * hidden, (group + 1) * hidden)
        inputs = low_back(second_norm)
        pre_act = low_back(matmul(inputs, up_w[:, columns]) + up_b[columns])
        activated = low(jax.nn.gelu(pre_act, approximate=False))
        feedforward = feedforward + low(matmul(activated, down_w[columns, :]))
    feedforward = low_back(feedforward + down_b)
    return middle + feedforward

def reference(tokens, tubelet_index, visible_count, norm1_gain, norm1_bias, qkv_weight, qv_bias, proj_weight, proj_bias, norm2_gain, norm2_bias, up_weight, up_bias, down_weight, down_bias, out_grad):
    params = tuple((item.astype(jnp.float32) for item in (norm1_gain, norm1_bias, qkv_weight, qv_bias, proj_weight, proj_bias, norm2_gain, norm2_bias, up_weight, up_bias, down_weight, down_bias)))
    stream = tokens.astype(jnp.float32) + positions(tubelet_index)
    keep = jnp.arange(SLOT, dtype=jnp.int32)[None, :] < visible_count[:, None]
    cotangent = out_grad.astype(jnp.float32)
    blocks = CLIPS // CLIPS_DEV
    stream_blocks = stream.reshape(blocks, CLIPS_DEV, SLOT, D)
    keep_blocks = keep.reshape(blocks, CLIPS_DEV, SLOT)
    cotangent_blocks = cotangent.reshape(blocks, CLIPS_DEV, SLOT, D)

    def advance(total, item):
        block_stream, block_keep, block_cotangent = item
        result, pull = jax.vjp(lambda weights, values: layer(weights, values, block_keep), params, block_stream)
        param_grads, stream_grad = pull(block_cotangent)
        total = jax.tree.map(lambda left, right: left + right, total, param_grads)
        return (total, (result, stream_grad))
    zeros = jax.tree.map(jnp.zeros_like, params)
    total, (results, stream_grads) = lax.scan(advance, zeros, (stream_blocks, keep_blocks, cotangent_blocks))
    layer_out = results.reshape(CLIPS, SLOT, D)
    in_grad = stream_grads.reshape(CLIPS, SLOT, D)
    return (layer_out, in_grad, total[0], total[1], total[2], total[3], total[4], total[5], total[6], total[7], total[8], total[9], total[10], total[11])
```

```python
import functools
import math

import jax
import jax.numpy as jnp
from jax import lax
from jax.experimental import pallas as pl
from jax.experimental.pallas import tpu as pltpu
from jax.sharding import PartitionSpec as P

HD = 64
EPSILON = 1e-06
NEGATIVE = -1000000000.0
BF = jnp.bfloat16
F32 = jnp.float32
MESH = pl.DeviceIdType.MESH
VMEM_LIMIT = 60 * 2**20
CHUNK = 128
F_BLOCK = 256


def flip(value, weight):
    return value + weight - 2 * weight * lax.rem(lax.div(value, weight), 2)


def bit_of(value, weight):
    return lax.rem(lax.div(value, weight), 2)


def greet(targets):
    barrier = pltpu.get_barrier_semaphore()
    for target in targets:
        pl.semaphore_signal(barrier, inc=1, device_id=target, device_id_type=MESH)
    pl.semaphore_wait(barrier, len(targets))


def gather_kernel(n_clips, blocks, w_ref, tok_ref, og_ref, wb_ref, tokb_ref, ogb_ref,
                  y_sem, h_sem, f_sem, core_sem, t_sem, local_sem):
    c = lax.axis_index("clips")
    t = lax.axis_index("tp")
    n_tp = wb_ref.shape[0]
    core = (c, flip(t, 1))
    side = (c, flip(t, 2))
    across = (flip(c, 1), t)
    along = (flip(c, 2), t)
    others = [(c, lax.rem(t + k, n_tp)) for k in range(1, n_tp)]
    greet(others + [across, along])
    own = t
    far = flip(t, 2)
    b0, b1 = bit_of(c, 1), bit_of(c, 2)
    per = tok_ref.shape[0] // n_tp
    slots = tok_ref.shape[1]
    copies = []
    own_copies = []
    for src, dst, s in ((tok_ref, tokb_ref, 0), (og_ref, ogb_ref, 1)):
        mine = pltpu.make_async_copy(src.at[pl.ds(t * per, per)],
                                     dst.at[:, pl.ds(t * slots, slots)], local_sem.at[s])
        mine.start()
        own_copies.append(mine)
    for k, target in enumerate(others):
        copy = pltpu.make_async_remote_copy(
            src_ref=tok_ref.at[pl.ds(target[1] * per, per)],
            dst_ref=tokb_ref.at[:, pl.ds(t * slots, slots)],
            send_sem=t_sem.at[0, 0, k], recv_sem=t_sem.at[0, 1, k],
            device_id=target, device_id_type=MESH)
        copy.start()
        copies.append(copy)

    def remote(shard, start, rows, sem, index, target):
        copy = pltpu.make_async_remote_copy(
            src_ref=wb_ref.at[shard, pl.ds(start, rows)],
            dst_ref=wb_ref.at[shard, pl.ds(start, rows)],
            send_sem=sem.at[(0, *index)], recv_sem=sem.at[(1, *index)],
            device_id=target, device_id_type=MESH)
        copy.start()
        copies.append(copy)
        return copy

    wb_ref[own] = w_ref[...]
    quarter = b1 * 2 + b0
    steps = []
    y_copies = []
    for i, (base, rows) in enumerate(blocks):
        q = rows // 4
        y_copies.append(remote(own, base + quarter * q, q, y_sem, (i,), side))
    for k, target in enumerate(others):
        copy = pltpu.make_async_remote_copy(
            src_ref=og_ref.at[pl.ds(target[1] * per, per)],
            dst_ref=ogb_ref.at[:, pl.ds(t * slots, slots)],
            send_sem=t_sem.at[1, 0, k], recv_sem=t_sem.at[1, 1, k],
            device_id=target, device_id_type=MESH)
        copy.start()
        copies.append(copy)
    core_own = [remote(own, base, rows, core_sem, (0, i), core) for i, (base, rows) in enumerate(blocks)]
    for i, (base, rows) in enumerate(blocks):
        q, h = rows // 4, rows // 8
        y_copies[i].wait_recv()
        z_a = remote(far, base + quarter * q, h, h_sem, (0, i), along)
        x_b = remote(far, base + quarter * q + h, h, h_sem, (1, i), across)
        steps.append((z_a, x_b))
    finals = []
    for i, (base, rows) in enumerate(blocks):
        q, h = rows // 4, rows // 8
        z_a, x_b = steps[i]
        via_z = (1 - b1) * 2 + b0
        via_x = b1 * 2 + (1 - b0)
        x_a0 = remote(far, base + quarter * q, h, f_sem, (0, i), across)
        z_b0 = remote(far, base + quarter * q + h, h, f_sem, (1, i), along)
        z_a.wait_recv()
        x_a1 = remote(far, base + via_z * q, h, f_sem, (2, i), across)
        x_b.wait_recv()
        z_b1 = remote(far, base + via_x * q + h, h, f_sem, (3, i), along)
        finals.append((x_a0, z_b0, x_a1, z_b1))
    core_far = []
    for i, (base, rows) in enumerate(blocks):
        for copy in finals[i]:
            copy.wait_recv()
        core_far.append(remote(far, base, rows, core_sem, (1, i), core))
    for copy in core_own + core_far:
        copy.wait_recv()
    for s in (0, 1):
        for k in range(n_tp - 1):
            copies_of = (tokb_ref, ogb_ref)[s]
            src = (tok_ref, og_ref)[s]
            pltpu.make_async_remote_copy(
                src_ref=src.at[pl.ds(0, per)],
                dst_ref=copies_of.at[:, pl.ds(lax.rem(t + n_tp - k - 1, n_tp) * slots, slots)],
                send_sem=t_sem.at[s, 0, k], recv_sem=t_sem.at[s, 1, k],
                device_id=others[k], device_id_type=MESH).wait_recv()
    for copy in own_copies:
        copy.wait()
    for copy in copies:
        copy.wait_send()


def gather_call(n_clips, w, tok, og, n_tp, blocks):
    rows, width = w.shape
    count, slots, wide = tok.shape
    nb = len(blocks)
    spec = pl.BlockSpec(memory_space=pltpu.VMEM)
    return pl.pallas_call(
        functools.partial(gather_kernel, n_clips, blocks),
        out_shape=(
            jax.ShapeDtypeStruct((n_tp, rows, width), BF),
            jax.ShapeDtypeStruct((count // n_tp, slots * n_tp, wide), BF),
            jax.ShapeDtypeStruct((count // n_tp, slots * n_tp, og.shape[2]), BF),
        ),
        in_specs=[spec] * 3,
        out_specs=(spec,) * 3,
        scratch_shapes=[
            pltpu.SemaphoreType.DMA((2, nb)),
            pltpu.SemaphoreType.DMA((2, 2, nb)),
            pltpu.SemaphoreType.DMA((2, 4, nb)),
            pltpu.SemaphoreType.DMA((2, 2, nb)),
            pltpu.SemaphoreType.DMA((2, 2, n_tp - 1)),
            pltpu.SemaphoreType.DMA((2,)),
        ],
        compiler_params=pltpu.CompilerParams(
            collective_id=0, has_side_effects=True, vmem_limit_bytes=VMEM_LIMIT),
        name="gather_weights",
    )(w, tok, og)


def reduce_stages(n_clips, chunk):
    stages = []
    rows = chunk
    weight = 1
    while weight < n_clips:
        if rows >= 32:
            rows //= 2
            stages.append((weight, rows, True))
        else:
            stages.append((weight, rows, False))
        weight *= 2
    return stages


def reduce_kernel(n_clips, stages, lags, g_ref, small_ref, part_ref, out_ref, smallo_ref, parto_ref,
                  core_buf, side_buf, *rest):
    bufs = rest[: len(stages)]
    small_buf, sem, small_sem, p_sem, local_sem = rest[len(stages):]
    c = lax.axis_index("clips")
    t = lax.axis_index("tp")
    n_tp = 4
    k, u = bit_of(t, 1), bit_of(t, 2)
    core = (c, flip(t, 1))
    side = (c, flip(t, 2))
    others = [(c, lax.rem(t + i, n_tp)) for i in range(1, n_tp)]
    peers = [(flip(c, weight), t) for weight, _, _ in stages]
    greet(others + peers)
    per = part_ref.shape[1]
    n_chunks = g_ref.shape[2] // CHUNK
    part_copies = []
    slots = parto_ref.shape[1]
    for i, target in enumerate(others):
        copy = pltpu.make_async_remote_copy(
            src_ref=part_ref.at[:, pl.ds(target[1] * slots, slots)],
            dst_ref=parto_ref.at[pl.ds(t * per_clips(part_ref), per_clips(part_ref))],
            send_sem=p_sem.at[0, i], recv_sem=p_sem.at[1, i], device_id=target, device_id_type=MESH)
        copy.start()
        part_copies.append(copy)
    mine = pltpu.make_async_copy(part_ref.at[:, pl.ds(t * slots, slots)],
                                 parto_ref.at[pl.ds(t * per_clips(part_ref), per_clips(part_ref))], local_sem)
    mine.start()

    smallo_ref[...] = small_ref[...]

    def kept(stage, chunk):
        start = chunk * CHUNK
        for weight, rows, halving in stages[:stage]:
            if halving:
                start = start + bit_of(c, weight) * rows
        return start

    def sent(stage, chunk):
        weight, rows, halving = stages[stage]
        start = kept(stage, chunk)
        if halving:
            return start + (1 - bit_of(c, weight)) * rows
        return start

    n_rs = 2 + len(stages)
    halvings = [i for i, s in enumerate(stages) if s[2]]
    gathers = list(reversed(halvings))
    n_all = n_rs + len(gathers)

    def copy_of(stage, chunk):
        chunk = jnp.int32(chunk) if isinstance(chunk, int) else chunk
        if stage == 0:
            src = g_ref.at[:, 1 - k, pl.ds(chunk * CHUNK, CHUNK)]
            dst = core_buf.at[:, pl.ds(chunk * CHUNK, CHUNK)]
            target = core
        elif stage == 1:
            src = core_buf.at[1 - u, pl.ds(chunk * CHUNK, CHUNK)]
            dst = side_buf.at[pl.ds(chunk * CHUNK, CHUNK)]
            target = side
        elif stage < n_rs:
            i = stage - 2
            _, rows, _ = stages[i]
            src = side_buf.at[pl.ds(pl.multiple_of(sent(i, chunk), 16), rows)]
            dst = bufs[i].at[pl.ds(pl.multiple_of(chunk * rows, 16), rows)]
            target = peers[i]
        else:
            i = gathers[stage - n_rs]
            _, rows, _ = stages[i]
            start = pl.multiple_of(kept(i + 1, chunk), 16)
            src = out_ref.at[pl.ds(start, rows)]
            dst = out_ref.at[pl.ds(start, rows)]
            target = peers[i]
        return pltpu.make_async_remote_copy(
            src_ref=src, dst_ref=dst, send_sem=sem.at[0, stage, chunk], recv_sem=sem.at[1, stage, chunk],
            device_id=target, device_id_type=MESH)

    def add(a, b):
        return (a.astype(F32) + b.astype(F32)).astype(BF)

    def finish(stage, chunk):
        copy_of(stage, chunk).wait_recv()
        rows = pl.ds(pl.multiple_of(chunk * CHUNK, CHUNK), CHUNK)
        if stage == 0:
            for side_of in (0, 1):
                core_buf[side_of, rows] = add(g_ref[side_of, k, rows], core_buf[side_of, rows])
        elif stage == 1:
            side_buf[rows] = add(core_buf[u, rows], side_buf[rows])
        elif stage < n_rs:
            i = stage - 2
            _, size, halving = stages[i]
            keep_rows = pl.ds(pl.multiple_of(kept(i + 1, chunk), 16), size)
            buf_rows = pl.ds(pl.multiple_of(chunk * size, 16), size)
            if not halving:
                copy_of(stage, chunk).wait_send()
            result = out_ref if stage == n_rs - 1 else side_buf
            result[keep_rows] = add(side_buf[keep_rows], bufs[i][buf_rows])

    starts = [0]
    for lag in lags[:n_all]:
        starts.append(starts[-1] + lag)

    def tick(i, _):
        for stage in reversed(range(n_all + 1)):
            chunk = i - starts[stage]

            @pl.when((chunk >= 0) & (chunk < n_chunks))
            def _():
                if stage > 0:
                    finish(stage - 1, chunk)
                if stage < n_all:
                    copy_of(stage, chunk).start()
        return 0

    lax.fori_loop(0, n_chunks + starts[-1], tick, 0)

    targets = [core, side] + peers
    for i, target in enumerate(targets):
        copy = pltpu.make_async_remote_copy(
            src_ref=smallo_ref, dst_ref=small_buf.at[i], send_sem=small_sem.at[0, i],
            recv_sem=small_sem.at[1, i], device_id=target, device_id_type=MESH)
        copy.start()
        copy.wait()
        smallo_ref[...] += small_buf[i]

    for i in range(n_tp - 1):
        owner = lax.rem(t + n_tp - i - 1, n_tp)
        pltpu.make_async_remote_copy(
            src_ref=part_ref.at[:, pl.ds(0, slots)],
            dst_ref=parto_ref.at[pl.ds(owner * per_clips(part_ref), per_clips(part_ref))],
            send_sem=p_sem.at[0, i], recv_sem=p_sem.at[1, i], device_id=others[i],
            device_id_type=MESH).wait_recv()
    mine.wait()
    for copy in part_copies:
        copy.wait_send()

    def drain(chunk, _):
        for stage in range(n_all):
            if 2 <= stage < n_rs and not stages[stage - 2][2]:
                continue
            copy_of(stage, chunk).wait_send()
        return 0

    lax.fori_loop(0, n_chunks, drain, 0)


def per_clips(part_ref):
    return part_ref.shape[0]


def reduce_call(n_clips, g, small, part, n_tp):
    _, _, rows, width = g.shape
    n_chunks = rows // CHUNK
    stages = reduce_stages(n_clips, CHUNK)
    n_all = 2 + len(stages) + sum(1 for s in stages if s[2])
    lags = [1, 2, 2] + [1] * n_all
    spec = pl.BlockSpec(memory_space=pltpu.VMEM)
    here, slots, wide = part.shape
    return pl.pallas_call(
        functools.partial(reduce_kernel, n_clips, stages, lags),
        out_shape=(
            jax.ShapeDtypeStruct((rows, width), BF),
            jax.ShapeDtypeStruct(small.shape, F32),
            jax.ShapeDtypeStruct((here * n_tp, slots // n_tp, wide), BF),
        ),
        in_specs=[spec] * 3,
        out_specs=(spec,) * 3,
        scratch_shapes=[
            pltpu.VMEM((2, rows, width), BF),
            pltpu.VMEM((rows, width), BF),
            *[pltpu.VMEM((n_chunks * size, width), BF) for _, size, _ in stages],
            pltpu.VMEM((2 + len(stages), *small.shape), F32),
            pltpu.SemaphoreType.DMA((2, n_all, n_chunks)),
            pltpu.SemaphoreType.DMA((2, 2 + len(stages))),
            pltpu.SemaphoreType.DMA((2, n_tp - 1)),
            pltpu.SemaphoreType.DMA,
        ],
        input_output_aliases={},
        compiler_params=pltpu.CompilerParams(
            collective_id=1, has_side_effects=True, vmem_limit_bytes=VMEM_LIMIT),
        name="reduce_grads",
    )(g, small, part)


def normalize(stream, gain, bias):
    center = stream - jnp.mean(stream, axis=-1, keepdims=True)
    spread = jnp.mean(center * center, axis=-1, keepdims=True)
    return center * lax.rsqrt(spread + EPSILON) * gain + bias


def gelu_exact(value):
    return jax.nn.gelu(value, approximate=False)


def per_device(n_clips, n_tp, tokens, tubelet_index, visible_count, norm1_gain, norm1_bias, qkv_weight, qv_bias,
               proj_weight, proj_bias, norm2_gain, norm2_bias, up_weight, up_bias, down_weight, down_bias, out_grad):
    count, rows, features = tokens.shape
    slots = rows * n_tp
    width = qkv_weight.shape[2]
    hidden = up_weight.shape[1]
    here = count // n_tp
    t = lax.axis_index("tp")
    scale = HD ** -0.5
    qkv_t = jnp.transpose(qkv_weight, (1, 2, 0)).reshape(3 * width, features)
    up_t = up_weight.T
    nf = hidden // F_BLOCK
    pieces = [proj_weight, qkv_t]
    for j in range(nf):
        pieces += [up_t[j * F_BLOCK:(j + 1) * F_BLOCK], down_weight[j * F_BLOCK:(j + 1) * F_BLOCK]]
    shard = jnp.concatenate(pieces, axis=0)
    a_rows = 4 * width
    blocks = [(0, a_rows)] + [(a_rows + 2 * F_BLOCK * j, 2 * F_BLOCK) for j in range(nf)]
    hi = (tubelet_index // 64).astype(BF)[..., None]
    lo = (tubelet_index % 64).astype(BF)[..., None]
    lane = jnp.arange(128)[None, None, :]
    extra = jnp.where(lane == 0, hi, jnp.where(lane == 1, lo, jnp.zeros((), BF)))
    packed_tok = jnp.concatenate([tokens, extra], axis=-1)
    weights, tok, og = gather_call(n_clips, shard, packed_tok, out_grad, n_tp, blocks)

    index = tok[..., features].astype(F32) * 64 + tok[..., features + 1].astype(F32)
    half = features // 2
    freq = jnp.exp(-math.log(10000.0) * jnp.arange(half, dtype=F32) / half)
    angle = index[..., None] * freq
    stream = tok[..., :features].astype(F32) + jnp.concatenate([jnp.sin(angle), jnp.cos(angle)], axis=-1)
    visible = lax.dynamic_slice(visible_count, (t * here,), (here,))
    keep = jnp.arange(slots, dtype=jnp.int32)[None, :] < visible[:, None]
    proj = weights[:, :width].reshape(features, features)
    qkv = weights[:, width:a_rows].reshape(n_tp, 3, width, features)
    ffn = weights[:, a_rows:].reshape(n_tp, nf, 2, F_BLOCK, features)
    up = ffn[:, :, 0].reshape(n_tp * hidden, features)
    down = ffn[:, :, 1].reshape(n_tp * hidden, features)
    biases = lax.all_gather(jnp.concatenate([qv_bias.reshape(-1), up_bias]), "tp", axis=0, tiled=False)
    qv_full = biases[:, : 2 * width].reshape(n_tp, 2, width)
    up_b = biases[:, 2 * width:].reshape(-1)

    first = normalize(stream, norm1_gain, norm1_bias).astype(BF)
    packed = jnp.einsum("csd,tjwd->jcstw", first, qkv, preferred_element_type=F32)
    heads = features // HD

    def split(x):
        return x.astype(BF).reshape(here, slots, heads, HD)
    queries = split(packed[0] + qv_full[:, 0])
    keys = split(packed[1])
    values = split(packed[2] + qv_full[:, 1])
    scores = jnp.einsum("cqhd,ckhd->chqk", queries, keys, preferred_element_type=F32) * scale
    scores = jnp.where(keep[:, None, None, :], scores, NEGATIVE)
    probs_full = jax.nn.softmax(scores, axis=-1)
    probs = probs_full.astype(BF)
    mixed = jnp.einsum("chqk,ckhd->cqhd", probs, values, preferred_element_type=F32).astype(BF).reshape(here, slots, features)
    attention = jnp.einsum("csw,wd->csd", mixed, proj, preferred_element_type=F32) + proj_bias
    middle = stream + attention
    second = normalize(middle, norm2_gain, norm2_bias).astype(BF)
    pre_act = jnp.einsum("csd,fd->csf", second, up, preferred_element_type=F32) + up_b
    activated, pull_act = jax.vjp(gelu_exact, pre_act)
    activated = activated.astype(BF)
    result = middle + jnp.einsum("csf,fd->csd", activated, down, preferred_element_type=F32) + down_bias

    down_grad = jnp.einsum("csf,csd->fd", activated, og, preferred_element_type=F32).astype(BF)
    down_bias_grad = jnp.sum(og.astype(F32), axis=(0, 1))
    act_grad = jnp.einsum("csd,fd->csf", og, down, preferred_element_type=F32)
    pre_grad = pull_act(act_grad)[0].astype(BF)
    up_grad = jnp.einsum("csf,csd->fd", pre_grad, second, preferred_element_type=F32).astype(BF)
    up_bias_grad = jnp.sum(pre_grad.astype(F32), axis=(0, 1))
    second_grad = jnp.einsum("csf,fd->csd", pre_grad, up, preferred_element_type=F32)
    _, pull_two = jax.vjp(normalize, middle, norm2_gain, norm2_bias)
    middle_part, gain_two_grad, bias_two_grad = pull_two(second_grad)
    middle_grad = og.astype(F32) + middle_part
    branch = middle_grad.astype(BF)
    proj_bias_grad = jnp.sum(branch.astype(F32), axis=(0, 1))
    proj_grad = jnp.einsum("csw,csd->wd", mixed, branch, preferred_element_type=F32).astype(BF)
    mixed_grad = jnp.einsum("csd,wd->csw", branch, proj, preferred_element_type=F32)
    mixed_grad = mixed_grad.astype(BF).reshape(here, slots, heads, HD)
    value_grad = jnp.einsum("chqk,cqhd->ckhd", probs, mixed_grad, preferred_element_type=F32).astype(BF)
    prob_grad = jnp.einsum("cqhd,ckhd->chqk", mixed_grad, values, preferred_element_type=F32)
    score_grad = probs_full * (prob_grad - jnp.sum(probs_full * prob_grad, axis=-1, keepdims=True))
    score_grad = score_grad.astype(BF)
    query_grad = (jnp.einsum("chqk,ckhd->cqhd", score_grad, keys, preferred_element_type=F32) * scale).astype(BF)
    key_grad = (jnp.einsum("chqk,cqhd->ckhd", score_grad, queries, preferred_element_type=F32) * scale).astype(BF)
    packed_grad = jnp.stack([query_grad, key_grad, value_grad]).reshape(3, here, slots, n_tp, width)
    qkv_grad = jnp.einsum("jcstw,csd->tjwd", packed_grad, first, preferred_element_type=F32).astype(BF)
    qb = jnp.sum(query_grad.astype(F32), axis=(0, 1)).reshape(features)
    vb = jnp.sum(value_grad.astype(F32), axis=(0, 1)).reshape(features)
    first_grad = jnp.einsum("jcstw,tjwd->csd", packed_grad, qkv, preferred_element_type=F32)
    _, pull_one = jax.vjp(normalize, stream, norm1_gain, norm1_bias)
    stream_part, gain_one_grad, bias_one_grad = pull_one(first_grad)
    in_grad = middle_grad + stream_part

    grads = jnp.concatenate([
        proj_grad.reshape(n_tp, width, features),
        qkv_grad.reshape(n_tp, 3 * width, features),
        jnp.stack([up_grad.reshape(n_tp, nf, F_BLOCK, features), down_grad.reshape(n_tp, nf, F_BLOCK, features)], axis=2)
        .reshape(n_tp, 2 * hidden, features),
    ], axis=1).reshape(2, 2, -1, features)
    small = jnp.concatenate([
        jnp.stack([gain_one_grad, bias_one_grad, gain_two_grad, bias_two_grad, proj_bias_grad, down_bias_grad, qb, vb]),
        up_bias_grad.reshape(-1, features),
        jnp.zeros((8 - n_tp * hidden // features, features), F32)], axis=0)
    part = jnp.concatenate([result, in_grad], axis=-1).astype(BF)
    total, vectors, rows_back = reduce_call(n_clips, grads, small, part, n_tp)

    total = total.astype(F32)
    ffn_grad = total[a_rows:].reshape(nf, 2, F_BLOCK, features)
    qkv_out = jnp.transpose(total[width:a_rows].reshape(3, width, features), (2, 0, 1))
    qv_out = lax.dynamic_slice(vectors[6:8], (0, t * width), (2, width))
    up_bias_out = lax.dynamic_slice(vectors[8:].reshape(-1), (t * hidden,), (hidden,))
    return (
        rows_back[..., :features].astype(F32),
        rows_back[..., features:].astype(F32),
        vectors[0],
        vectors[1],
        qkv_out,
        qv_out,
        total[:width],
        vectors[4],
        vectors[2],
        vectors[3],
        ffn_grad[:, 0].reshape(hidden, features).T,
        up_bias_out,
        ffn_grad[:, 1].reshape(hidden, features),
        vectors[5],
    )


def solution(mesh):
    placed = (
        P("clips", "tp", None), P("clips", "tp"), P("clips"), P(), P(), P(None, None, "tp"), P(None, "tp"),
        P("tp", None), P(), P(), P(), P(None, "tp"), P("tp"), P("tp", None), P(), P("clips", "tp", None),
    )
    return jax.shard_map(
        functools.partial(per_device, mesh.shape["clips"], mesh.shape["tp"]),
        mesh=mesh,
        in_specs=placed,
        out_specs=(
            P("clips", "tp", None), P("clips", "tp", None), P(), P(), P(None, None, "tp"), P(None, "tp"),
            P("tp", None), P(), P(), P(), P(None, "tp"), P("tp"), P("tp", None), P(),
        ),
        check_vma=False,
    )
```

```python
import functools
import math

import jax
import jax.numpy as jnp
import numpy as np
from jax import lax
from jax.experimental import pallas as pl
from jax.experimental.pallas import tpu as pltpu
from jax.sharding import PartitionSpec as P

HD = 64
EPSILON = 1e-06
NEGATIVE = -1000000000.0
BF = jnp.bfloat16
F32 = jnp.float32
MESH = pl.DeviceIdType.MESH
VMEM_LIMIT = 62 * 2**20
CHUNK = 128
F_BLOCK = 256
ROWS = 128
N_TP = 4
TABLE = 64
NN = (((1,), (0,)), ((), ()))
NT = (((1,), (1,)), ((), ()))
TN = (((0,), (0,)), ((), ()))


def dot(a, b, dims):
    return lax.dot_general(a, b, dims, preferred_element_type=F32)


def flip(value, weight):
    return value + weight - 2 * weight * lax.rem(lax.div(value, weight), 2)


def bit_of(value, weight):
    return lax.rem(lax.div(value, weight), 2)


def aligned(value, multiple=16):
    return value if isinstance(value, int) else pl.multiple_of(value, multiple)


def gelu_parts(x):
    e = jnp.exp(-0.5 * x * x)
    z = jnp.abs(x) * (0.3275911 / math.sqrt(2.0))
    r = 1.0 / (1.0 + z)
    poly = r * (0.254829592 + r * (-0.284496736 + r * (1.421413741 + r * (-1.453152027 + r * 1.061405429))))
    tail = 0.5 * poly * e
    cdf = jnp.where(x >= 0, 1.0 - tail, tail)
    return x * cdf, cdf + x * (e * (1.0 / math.sqrt(2.0 * math.pi)))


def stats(v):
    mean = jnp.mean(v, axis=-1, keepdims=True)
    center = v - mean
    rstd = lax.rsqrt(jnp.mean(center * center, axis=-1, keepdims=True) + EPSILON)
    return center * rstd, rstd


def norm_back(v, dy, gain):
    xhat, rstd = stats(v)
    dx = dy * gain
    m1 = jnp.mean(dx, axis=-1, keepdims=True)
    m2 = jnp.mean(dx * xhat, axis=-1, keepdims=True)
    return (dx - m1 - xhat * m2) * rstd, jnp.sum(dy * xhat, axis=0, keepdims=True), jnp.sum(dy, axis=0, keepdims=True)


def reduce_stages(n_clips):
    stages = []
    rows = CHUNK
    weight = 1
    while weight < n_clips:
        halving = rows >= 32
        if halving:
            rows //= 2
        stages.append((weight, rows, halving))
        weight *= 2
    return stages


def layer_kernel(dims, stages, lags, count_ref, tok_ref, ext_ref, og_ref, proj_ref, qkv_ref, up_ref, down_ref, vec_ref,
                 bias_ref, table_ref, grad_ref, small_ref, res_ref, ing_ref,
                 w, tokb, extb, ogb, biasb, stream, first, qkvt, probs, mixed, middle, second, ff, sg, branch, outp, inp,
                 core_buf, side_buf, *rest):
    here, slots, width, hidden, features = dims
    bufs = rest[: len(stages)]
    small_buf, l_sem, t_sem, y_sem, q_sem, f_sem, c_sem, r_sem, s_sem, o_sem = rest[len(stages):]
    c = lax.axis_index("clips")
    t = lax.axis_index("tp")
    k, u = bit_of(t, 1), bit_of(t, 2)
    core = (c, flip(t, 1))
    side = (c, flip(t, 2))
    across = (flip(c, 1), t)
    along = (flip(c, 2), t)
    others = [(c, lax.rem(t + i, N_TP)) for i in range(1, N_TP)]
    peers = [(flip(c, weight), t) for weight, _, _ in stages]
    own_slots = slots // N_TP
    n_rows = here * slots
    a_rows = 4 * width
    total_rows = a_rows + 2 * hidden
    nf = hidden // F_BLOCK
    blocks = [(0, a_rows)] + [(a_rows + 2 * F_BLOCK * j, 2 * F_BLOCK) for j in range(nf)]
    n_chunks = total_rows // CHUNK
    b0, b1 = bit_of(c, 1), bit_of(c, 2)
    quarter = b1 * 2 + b0
    via_z = (1 - b1) * 2 + b0
    via_x = b1 * 2 + (1 - b0)

    pieces = [[(proj_ref, 0, 0, width), (qkv_ref, 0, width, 3 * width)]]
    for j in range(nf):
        base = a_rows + 2 * F_BLOCK * j
        pieces.append([(up_ref, j * F_BLOCK, base, F_BLOCK), (down_ref, j * F_BLOCK, base + F_BLOCK, F_BLOCK)])

    def own_copies(i):
        return [pltpu.make_async_copy(ref.at[pl.ds(at, rows)], w.at[u, k, pl.ds(to, rows)], l_sem.at[i, n])
                for n, (ref, at, to, rows) in enumerate(pieces[i])]

    def row_copies():
        return [pltpu.make_async_copy(src.at[pl.ds(t * here, here)], dst.at[:, pl.ds(t * own_slots, own_slots)],
                                      l_sem.at[nf + 1, n])
                for n, (src, dst) in enumerate(((tok_ref, tokb), (ext_ref, extb), (og_ref, ogb)))] + [
                    pltpu.make_async_copy(bias_ref, biasb.at[t], l_sem.at[nf + 1, 3])]

    for i in range(nf + 1):
        for copy in own_copies(i):
            copy.start()
    for copy in row_copies():
        copy.start()

    barrier = pltpu.get_barrier_semaphore()
    targets = others + peers
    for target in targets:
        pl.semaphore_signal(barrier, inc=1, device_id=target, device_id_type=MESH)
    pl.semaphore_wait(barrier, len(targets))

    def remote(src, dst, sem, index, target):
        return pltpu.make_async_remote_copy(src_ref=src, dst_ref=dst, send_sem=sem.at[(0, *index)],
                                            recv_sem=sem.at[(1, *index)], device_id=target, device_id_type=MESH)

    def rows_copy(n, i):
        target = others[i]
        if n == 3:
            return remote(bias_ref, biasb.at[t], t_sem, (n, i), target)
        src = (tok_ref, ext_ref, og_ref)[n]
        dst = (tokb, extb, ogb)[n]
        return remote(src.at[pl.ds(target[1] * here, here)], dst.at[:, pl.ds(t * own_slots, own_slots)], t_sem,
                      (n, i), target)

    def w_copy(kind, i):
        base, rows = blocks[i]
        q, h = rows // 4, rows // 8
        su, start, size, sem, index, target = {
            "y": (u, base + quarter * q, q, y_sem, (i,), side),
            "x": (1 - u, base + quarter * q, q, q_sem, (0, i), across),
            "z": (1 - u, base + quarter * q, q, q_sem, (1, i), along),
            "xf": (1 - u, base + via_z * q, h, f_sem, (0, i), across),
            "zf": (1 - u, base + via_x * q + h, h, f_sem, (1, i), along),
            "co": (u, base, rows, c_sem, (0, i), core),
            "cf": (1 - u, base, rows, c_sem, (1, i), core),
        }[kind]
        view = w.at[su, k, pl.ds(aligned(start), size)]
        return remote(view, view, sem, index, target)

    def begin(i):
        for copy in own_copies(i):
            copy.wait()
        w_copy("y", i).start()
        w_copy("co", i).start()

    def step1(i):
        w_copy("y", i).wait_recv()
        w_copy("x", i).start()
        w_copy("z", i).start()

    def step2(i):
        w_copy("z", i).wait_recv()
        w_copy("xf", i).start()
        w_copy("x", i).wait_recv()
        w_copy("zf", i).start()

    def step3(i):
        w_copy("xf", i).wait_recv()
        w_copy("zf", i).wait_recv()
        w_copy("cf", i).start()

    def step4(i):
        w_copy("co", i).wait_recv()
        w_copy("cf", i).wait_recv()
        for kind in ("y", "x", "z", "xf", "zf", "co", "cf"):
            w_copy(kind, i).wait_send()

    def start_rows(n):
        for i in range(N_TP - 1):
            rows_copy(n, i).start()

    def wait_rows(n):
        for i in range(N_TP - 1):
            rows_copy(n, i).wait_recv()

    begin(0)
    start_rows(3)
    start_rows(1)
    start_rows(0)
    for i in range(1, nf + 1):
        begin(i)
        if i == 1:
            start_rows(2)

    small_ref[...] = jnp.zeros_like(small_ref)
    ff[...] = jnp.zeros_like(ff)
    sg[...] = jnp.zeros_like(sg)

    step1(0)
    for copy in row_copies():
        copy.wait()
    wait_rows(3)
    wait_rows(1)
    wait_rows(0)
    half = features // 2

    def vec(i):
        return vec_ref[pl.ds(i, 1), :]

    def first_rows(i, _):
        b, at = lax.div(i, slots // ROWS), lax.rem(i, slots // ROWS) * ROWS
        rows = pl.ds(pl.multiple_of(i * ROWS, ROWS), ROWS)
        here_rows = pl.ds(pl.multiple_of(at, ROWS), ROWS)
        place = extb[b, here_rows, :].astype(F32)
        lane = lax.broadcasted_iota(jnp.int32, (ROWS, 2 * TABLE), 1)
        lane = lax.rem(lane, TABLE).astype(F32)
        hot_hi = jnp.where(lane == place[:, 0:1], 1.0, 0.0).astype(BF)
        hot_lo = jnp.where(lane == place[:, 1:2], 1.0, 0.0).astype(BF)
        hi = dot(hot_hi, table_ref[0 : 2 * TABLE, :], NN)
        lo = dot(hot_lo, table_ref[2 * TABLE :, :], NN)
        sh, ch, sl, cl = hi[:, :half], hi[:, half:], lo[:, :half], lo[:, half:]
        pos = jnp.concatenate([sh * cl + ch * sl, ch * cl - sh * sl], axis=1)
        v = tokb[b, here_rows, :].astype(F32) + pos
        stream[rows, :] = v
        xhat, _ = stats(v)
        first[rows, :] = (xhat * vec(0) + vec(1)).astype(BF)
        return 0

    lax.fori_loop(0, n_rows // ROWS, first_rows, 0)
    step2(0)
    step1(1)
    step3(0)
    step4(0)

    scale = HD ** -0.5

    def qkv_of(g, _):
        gu, gk = lax.div(g, 2), lax.rem(g, 2)
        out = dot(w[gu, gk, width:a_rows, :], first[...], NT)
        out = out + biasb[g, :, 0:BIAS_UP].T[0 : 3 * width, 0:1]
        qkvt[g, 0:width, :] = (out[0:width].astype(BF).astype(F32) * scale).astype(BF)
        qkvt[g, width : 3 * width, :] = out[width : 3 * width].astype(BF)
        return 0

    lax.fori_loop(0, N_TP, qkv_of, 0)
    step2(1)
    step1(2)

    per_group = width // HD

    def attend(g, _):
        for b in range(here):
            cols = slice(b * slots, (b + 1) * slots)
            visible = count_ref[t * here + b]
            keep = lax.broadcasted_iota(jnp.int32, (slots, slots), 0) < visible
            for r in range(per_group):
                q = qkvt[g, r * HD : (r + 1) * HD, cols]
                key = qkvt[g, width + r * HD : width + (r + 1) * HD, cols]
                value = qkvt[g, 2 * width + r * HD : 2 * width + (r + 1) * HD, cols]
                s = jnp.where(keep, dot(key, q, TN), NEGATIVE)
                e = jnp.exp(s - jnp.max(s, axis=0, keepdims=True))
                p = (e * (1.0 / jnp.sum(e, axis=0, keepdims=True))).astype(BF)
                probs[b, g * per_group + r] = p
                mixed[g, r * HD : (r + 1) * HD, cols] = dot(value, p, NN).astype(BF)

        @pl.when(g == 0)
        def _():
            step3(1)

        @pl.when(g == 1)
        def _():
            step2(2)

        @pl.when(g == 2)
        def _():
            step1(3)

        return 0

    lax.fori_loop(0, N_TP, attend, 0)

    def second_rows(i, _):
        rows = pl.ds(pl.multiple_of(i * ROWS, ROWS), ROWS)
        total = stream[rows, :] + vec(4)
        for g in range(N_TP):
            total = total + dot(mixed[g, :, rows], w[g // 2, g % 2, 0:width, :], TN)
        middle[rows, :] = total
        xhat, _ = stats(total)
        second[rows, :] = (xhat * vec(2) + vec(3)).astype(BF)
        return 0

    lax.fori_loop(0, n_rows // ROWS, second_rows, 0)
    wait_rows(2)

    def kept(stage, chunk):
        start = chunk * CHUNK
        for weight, rows, halving in stages[:stage]:
            if halving:
                start = start + bit_of(c, weight) * rows
        return start

    n_rs = 2 + len(stages)
    halvings = [i for i, s in enumerate(stages) if s[2]]
    gathers = list(reversed(halvings))
    n_all = n_rs + len(gathers)

    def shifted(chunk):
        return lax.rem(chunk + a_rows // CHUNK, n_chunks)

    def copy_of(stage, chunk):
        at = shifted(chunk)
        rows = pl.ds(aligned(at * CHUNK), CHUNK)
        if stage == 0:
            src, dst, target = w.at[:, 1 - k, rows], core_buf.at[:, rows], core
        elif stage == 1:
            src, dst, target = core_buf.at[1 - u, rows], side_buf.at[rows], side
        elif stage < n_rs:
            i = stage - 2
            weight, size, halving = stages[i]
            start = kept(i, at)
            if halving:
                start = start + (1 - bit_of(c, weight)) * size
            src = side_buf.at[pl.ds(aligned(start), size)]
            dst = bufs[i].at[pl.ds(aligned(at * size), size)]
            target = peers[i]
        else:
            i = gathers[stage - n_rs]
            size = stages[i][1]
            src = grad_ref.at[pl.ds(aligned(kept(i + 1, at)), size)]
            dst, target = src, peers[i]
        return remote(src, dst, r_sem, (stage, chunk), target)

    def add(a, b):
        return (a.astype(F32) + b.astype(F32)).astype(BF)

    def finish(stage, chunk):
        copy_of(stage, chunk).wait_recv()
        at = shifted(chunk)
        rows = pl.ds(aligned(at * CHUNK), CHUNK)
        if stage == 0:
            for n in (0, 1):
                core_buf[n, rows] = add(w[n, k, rows], core_buf[n, rows])
        elif stage == 1:
            side_buf[rows] = add(core_buf[u, rows], side_buf[rows])
        elif stage < n_rs:
            i = stage - 2
            _, size, halving = stages[i]
            keep_rows = pl.ds(aligned(kept(i + 1, at)), size)
            if not halving:
                copy_of(stage, chunk).wait_send()
            result = grad_ref if stage == n_rs - 1 else side_buf
            result[keep_rows] = add(side_buf[keep_rows], bufs[i][pl.ds(aligned(at * size), size)])

    starts = [0]
    for lag in lags[:n_all]:
        starts.append(starts[-1] + lag)

    def tick(i):
        for stage in reversed(range(n_all + 1)):
            chunk = i - starts[stage]

            @pl.when((chunk >= 0) & (chunk < n_chunks))
            def _():
                if stage > 0:
                    finish(stage - 1, chunk)
                if stage < n_all:
                    copy_of(stage, chunk).start()

    per_block = 2 * F_BLOCK // CHUNK

    def ffn(i, _):
        j, g = lax.div(i, N_TP), lax.rem(i, N_TP)
        gu, gk = lax.div(g, 2), lax.rem(g, 2)

        @pl.when(i == 0)
        def _():
            step4(1)
            step2(3)
            step3(2)

        @pl.when(i == N_TP)
        def _():
            step4(2)
            step3(3)

        @pl.when(i == 2 * N_TP)
        def _():
            step4(3)

        base = a_rows + j * 2 * F_BLOCK
        up_rows = pl.ds(pl.multiple_of(base, F_BLOCK), F_BLOCK)
        down_rows = pl.ds(pl.multiple_of(base + F_BLOCK, F_BLOCK), F_BLOCK)
        up, down = w[gu, gk, up_rows, :], w[gu, gk, down_rows, :]
        lanes = pl.ds(pl.multiple_of(BIAS_UP + j * F_BLOCK, F_BLOCK // 2), F_BLOCK)
        pre = dot(second[...], up, NT) + biasb[g, 0:1, lanes]
        act, slope = gelu_parts(pre)
        act = act.astype(BF)
        ff[...] += dot(act, down, NN)
        og = ogb[...].reshape(n_rows, features)
        pg = (dot(og, down, NT) * slope).astype(BF)
        sg[...] += dot(pg, up, NN)
        w[gu, gk, down_rows, :] = dot(act, og, TN).astype(BF)
        w[gu, gk, up_rows, :] = dot(pg, second[...], TN).astype(BF)
        small_ref[pl.ds(8 + g, 1), pl.ds(pl.multiple_of(j * F_BLOCK, F_BLOCK), F_BLOCK)] = jnp.sum(
            pg.astype(F32), axis=0, keepdims=True)

        @pl.when(i >= N_TP)
        def _():
            tick(i - N_TP)

        return 0

    lax.fori_loop(0, nf * N_TP, ffn, 0)
    done = (nf - 1) * N_TP

    def middle_rows(i, _):
        b, at = lax.div(i, slots // ROWS), lax.rem(i, slots // ROWS) * ROWS
        rows = pl.ds(pl.multiple_of(i * ROWS, ROWS), ROWS)
        here_rows = pl.ds(pl.multiple_of(at, ROWS), ROWS)
        m = middle[rows, :]
        outp[b, here_rows, :] = (m + ff[rows, :] + vec(5)).astype(BF)
        dv, dgain, dbias = norm_back(m, sg[rows, :], vec(2))
        og = ogb[b, here_rows, :].astype(F32)
        mg = og + dv
        ff[rows, :] = mg
        bg = mg.astype(BF)
        branch[rows, :] = bg
        small_ref[2:3, :] += dgain
        small_ref[3:4, :] += dbias
        small_ref[4:5, :] += jnp.sum(bg.astype(F32), axis=0, keepdims=True)
        small_ref[5:6, :] += jnp.sum(og, axis=0, keepdims=True)
        return 0

    lax.fori_loop(0, n_rows // ROWS, middle_rows, 0)

    def back_copy(n, i):
        src, dst = ((outp, res_ref), (inp, ing_ref))[n]
        target = others[i]
        return remote(src.at[:, pl.ds(target[1] * own_slots, own_slots)], dst.at[pl.ds(t * here, here)], o_sem,
                      (n, i), target)

    def back_own(n):
        src, dst = ((outp, res_ref), (inp, ing_ref))[n]
        return pltpu.make_async_copy(src.at[:, pl.ds(t * own_slots, own_slots)], dst.at[pl.ds(t * here, here)],
                                     l_sem.at[nf + 2, n])

    def send_back(n):
        back_own(n).start()
        for i in range(N_TP - 1):
            back_copy(n, i).start()

    send_back(0)
    sg[...] = jnp.zeros_like(sg)

    def back_group(g, _):
        gu, gk = lax.div(g, 2), lax.rem(g, 2)
        bg = branch[...]
        pw = w[gu, gk, 0:width, :]
        dmix = dot(pw, bg, NT).astype(BF)
        w[gu, gk, 0:width, :] = dot(mixed[g], bg, NN).astype(BF)
        for b in range(here):
            cols = slice(b * slots, (b + 1) * slots)
            for r in range(per_group):
                q_rows = slice(r * HD, (r + 1) * HD)
                k_rows = slice(width + r * HD, width + (r + 1) * HD)
                v_rows = slice(2 * width + r * HD, 2 * width + (r + 1) * HD)
                q, key, value = qkvt[g, q_rows, cols], qkvt[g, k_rows, cols], qkvt[g, v_rows, cols]
                dm = dmix[q_rows, cols]
                p = probs[b, g * per_group + r]
                pf = p.astype(F32)
                dp = dot(value, dm, TN)
                ds = (pf * (dp - jnp.sum(pf * dp, axis=0, keepdims=True))).astype(BF)
                qkvt[g, q_rows, cols] = (dot(key, ds, NN) * scale).astype(BF)
                qkvt[g, k_rows, cols] = dot(q, ds, NT).astype(BF)
                qkvt[g, v_rows, cols] = dot(dm, p, NT).astype(BF)
        dqkv = qkvt[g]
        sg[...] += dot(dqkv, w[gu, gk, width:a_rows, :], TN)
        w[gu, gk, width:a_rows, :] = dot(dqkv, first[...], NN).astype(BF)
        small_ref[pl.ds(12 + g, 1), 0 : 3 * width] = dot(jnp.ones((8, n_rows), BF), dqkv, NT)[0:1]
        tick(done + g)
        return 0

    lax.fori_loop(0, N_TP, back_group, 0)

    def last_rows(i, _):
        b, at = lax.div(i, slots // ROWS), lax.rem(i, slots // ROWS) * ROWS
        rows = pl.ds(pl.multiple_of(i * ROWS, ROWS), ROWS)
        here_rows = pl.ds(pl.multiple_of(at, ROWS), ROWS)
        dv, dgain, dbias = norm_back(stream[rows, :], sg[rows, :], vec(0))
        inp[b, here_rows, :] = (ff[rows, :] + dv).astype(BF)
        small_ref[0:1, :] += dgain
        small_ref[1:2, :] += dbias
        return 0

    lax.fori_loop(0, n_rows // ROWS, last_rows, 0)
    send_back(1)

    small_targets = [core, side] + peers

    def small_copy(i):
        return remote(small_ref, small_buf.at[i], s_sem, (i,), small_targets[i])

    done = done + N_TP

    def rest_of(i, _):
        for n in range(len(small_targets) + 1):
            @pl.when(i == done + n)
            def _():
                if n > 0:
                    small_copy(n - 1).wait()
                    small_ref[...] += small_buf[n - 1]
                if n < len(small_targets):
                    small_copy(n).start()
        tick(i)
        return 0

    lax.fori_loop(done, n_chunks + starts[-1], rest_of, 0)

    for n in (0, 1):
        for i in range(N_TP - 1):
            back_copy(n, i).wait_recv()
            back_copy(n, i).wait_send()
        back_own(n).wait()
    for n in range(4):
        for i in range(N_TP - 1):
            rows_copy(n, i).wait_send()

    def drain(chunk, _):
        for stage in range(n_all):
            if 2 <= stage < n_rs and not stages[stage - 2][2]:
                continue
            copy_of(stage, chunk).wait_send()
        return 0

    lax.fori_loop(0, n_chunks, drain, 0)


BIAS_UP = 640


def layer_call(n_clips, counts, tok, ext, og, proj, qkv, up, down, vectors, biases, table):
    count, own_slots, features = tok.shape
    width = proj.shape[0]
    hidden = up.shape[0]
    here = count // N_TP
    slots = own_slots * N_TP
    n_rows = here * slots
    rows = 4 * width + 2 * hidden
    nf = hidden // F_BLOCK
    n_chunks = rows // CHUNK
    heads = features // HD
    stages = reduce_stages(n_clips)
    n_all = 2 + len(stages) + sum(1 for s in stages if s[2])
    lags = [1, 2, 2] + [1] * (n_all - 4) + [2]
    hbm = pl.BlockSpec(memory_space=pl.ANY)
    vmem = pl.BlockSpec(memory_space=pltpu.VMEM)
    smem = pl.BlockSpec(memory_space=pltpu.SMEM)
    dma = pltpu.SemaphoreType.DMA
    nb = nf + 1
    return pl.pallas_call(
        functools.partial(layer_kernel, (here, slots, width, hidden, features), stages, lags),
        out_shape=(
            jax.ShapeDtypeStruct((rows, features), BF),
            jax.ShapeDtypeStruct((16, features), F32),
            jax.ShapeDtypeStruct((count, own_slots, features), BF),
            jax.ShapeDtypeStruct((count, own_slots, features), BF),
        ),
        in_specs=[smem, hbm, hbm, hbm, hbm, hbm, hbm, hbm, vmem, vmem, vmem],
        out_specs=(vmem, vmem, hbm, hbm),
        scratch_shapes=[
            pltpu.VMEM((2, 2, rows, features), BF),
            pltpu.VMEM((here, slots, features), BF),
            pltpu.VMEM((here, slots, 128), BF),
            pltpu.VMEM((here, slots, features), BF),
            pltpu.VMEM((N_TP, *biases.shape), F32),
            pltpu.VMEM((n_rows, features), F32),
            pltpu.VMEM((n_rows, features), BF),
            pltpu.VMEM((N_TP, 3 * width, n_rows), BF),
            pltpu.VMEM((here, heads, slots, slots), BF),
            pltpu.VMEM((N_TP, width, n_rows), BF),
            pltpu.VMEM((n_rows, features), F32),
            pltpu.VMEM((n_rows, features), BF),
            pltpu.VMEM((n_rows, features), F32),
            pltpu.VMEM((n_rows, features), F32),
            pltpu.VMEM((n_rows, features), BF),
            pltpu.VMEM((here, slots, features), BF),
            pltpu.VMEM((here, slots, features), BF),
            pltpu.VMEM((2, rows, features), BF),
            pltpu.VMEM((rows, features), BF),
            *[pltpu.VMEM((n_chunks * size, features), BF) for _, size, _ in stages],
            pltpu.VMEM((2 + len(stages), 16, features), F32),
            dma((nf + 3, 4)),
            dma((2, 4, N_TP - 1)),
            dma((2, nb)),
            dma((2, 2, nb)),
            dma((2, 2, nb)),
            dma((2, 2, nb)),
            dma((2, n_all, n_chunks)),
            dma((2, 2 + len(stages))),
            dma((2, 2, N_TP - 1)),
        ],
        compiler_params=pltpu.CompilerParams(collective_id=0, has_side_effects=True, vmem_limit_bytes=VMEM_LIMIT),
        name="encoder_layer",
    )(counts, tok, ext, og, proj, qkv, up, down, vectors, biases, table)


def place_table(features, largest):
    half = features // 2
    freq = np.exp(-math.log(10000.0) * np.arange(half, dtype=np.float64) / half).astype(np.float32).astype(np.float64)
    parts = []
    for step in (TABLE, 1):
        angle = step * np.arange(TABLE, dtype=np.float64)[:, None] * freq
        values = np.concatenate([np.sin(angle), np.cos(angle)], axis=1).astype(np.float32)
        high = values.astype(BF)
        parts += [high, (values - high.astype(np.float32)).astype(BF)]
    return np.concatenate(parts, axis=0)


def per_device(n_clips, tokens, tubelet_index, visible_count, norm1_gain, norm1_bias, qkv_weight, qv_bias,
               proj_weight, proj_bias, norm2_gain, norm2_bias, up_weight, up_bias, down_weight, down_bias, out_grad):
    count, rows, features = tokens.shape
    width = qkv_weight.shape[2]
    hidden = up_weight.shape[1]
    t = lax.axis_index("tp")
    qkv_t = jnp.transpose(qkv_weight, (1, 2, 0)).reshape(3 * width, features)
    up_t = up_weight.T
    hi = (tubelet_index // TABLE).astype(BF)[..., None]
    lo = (tubelet_index % TABLE).astype(BF)[..., None]
    lane = jnp.arange(128)[None, None, :]
    ext = jnp.where(lane == 0, hi, jnp.where(lane == 1, lo, jnp.zeros((), BF)))
    zeros = jnp.zeros((width,), F32)
    line = jnp.concatenate([qv_bias[0], zeros, qv_bias[1], jnp.zeros((BIAS_UP - 3 * width,), F32), up_bias])
    biases = jnp.zeros((8, line.shape[0]), F32).at[0].set(line)
    none = jnp.zeros((features,), F32)
    vectors = jnp.stack([norm1_gain, norm1_bias, norm2_gain, norm2_bias, proj_bias, down_bias, none, none])
    table = jnp.asarray(place_table(features, 2560))
    total, small, rows_out, rows_in = layer_call(
        n_clips, visible_count, tokens, ext, out_grad, proj_weight, qkv_t, up_t, down_weight, vectors, biases, table)
    total = total.astype(F32)
    a_rows = 4 * width
    nf = hidden // F_BLOCK
    ffn_grad = total[a_rows:].reshape(nf, 2, F_BLOCK, features)
    qkv_out = jnp.transpose(total[width:a_rows].reshape(3, width, features), (2, 0, 1))
    qkv_b = lax.dynamic_slice(small, (12 + t, 0), (1, features))[0]
    qv_out = jnp.stack([qkv_b[:width], qkv_b[2 * width : 3 * width]])
    up_b = lax.dynamic_slice(small, (8 + t, 0), (1, features))[0]
    return (
        rows_out.astype(F32),
        rows_in.astype(F32),
        small[0],
        small[1],
        qkv_out,
        qv_out,
        total[:width],
        small[4],
        small[2],
        small[3],
        ffn_grad[:, 0].reshape(hidden, features).T,
        up_b,
        ffn_grad[:, 1].reshape(hidden, features),
        small[5],
    )


def solution(mesh):
    placed = (
        P("clips", "tp", None), P("clips", "tp"), P("clips"), P(), P(), P(None, None, "tp"), P(None, "tp"),
        P("tp", None), P(), P(), P(), P(None, "tp"), P("tp"), P("tp", None), P(), P("clips", "tp", None),
    )
    return jax.shard_map(
        functools.partial(per_device, mesh.shape["clips"]),
        mesh=mesh,
        in_specs=placed,
        out_specs=(
            P("clips", "tp", None), P("clips", "tp", None), P(), P(), P(None, None, "tp"), P(None, "tp"),
            P("tp", None), P(), P(), P(), P(None, "tp"), P("tp"), P("tp", None), P(),
        ),
        check_vma=False,
    )
```

```python
import functools
import math

import jax
import jax.numpy as jnp
import numpy as np
from jax import lax
from jax.experimental import pallas as pl
from jax.experimental.pallas import tpu as pltpu
from jax.sharding import PartitionSpec as P

HD = 64
EPSILON = 1e-06
NEGATIVE = -1000000000.0
BF = jnp.bfloat16
F32 = jnp.float32
MESH = pl.DeviceIdType.MESH
VMEM_LIMIT = 62 * 2**20
CHUNK = 128
F_BLOCK = 256
ROWS = 128
N_TP = 4
TABLE = 64
NN = (((1,), (0,)), ((), ()))
NT = (((1,), (1,)), ((), ()))
TN = (((0,), (0,)), ((), ()))


def dot(a, b, dims):
    return lax.dot_general(a, b, dims, preferred_element_type=F32)


def flip(value, weight):
    return value + weight - 2 * weight * lax.rem(lax.div(value, weight), 2)


def bit_of(value, weight):
    return lax.rem(lax.div(value, weight), 2)


def row(ref):
    return ref[...].reshape(1, ref.shape[0])


def div(value, by):
    return value // by if isinstance(value, int) else lax.div(value, by)


def mod(value, by):
    return value % by if isinstance(value, int) else lax.rem(value, by)


def aligned(value, multiple=16):
    return value if isinstance(value, int) else pl.multiple_of(value, multiple)


def gelu_parts(x):
    e = jnp.exp(-0.5 * x * x)
    z = jnp.abs(x) * (0.3275911 / math.sqrt(2.0))
    r = 1.0 / (1.0 + z)
    poly = r * (0.254829592 + r * (-0.284496736 + r * (1.421413741 + r * (-1.453152027 + r * 1.061405429))))
    tail = 0.5 * poly * e
    cdf = jnp.where(x >= 0, 1.0 - tail, tail)
    return x * cdf, cdf + x * (e * (1.0 / math.sqrt(2.0 * math.pi)))


def stats(v):
    mean = jnp.mean(v, axis=-1, keepdims=True)
    center = v - mean
    rstd = lax.rsqrt(jnp.mean(center * center, axis=-1, keepdims=True) + EPSILON)
    return center * rstd, rstd


def norm_back(v, dy, gain):
    xhat, rstd = stats(v)
    dx = dy * gain
    m1 = jnp.mean(dx, axis=-1, keepdims=True)
    m2 = jnp.mean(dx * xhat, axis=-1, keepdims=True)
    return (dx - m1 - xhat * m2) * rstd, jnp.sum(dy * xhat, axis=0, keepdims=True), jnp.sum(dy, axis=0, keepdims=True)


ORDERS = (((0, 1, 2), 0), ((1, 0, 2), 2))
LAGS = ((1, 2, 2, 1, 1, 1, 1, 2), (1, 2, 1, 1, 1, 1, 1, 2))
EVERY, OFFSET = 4, 3


def reduce_plan(n_clips, which):
    bits = n_clips.bit_length() - 1
    first, side_at = ORDERS[which]
    order = [b for b in first if b < bits] + list(range(3, bits))
    plan = [("core", 0, CHUNK, False)]
    rows = CHUNK
    gathers = []
    for n, bit in enumerate(order):
        if n == side_at:
            plan.append(("side", 0, rows, False))
        halving = rows >= 32
        if halving:
            rows //= 2
            gathers.append(("gather", bit, rows, True))
        plan.append(("reduce", bit, rows, halving))
    return plan, plan + gathers[::-1]


def layer_kernel(dims, n_clips, count_ref, tok_ref, ext_ref, og_ref, proj_ref, qkv_ref, up_ref, down_ref,
                 gain1_ref, bias1_ref, gain2_ref, bias2_ref, projb_ref, downb_ref, upb_ref, qvb_ref, table_ref,
                 grad_ref, upg_ref, small_ref, res_ref, ing_ref,
                 w, tokb, extb, ogb, qvb, upb, stream, first, qkvt, probs, mixed, middle, second, ff, sg, branch, outp,
                 inp, core_buf, side_buf, land_a, land_c, small, small_buf, l_sem, t_sem, y_sem, q_sem, f_sem, c_sem,
                 r_sem, s_sem, o_sem):
    here, slots, width, hidden, features = dims
    bits = n_clips.bit_length() - 1
    c = lax.axis_index("clips")
    t = lax.axis_index("tp")
    k, u = bit_of(t, 1), bit_of(t, 2)
    core = (c, flip(t, 1))
    side = (c, flip(t, 2))
    across = (flip(c, 1), t)
    along = (flip(c, 2), t)
    others = [(c, lax.rem(t + i, N_TP)) for i in range(1, N_TP)]
    peers = [(flip(c, 2 ** bit), t) for bit in range(bits)]
    c_bits = [bit_of(c, 2 ** bit) for bit in range(bits)]
    own_slots = slots // N_TP
    n_rows = here * slots
    nf = hidden // F_BLOCK
    n_chunks = 3 * features // CHUNK
    b0, b1 = bit_of(c, 1), bit_of(c, 2)
    quarter = b1 * 2 + b0
    via_z = (1 - b1) * 2 + b0
    via_x = b1 * 2 + (1 - b0)
    blocks = [(0, 1, F_BLOCK * j, F_BLOCK) for j in range(features // F_BLOCK)] + [
        (1, 2, F_BLOCK * j, F_BLOCK) for j in range(nf)]
    na = features // F_BLOCK
    nb = len(blocks)
    half = features // 2
    tiles = features // F_BLOCK

    def weights_in():
        copies = [pltpu.make_async_copy(qkv_ref, w.at[u, k, 0, pl.ds(0, 3 * width)], l_sem.at[0]),
                  pltpu.make_async_copy(proj_ref, w.at[u, k, 0, pl.ds(3 * width, width)], l_sem.at[1]),
                  pltpu.make_async_copy(down_ref, w.at[u, k, 2], l_sem.at[2])]
        for i in range(tiles):
            for j in range(nf):
                copies.append(pltpu.make_async_copy(
                    up_ref.at[pl.ds(F_BLOCK * i, F_BLOCK), pl.ds(F_BLOCK * j, F_BLOCK)], probs.at[0, i * nf + j],
                    l_sem.at[3 + i * nf + j]))
        return copies

    def row_copies():
        mine = pl.ds(t * here, here)
        cols = pl.ds(t * own_slots, own_slots)
        return [pltpu.make_async_copy(tok_ref.at[mine], tokb.at[:, cols], o_sem.at[0, 2, 0]),
                pltpu.make_async_copy(og_ref.at[mine], ogb.at[:, cols], o_sem.at[0, 2, 1]),
                pltpu.make_async_copy(ext_ref, extb.at[t], o_sem.at[0, 2, 2]),
                pltpu.make_async_copy(qvb_ref, qvb.at[t], o_sem.at[1, 2, 0])]

    own_w = weights_in()
    for copy in own_w + row_copies():
        copy.start()

    barrier = pltpu.get_barrier_semaphore()
    targets = others + peers
    for target in targets:
        pl.semaphore_signal(barrier, inc=1, device_id=target, device_id_type=MESH)
    pl.semaphore_wait(barrier, len(targets))

    def remote(src, dst, sem, index, target):
        return pltpu.make_async_remote_copy(src_ref=src, dst_ref=dst, send_sem=sem.at[(0, *index)],
                                            recv_sem=sem.at[(1, *index)], device_id=target, device_id_type=MESH)

    def rows_copy(n, i):
        target = others[i]
        mine = pl.ds(target[1] * here, here)
        cols = pl.ds(t * own_slots, own_slots)
        src, dst = (lambda: (tok_ref.at[mine], tokb.at[:, cols]), lambda: (ext_ref, extb.at[t]),
                    lambda: (og_ref.at[mine], ogb.at[:, cols]), lambda: (qvb_ref, qvb.at[t]),
                    lambda: (upb.at[t], upb.at[t]))[n]()
        return remote(src, dst, t_sem, (n, i), target)

    def w_copy(kind, i):
        part, parts, base, rows = blocks[i]
        q, h = rows // 4, rows // 8
        su, start, size, sem, index, target = {
            "y": (u, base + quarter * q, q, y_sem, (i,), side),
            "x": (1 - u, base + quarter * q, q, q_sem, (0, i), across),
            "z": (1 - u, base + quarter * q, q, q_sem, (1, i), along),
            "xf": (1 - u, base + via_z * q, h, f_sem, (0, i), across),
            "zf": (1 - u, base + via_x * q + h, h, f_sem, (1, i), along),
            "co": (u, base, rows, c_sem, (0, i), core),
            "cf": (1 - u, base, rows, c_sem, (1, i), core),
        }[kind]
        view = w.at[su, k, pl.ds(part, parts), pl.ds(aligned(start), size)]
        return remote(view, view, sem, index, target)

    def step1(i):
        w_copy("y", i).wait_recv()
        w_copy("x", i).start()
        w_copy("z", i).start()

    def step2(i):
        w_copy("z", i).wait_recv()
        w_copy("xf", i).start()
        w_copy("x", i).wait_recv()
        w_copy("zf", i).start()

    def step3(i):
        w_copy("xf", i).wait_recv()
        w_copy("zf", i).wait_recv()
        w_copy("cf", i).start()

    def step4(i):
        w_copy("co", i).wait_recv()
        w_copy("cf", i).wait_recv()
        for kind in ("y", "x", "z", "xf", "zf", "co", "cf"):
            w_copy(kind, i).wait_send()

    def start_rows(n):
        for i in range(N_TP - 1):
            rows_copy(n, i).start()

    def wait_rows(n):
        for i in range(N_TP - 1):
            rows_copy(n, i).wait_recv()

    upb[pl.ds(t, 1), :, :] = row(upb_ref).reshape(1, 1, hidden)
    own_w[0].wait()
    for i in range(na):
        if i == na - 1:
            own_w[1].wait()
        w_copy("y", i).start()
    for n in (1, 3, 4):
        start_rows(n)
    for i in range(na):
        w_copy("co", i).start()
    for copy in own_w[2:]:
        copy.wait()
    for i in range(tiles):
        for j in range(nf):
            w[u, k, 1, j * F_BLOCK : (j + 1) * F_BLOCK, i * F_BLOCK : (i + 1) * F_BLOCK] = probs[0, i * nf + j].T
    for copy in row_copies():
        copy.wait()

    step1(0)
    start_rows(0)
    small[...] = jnp.zeros_like(small)
    step1(1)
    step2(0)
    step1(2)
    w_copy("y", na).start()
    ff[...] = jnp.zeros_like(ff)
    sg[...] = jnp.zeros_like(sg)
    step2(1)
    step2(2)
    w_copy("y", na + 1).start()
    for i in range(na):
        step3(i)
    for n in (1, 3, 4, 0):
        wait_rows(n)
    start_rows(2)

    per_clip = slots // ROWS
    sources = ROWS // own_slots

    def rows_at(i):
        return lax.div(i, per_clip), pl.ds(pl.multiple_of(lax.rem(i, per_clip) * ROWS, ROWS), ROWS), pl.ds(
            pl.multiple_of(i * ROWS, ROWS), ROWS)

    def first_rows(i, _):
        b, here_rows, rows = rows_at(i)
        line = lax.broadcasted_iota(jnp.int32, (2 * TABLE, own_slots), 0) & (TABLE - 1)
        pos = []
        for n in range(sources):
            place = extb[lax.rem(i, per_clip) * sources + n, pl.ds(t * here + b, 1), :]
            hot = [jnp.where(line == lax.broadcast_in_dim(v, line.shape, (0, 1)), 1.0, 0.0).astype(BF)
                   for v in (lax.shift_right_logical(place, 6), place & (TABLE - 1))]
            hi = dot(hot[0], table_ref[0 : 2 * TABLE, :], TN)
            lo = dot(hot[1], table_ref[2 * TABLE :, :], TN)
            sh, ch, sl, cl = hi[:, :half], hi[:, half:], lo[:, :half], lo[:, half:]
            pos.append(jnp.concatenate([sh * cl + ch * sl, ch * cl - sh * sl], axis=1))
        v = tokb[b, here_rows, :].astype(F32) + jnp.concatenate(pos, axis=0)
        stream[rows, :] = v
        xhat, _ = stats(v)
        first[rows, :] = (xhat * row(gain1_ref) + row(bias1_ref)).astype(BF)
        return 0

    lax.fori_loop(0, n_rows // ROWS, first_rows, 0)
    for i in range(na):
        step4(i)
    for i in range(na, nb):
        w_copy("co", i).start()

    scale = HD ** -0.5

    def qkv_of(g, _):
        gu, gk = lax.div(g, 2), lax.rem(g, 2)
        out = dot(w[gu, gk, 0, 0 : 3 * width, :], first[...], NT)
        add = jnp.concatenate([qvb[g, :, :], jnp.zeros((6, width), F32)], axis=0)
        add = jnp.concatenate([add, jnp.zeros((8, 64), F32)], axis=1).T
        qkvt[g, 0:width, :] = ((out[0:width] + add[0:width, 0:1]).astype(BF).astype(F32) * scale).astype(BF)
        qkvt[g, width : 2 * width, :] = out[width : 2 * width].astype(BF)
        qkvt[g, 2 * width :, :] = (out[2 * width :] + add[0:width, 1:2]).astype(BF)

        @pl.when(g == 1)
        def _():
            step1(na)
            w_copy("y", na + 2).start()

        return 0

    lax.fori_loop(0, N_TP, qkv_of, 0)

    per_group = width // HD

    def attend(g, _):
        for b in range(here):
            cols = slice(b * slots, (b + 1) * slots)
            visible = count_ref[t * here + b]
            keep = lax.broadcasted_iota(jnp.int32, (slots, slots), 0) < visible
            for r in range(per_group):
                q = qkvt[g, r * HD : (r + 1) * HD, cols]
                key = qkvt[g, width + r * HD : width + (r + 1) * HD, cols]
                value = qkvt[g, 2 * width + r * HD : 2 * width + (r + 1) * HD, cols]
                s = jnp.where(keep, dot(key, q, TN), NEGATIVE)
                e = jnp.exp(s - jnp.max(s, axis=0, keepdims=True))
                p = (e * (1.0 / jnp.sum(e, axis=0, keepdims=True))).astype(BF)
                probs[b, g * per_group + r] = p
                mixed[g, r * HD : (r + 1) * HD, cols] = dot(value, p, NN).astype(BF)

        @pl.when(g == 1)
        def _():
            step1(na + 1)

        @pl.when(g == 2)
        def _():
            step2(na)

        return 0

    lax.fori_loop(0, N_TP, attend, 0)
    step3(na)

    def second_rows(i, _):
        _, _, rows = rows_at(i)
        total = stream[rows, :] + row(projb_ref)
        for g in range(N_TP):
            total = total + dot(mixed[g, :, rows], w[g // 2, g % 2, 0, 3 * width :, :], TN)
        middle[rows, :] = total
        xhat, _ = stats(total)
        second[rows, :] = (xhat * row(gain2_ref) + row(bias2_ref)).astype(BF)
        return 0

    lax.fori_loop(0, n_rows // ROWS, second_rows, 0)
    step4(na)
    wait_rows(2)

    plans = [reduce_plan(n_clips, n) for n in (0, 1)]
    lands = (land_a, land_c)
    f_chunks = nf * 2 * F_BLOCK // CHUNK
    per_f = F_BLOCK // CHUNK

    def place_of(chunk):
        last = div(chunk, f_chunks)
        in_block = mod(chunk, 2 * per_f)
        part = (1 - last) * (1 + div(in_block, per_f))
        row = (1 - last) * (div(chunk, 2 * per_f) * F_BLOCK + mod(in_block, per_f) * CHUNK)
        return part, row + last * (chunk - f_chunks) * CHUNK

    def kept(which, stage):
        start = 0
        for kind, bit, rows, halving in plans[which][0][:stage]:
            if halving:
                start = start + c_bits[bit] * rows
        return start

    def copy_of(which, stage, chunk):
        kind, bit, rows, halving = plans[which][1][stage]
        both = ("side", 0) not in [p[:2] for p in plans[which][1][:stage]]
        base = chunk * CHUNK
        if kind == "core":
            part, row = place_of(chunk)
            src = w.at[:, 1 - k, part, pl.ds(aligned(row), CHUNK)]
            dst, target = core_buf.at[:, pl.ds(aligned(base), CHUNK)], core
        elif kind == "side":
            start = aligned(base + kept(which, stage))
            src, dst, target = core_buf.at[1 - u, pl.ds(start, rows)], side_buf.at[pl.ds(start, rows)], side
        elif kind == "reduce":
            start = base + kept(which, stage)
            if halving:
                start = start + (1 - c_bits[bit]) * rows
            at = pl.ds(aligned(land_at(which, stage, chunk)), rows)
            if both:
                src, dst = core_buf.at[:, pl.ds(aligned(start), rows)], lands[which].at[:, at]
            else:
                src, dst = side_buf.at[pl.ds(aligned(start), rows)], lands[which].at[0, at]
            target = peers[bit]
        else:
            depth = [p[:2] for p in plans[which][0]].index(("reduce", bit))
            part, row = place_of(chunk)
            src = grad_ref.at[part, pl.ds(aligned(row + kept(which, depth + 1)), rows)]
            dst, target = src, peers[bit]
        send = chunk if kind == "reduce" and not halving else which
        return pltpu.make_async_remote_copy(
            src_ref=src, dst_ref=dst, send_sem=r_sem.at[0, stage, send], recv_sem=r_sem.at[1, stage, chunk],
            device_id=target, device_id_type=MESH)

    def land_at(which, stage, chunk):
        at = 0
        for kind, bit, rows, halving in plans[which][0][:stage]:
            if kind == "reduce":
                at += rows
        size = sum(p[2] for p in plans[which][0] if p[0] == "reduce")
        index = div(chunk, EVERY)
        if which == 0:
            index = index * (EVERY - 1) + mod(mod(chunk, EVERY) + EVERY - OFFSET - 1, EVERY)
        return index * size + at

    def add(a, b):
        return (a.astype(F32) + b.astype(F32)).astype(BF)

    def finish(which, stage, chunk):
        copy_of(which, stage, chunk).wait_recv()
        kind, bit, rows, halving = plans[which][1][stage]
        both = ("side", 0) not in [p[:2] for p in plans[which][1][:stage]]
        base = chunk * CHUNK
        last = stage == len(plans[which][0]) - 1
        if kind == "core":
            part, row = place_of(chunk)
            at = pl.ds(aligned(base), CHUNK)
            for n in (0, 1):
                core_buf[n, at] = add(w[n, k, part, pl.ds(aligned(row), CHUNK)], core_buf[n, at])
        elif kind == "side":
            at = pl.ds(aligned(base + kept(which, stage)), rows)
            side_buf[at] = add(core_buf[u, at], side_buf[at])
        elif kind == "reduce":
            at = pl.ds(aligned(base + kept(which, stage + 1)), rows)
            land = pl.ds(aligned(land_at(which, stage, chunk)), rows)
            if not halving:
                copy_of(which, stage, chunk).wait_send()
            if both:
                for n in (0, 1):
                    core_buf[n, at] = add(core_buf[n, at], lands[which][n, land])
            elif last:
                part, row = place_of(chunk)
                grad_ref[part, pl.ds(aligned(row + kept(which, stage + 1)), rows)] = add(
                    side_buf[at], lands[which][0, land])
            else:
                side_buf[at] = add(side_buf[at], lands[which][0, land])

    starts = []
    for which in (0, 1):
        lags = list(LAGS[which]) + [1] * 32
        starts.append([sum(lags[:n]) for n in range(len(plans[which][1]) + 1)])

    def step(which, stage, chunk):
        if stage > 0:
            finish(which, stage - 1, chunk)
        if stage < len(plans[which][1]):
            copy_of(which, stage, chunk).start()

    def tick(i):
        for which in (0, 1):
            for stage in range(len(plans[which][1]) + 1):
                chunk = i - starts[which][stage]
                mine = lax.rem(chunk + EVERY, EVERY) == OFFSET
                if which == 0:
                    mine = jnp.logical_not(mine)

                @pl.when((chunk >= 0) & (chunk < n_chunks) & mine)
                def _():
                    step(which, stage, chunk)

    def ffn(i, _):
        j, g = lax.div(i, N_TP), lax.rem(i, N_TP)
        gu, gk = lax.div(g, 2), lax.rem(g, 2)
        for at, work in ((0, lambda: step2(na + 1)), (1, lambda: step1(na + 2)), (2, lambda: step3(na + 1)),
                         (3, lambda: step2(na + 2)), (4, lambda: step4(na + 1)), (6, lambda: step3(na + 2)),
                         (8, lambda: step4(na + 2))):
            @pl.when(i == at)
            def _():
                work()

        hid = pl.ds(pl.multiple_of(j * F_BLOCK, F_BLOCK), F_BLOCK)
        up, down = w[gu, gk, 1, hid, :], w[gu, gk, 2, hid, :]
        pre = dot(second[...], up, NT) + upb[g, :, hid]
        act, slope = gelu_parts(pre)
        act = act.astype(BF)
        ff[...] += dot(act, down, NN)
        og = ogb[...].reshape(n_rows, features)
        pg = (dot(og, down, NT) * slope).astype(BF)
        sg[...] += dot(pg, up, NN)
        w[gu, gk, 2, hid, :] = dot(act, og, TN).astype(BF)
        w[gu, gk, 1, hid, :] = dot(pg, second[...], TN).astype(BF)
        small[pl.ds(8 + g, 1), hid] = jnp.sum(pg.astype(F32), axis=0, keepdims=True)

        @pl.when(i >= N_TP)
        def _():
            tick(i - N_TP)

        return 0

    lax.fori_loop(0, nf * N_TP, ffn, 0)
    done = (nf - 1) * N_TP

    def middle_rows(i, _):
        b, here_rows, rows = rows_at(i)
        m = middle[rows, :]
        outp[b, here_rows, :] = (m + ff[rows, :] + row(downb_ref)).astype(BF)
        dv, dgain, dbias = norm_back(m, sg[rows, :], row(gain2_ref))
        og = ogb[b, here_rows, :].astype(F32)
        mg = og + dv
        ff[rows, :] = mg
        bg = mg.astype(BF)
        branch[rows, :] = bg
        small[2:3, :] += dgain
        small[3:4, :] += dbias
        small[4:5, :] += jnp.sum(bg.astype(F32), axis=0, keepdims=True)
        small[5:6, :] += jnp.sum(og, axis=0, keepdims=True)
        return 0

    lax.fori_loop(0, n_rows // ROWS, middle_rows, 0)

    def back_copy(n, i):
        src, dst = ((outp, res_ref), (inp, ing_ref))[n]
        target = others[i]
        return remote(src.at[:, pl.ds(target[1] * own_slots, own_slots)], dst.at[pl.ds(t * here, here)], o_sem,
                      (n, i), target)

    def back_own(n):
        src, dst = ((outp, res_ref), (inp, ing_ref))[n]
        return pltpu.make_async_copy(src.at[:, pl.ds(t * own_slots, own_slots)], dst.at[pl.ds(t * here, here)],
                                     l_sem.at[n])

    def send_back(n):
        back_own(n).start()
        for i in range(N_TP - 1):
            back_copy(n, i).start()

    send_back(0)
    sg[...] = jnp.zeros_like(sg)

    def back_group(g, _):
        gu, gk = lax.div(g, 2), lax.rem(g, 2)
        bg = branch[...]
        dmix = dot(w[gu, gk, 0, 3 * width :, :], bg, NT).astype(BF)
        w[gu, gk, 0, 3 * width :, :] = dot(mixed[g], bg, NN).astype(BF)
        for b in range(here):
            cols = slice(b * slots, (b + 1) * slots)
            for r in range(per_group):
                q_rows = slice(r * HD, (r + 1) * HD)
                k_rows = slice(width + r * HD, width + (r + 1) * HD)
                v_rows = slice(2 * width + r * HD, 2 * width + (r + 1) * HD)
                q, key, value = qkvt[g, q_rows, cols], qkvt[g, k_rows, cols], qkvt[g, v_rows, cols]
                dm = dmix[q_rows, cols]
                p = probs[b, g * per_group + r]
                pf = p.astype(F32)
                dp = dot(value, dm, TN)
                ds = (pf * (dp - jnp.sum(pf * dp, axis=0, keepdims=True))).astype(BF)
                qkvt[g, q_rows, cols] = (dot(key, ds, NN) * scale).astype(BF)
                qkvt[g, k_rows, cols] = dot(q, ds, NT).astype(BF)
                qkvt[g, v_rows, cols] = dot(dm, p, NT).astype(BF)
        dqkv = qkvt[g]
        sg[...] += dot(dqkv, w[gu, gk, 0, 0 : 3 * width, :], TN)
        w[gu, gk, 0, 0 : 3 * width, :] = dot(dqkv, first[...], NN).astype(BF)
        small[pl.ds(12 + g, 1), 0 : 3 * width] = dot(jnp.ones((8, n_rows), BF), dqkv, NT)[0:1]
        tick(done + g)
        return 0

    lax.fori_loop(0, N_TP, back_group, 0)

    def last_rows(i, _):
        b, here_rows, rows = rows_at(i)
        dv, dgain, dbias = norm_back(stream[rows, :], sg[rows, :], row(gain1_ref))
        inp[b, here_rows, :] = (ff[rows, :] + dv).astype(BF)
        small[0:1, :] += dgain
        small[1:2, :] += dbias
        return 0

    lax.fori_loop(0, n_rows // ROWS, last_rows, 0)
    send_back(1)

    small_targets = [core, side] + peers

    def small_copy(i):
        return remote(small, small_buf.at[i], s_sem, (i,), small_targets[i])

    done = done + N_TP

    def rest_of(i, _):
        tick(i)
        return 0

    lax.fori_loop(done, n_chunks, rest_of, 0)
    state = {}
    for chunk in range(n_chunks):
        which = int(chunk % EVERY == OFFSET)
        n_all = len(plans[which][1])
        stage = max(n for n in range(n_all + 1) if chunk + starts[which][n] < n_chunks)
        if stage < n_all:
            state[chunk] = (which, stage)
    turn = 0
    up_left = True
    while state or turn <= len(small_targets):
        if turn <= len(small_targets):
            if turn > 0:
                small_copy(turn - 1).wait()
                small[...] += small_buf[turn - 1]
            if turn < len(small_targets):
                small_copy(turn).start()
        for chunk in sorted(state):
            which, stage = state[chunk]
            step(which, stage + 1, chunk)
            state[chunk] = (which, stage + 1)
            if stage + 1 == len(plans[which][1]):
                del state[chunk]
        if up_left and not [chunk for chunk in state if chunk < f_chunks]:
            up_left = False
            for m in range(tiles):
                for j in range(nf):
                    upg_ref[m * F_BLOCK : (m + 1) * F_BLOCK, j * F_BLOCK : (j + 1) * F_BLOCK] = grad_ref[
                        1, j * F_BLOCK : (j + 1) * F_BLOCK, m * F_BLOCK : (m + 1) * F_BLOCK].T
        turn += 1
    small_ref[0:6, :] = small[0:6, :]
    small_ref[6:7, :] = small[pl.ds(8 + t, 1), :]
    small_ref[7:8, :] = small[pl.ds(12 + t, 1), :]

    for n in (0, 1):
        for i in range(N_TP - 1):
            back_copy(n, i).wait_recv()
            back_copy(n, i).wait_send()
        back_own(n).wait()
    for n in range(5):
        for i in range(N_TP - 1):
            rows_copy(n, i).wait_send()

    for which in (0, 1):
        count = len([chunk for chunk in range(n_chunks) if (chunk % EVERY == OFFSET) == bool(which)])
        for stage, (kind, _, rows, halving) in enumerate(plans[which][1]):
            if kind != "reduce" or halving:
                both = ("side", 0) not in [p[:2] for p in plans[which][1][:stage]]
                view = core_buf.at[:, pl.ds(0, count * rows)] if both and kind != "side" else side_buf.at[
                    pl.ds(0, count * rows)]
                pltpu.make_async_remote_copy(
                    src_ref=view, dst_ref=view, send_sem=r_sem.at[0, stage, which], recv_sem=r_sem.at[1, stage, which],
                    device_id=core, device_id_type=MESH).wait_send()


def layer_call(n_clips, counts, tok, ext, og, proj, qkv, up, down, vectors, qv_bias, table):
    count, own_slots, features = tok.shape
    width = proj.shape[0]
    hidden = up.shape[1]
    here = count // N_TP
    slots = own_slots * N_TP
    n_rows = here * slots
    nf = hidden // F_BLOCK
    n_chunks = 3 * features // CHUNK
    heads = features // HD
    bits = n_clips.bit_length() - 1
    sizes = [sum(p[2] for p in reduce_plan(n_clips, n)[0] if p[0] == "reduce") for n in (0, 1)]
    n_all = max(len(reduce_plan(n_clips, n)[1]) for n in (0, 1))
    n_second = -(-n_chunks // EVERY)
    hbm = pl.BlockSpec(memory_space=pl.ANY)
    vmem = pl.BlockSpec(memory_space=pltpu.VMEM)
    smem = pl.BlockSpec(memory_space=pltpu.SMEM)
    dma = pltpu.SemaphoreType.DMA
    nb = nf + features // F_BLOCK
    return pl.pallas_call(
        functools.partial(layer_kernel, (here, slots, width, hidden, features), n_clips),
        out_shape=(
            jax.ShapeDtypeStruct((3, features, features), BF),
            jax.ShapeDtypeStruct((features, hidden), BF),
            jax.ShapeDtypeStruct((8, features), F32),
            jax.ShapeDtypeStruct((count, own_slots, features), BF),
            jax.ShapeDtypeStruct((count, own_slots, features), BF),
        ),
        in_specs=[smem, hbm, vmem] + [hbm] * 5 + [vmem] * 9,
        out_specs=(vmem, vmem, vmem, hbm, hbm),
        scratch_shapes=[
            pltpu.VMEM((2, 2, 3, features, features), BF),
            pltpu.VMEM((here, slots, features), BF),
            pltpu.VMEM((N_TP, *ext.shape), jnp.int32),
            pltpu.VMEM((here, slots, features), BF),
            pltpu.VMEM((N_TP, *qv_bias.shape), F32),
            pltpu.VMEM((N_TP, 1, hidden), F32),
            pltpu.VMEM((n_rows, features), F32),
            pltpu.VMEM((n_rows, features), BF),
            pltpu.VMEM((N_TP, 3 * width, n_rows), BF),
            pltpu.VMEM((here, heads, slots, slots), BF),
            pltpu.VMEM((N_TP, width, n_rows), BF),
            pltpu.VMEM((n_rows, features), F32),
            pltpu.VMEM((n_rows, features), BF),
            pltpu.VMEM((n_rows, features), F32),
            pltpu.VMEM((n_rows, features), F32),
            pltpu.VMEM((n_rows, features), BF),
            pltpu.VMEM((here, slots, features), BF),
            pltpu.VMEM((here, slots, features), BF),
            pltpu.VMEM((2, 3 * features, features), BF),
            pltpu.VMEM((3 * features, features), BF),
            pltpu.VMEM((1, n_second * (EVERY - 1) * sizes[0], features), BF),
            pltpu.VMEM((2, n_second * sizes[1], features), BF),
            pltpu.VMEM((16, features), F32),
            pltpu.VMEM((2 + bits, 16, features), F32),
            dma((3 + nf * features // F_BLOCK,)),
            dma((2, 5, N_TP - 1)),
            dma((2, nb)),
            dma((2, 2, nb)),
            dma((2, 2, nb)),
            dma((2, 2, nb)),
            dma((2, n_all, n_chunks)),
            dma((2, 2 + bits)),
            dma((2, 3, N_TP - 1)),
        ],
        compiler_params=pltpu.CompilerParams(collective_id=0, has_side_effects=True, vmem_limit_bytes=VMEM_LIMIT),
        name="encoder_layer",
    )(counts, tok, ext, og, proj, qkv, up, down, *vectors, qv_bias, table)


def widen_kernel(qkv_ref, proj_ref, down_ref, up_ref, out_ref, in_ref, small_ref, qkvo_ref, projo_ref, downo_ref,
                 upo_ref, outo_ref, ino_ref, qvo_ref, g1_ref, b1_ref, g2_ref, b2_ref, pb_ref, db_ref, ub_ref):
    for src, dst in ((qkv_ref, qkvo_ref), (proj_ref, projo_ref), (down_ref, downo_ref)):
        dst[...] = src[0].astype(F32)
    for src, dst in ((up_ref, upo_ref), (out_ref, outo_ref), (in_ref, ino_ref)):
        dst[...] = src[...].astype(F32)
    width = qvo_ref.shape[1]

    @pl.when(pl.program_id(0) == 0)
    def _():
        for i, ref in enumerate((g1_ref, b1_ref, g2_ref, b2_ref, pb_ref, db_ref, ub_ref)):
            ref[...] = small_ref[i, :]
        qvo_ref[0:1, :] = small_ref[7:8, 0:width]
        qvo_ref[1:2, :] = small_ref[7:8, 2 * width : 3 * width]


def widen_call(grads, up_grad, small, rows_out, rows_in, width):
    _, features, _ = grads.shape
    hidden = up_grad.shape[1]
    count, own_slots, _ = rows_out.shape
    steps = 4
    whole = pl.BlockSpec(memory_space=pltpu.VMEM)

    def rows_of(rows, first):
        return pl.BlockSpec((1, rows // steps, features), lambda i: (first[0], first[1] // (rows // steps) + i, 0))

    def flat(rows, cols):
        return pl.BlockSpec((rows // steps, cols), lambda i: (i, 0))

    clips = pl.BlockSpec((count // steps, own_slots, features), lambda i: (i, 0, 0))
    vector = jax.ShapeDtypeStruct((features,), F32)
    return pl.pallas_call(
        widen_kernel,
        grid=(steps,),
        out_shape=(
            jax.ShapeDtypeStruct((3 * width, features), F32),
            jax.ShapeDtypeStruct((width, features), F32),
            jax.ShapeDtypeStruct((hidden, features), F32),
            jax.ShapeDtypeStruct((features, hidden), F32),
            jax.ShapeDtypeStruct((count, own_slots, features), F32),
            jax.ShapeDtypeStruct((count, own_slots, features), F32),
            jax.ShapeDtypeStruct((2, width), F32),
        ) + (vector,) * 6 + (jax.ShapeDtypeStruct((hidden,), F32),),
        in_specs=[rows_of(3 * width, (0, 0)), rows_of(width, (0, 3 * width)), rows_of(hidden, (2, 0)),
                  flat(features, hidden), clips, clips, whole],
        out_specs=(flat(3 * width, features), flat(width, features), flat(hidden, features), flat(features, hidden),
                   clips, clips) + (whole,) * 8,
        compiler_params=pltpu.CompilerParams(vmem_limit_bytes=VMEM_LIMIT),
        name="widen",
    )(grads, grads, grads, up_grad, rows_out, rows_in, small)


def place_table(features, largest):
    half = features // 2
    freq = np.exp(-math.log(10000.0) * np.arange(half, dtype=np.float64) / half).astype(np.float32).astype(np.float64)
    parts = []
    for step in (TABLE, 1):
        angle = step * np.arange(TABLE, dtype=np.float64)[:, None] * freq
        values = np.concatenate([np.sin(angle), np.cos(angle)], axis=1).astype(np.float32)
        high = values.astype(BF)
        parts += [high, (values - high.astype(np.float32)).astype(BF)]
    return np.concatenate(parts, axis=0)


def per_device(n_clips, tokens, tubelet_index, visible_count, norm1_gain, norm1_bias, qkv_weight, qv_bias,
               proj_weight, proj_bias, norm2_gain, norm2_bias, up_weight, up_bias, down_weight, down_bias, out_grad):
    count, rows, features = tokens.shape
    width = qkv_weight.shape[2]
    hidden = up_weight.shape[1]
    qkv_t = jnp.transpose(qkv_weight, (1, 2, 0)).reshape(3 * width, features)
    vectors = (norm1_gain, norm1_bias, norm2_gain, norm2_bias, proj_bias, down_bias, up_bias)
    table = jnp.asarray(place_table(features, 2560))
    grads, up_grad, small, rows_out, rows_in = layer_call(
        n_clips, visible_count, tokens, tubelet_index, out_grad, proj_weight, qkv_t, up_weight, down_weight, vectors, qv_bias,
        table)
    qkv_grad, proj_grad, down_grad, up_grad, rows_out, rows_in, qv_grad, g1, b1, g2, b2, pb, db, ub = widen_call(
        grads, up_grad, small, rows_out, rows_in, width)
    qkv_grad = jnp.transpose(qkv_grad.reshape(3, width, features), (2, 0, 1))
    return rows_out, rows_in, g1, b1, qkv_grad, qv_grad, proj_grad, pb, g2, b2, up_grad, ub, down_grad, db


def solution(mesh):
    placed = (
        P("clips", "tp", None), P("clips", "tp"), P("clips"), P(), P(), P(None, None, "tp"), P(None, "tp"),
        P("tp", None), P(), P(), P(), P(None, "tp"), P("tp"), P("tp", None), P(), P("clips", "tp", None),
    )
    return jax.shard_map(
        functools.partial(per_device, mesh.shape["clips"]),
        mesh=mesh,
        in_specs=placed,
        out_specs=(
            P("clips", "tp", None), P("clips", "tp", None), P(), P(), P(None, None, "tp"), P(None, "tp"),
            P("tp", None), P(), P(), P(), P(None, "tp"), P("tp"), P("tp", None), P(),
        ),
        check_vma=False,
    )
```

```python
import functools
import math

import jax
import jax.numpy as jnp
import numpy as np
from jax import lax
from jax.experimental import pallas as pl
from jax.experimental.pallas import tpu as pltpu
from jax.sharding import PartitionSpec as P

HD = 64
EPSILON = 1e-06
NEGATIVE = -1000000000.0
BF = jnp.bfloat16
F32 = jnp.float32
MESH = pl.DeviceIdType.MESH
VMEM_LIMIT = 62 * 2**20
CHUNK = 128
F_BLOCK = 256
ROWS = 128
N_TP = 4
TABLE = 64
NN = (((1,), (0,)), ((), ()))
NT = (((1,), (1,)), ((), ()))
TN = (((0,), (0,)), ((), ()))


def dot(a, b, dims):
    return lax.dot_general(a, b, dims, preferred_element_type=F32)


def flip(value, weight):
    return value + weight - 2 * weight * lax.rem(lax.div(value, weight), 2)


def bit_of(value, weight):
    return lax.rem(lax.div(value, weight), 2)


def row(ref):
    return ref[...].reshape(1, ref.shape[0])


def div(value, by):
    return value // by if isinstance(value, int) else lax.div(value, by)


def mod(value, by):
    return value % by if isinstance(value, int) else lax.rem(value, by)


def aligned(value, multiple=16):
    return value if isinstance(value, int) else pl.multiple_of(value, multiple)


def gelu_parts(x):
    e = jnp.exp(-0.5 * x * x)
    z = jnp.abs(x) * (0.3275911 / math.sqrt(2.0))
    r = 1.0 / (1.0 + z)
    poly = r * (0.254829592 + r * (-0.284496736 + r * (1.421413741 + r * (-1.453152027 + r * 1.061405429))))
    tail = 0.5 * poly * e
    cdf = jnp.where(x >= 0, 1.0 - tail, tail)
    return x * cdf, cdf + x * (e * (1.0 / math.sqrt(2.0 * math.pi)))


def stats(v):
    mean = jnp.mean(v, axis=-1, keepdims=True)
    center = v - mean
    rstd = lax.rsqrt(jnp.mean(center * center, axis=-1, keepdims=True) + EPSILON)
    return center * rstd, rstd


def norm_back(v, dy, gain):
    xhat, rstd = stats(v)
    dx = dy * gain
    m1 = jnp.mean(dx, axis=-1, keepdims=True)
    m2 = jnp.mean(dx * xhat, axis=-1, keepdims=True)
    return (dx - m1 - xhat * m2) * rstd, jnp.sum(dy * xhat, axis=0, keepdims=True), jnp.sum(dy, axis=0, keepdims=True)


LAGS = (1, 2, 2, 1, 1, 1, 1, 2)
BACK = {("t", 2): [(n, piece) for n in (0, 1) for piece in range(4)]}


def reduce_plan(n_clips):
    plan = [("core", 0, CHUNK, False), ("side", 0, CHUNK, False)]
    rows = CHUNK
    gathers = []
    for bit in range(n_clips.bit_length() - 1):
        halving = rows >= 32
        if halving:
            rows //= 2
            gathers.append(("gather", bit, rows, True))
        plan.append(("reduce", bit, rows, halving))
    return plan, plan + gathers[::-1]


def layer_kernel(dims, n_clips, count_ref, tok_ref, ext_ref, og_ref, proj_ref, qkv_ref, up_ref, down_ref,
                 gain1_ref, bias1_ref, gain2_ref, bias2_ref, projb_ref, downb_ref, upb_ref, qvb_ref, table_ref,
                 grad_ref, upg_ref, small_ref, res_ref, ing_ref,
                 w, tokb, extb, ogb, qvb, upb, stream, first, qkvt, probs, mixed, middle, second, ff, sg, branch, outp,
                 inp, core_buf, side_buf, land, small, upsum, small_buf, l_sem, t_sem, y_sem, q_sem, f_sem, c_sem,
                 r_sem, s_sem, o_sem, b_sem):
    here, slots, width, hidden, features = dims
    bits = n_clips.bit_length() - 1
    c = lax.axis_index("clips")
    t = lax.axis_index("tp")
    k, u = bit_of(t, 1), bit_of(t, 2)
    core = (c, flip(t, 1))
    side = (c, flip(t, 2))
    across = (flip(c, 1), t)
    along = (flip(c, 2), t)
    others = [(c, lax.rem(t + i, N_TP)) for i in range(1, N_TP)]
    peers = [(flip(c, 2 ** bit), t) for bit in range(bits)]
    c_bits = [bit_of(c, 2 ** bit) for bit in range(bits)]
    own_slots = slots // N_TP
    n_rows = here * slots
    nf = hidden // F_BLOCK
    n_chunks = 3 * features // CHUNK
    b0, b1 = bit_of(c, 1), bit_of(c, 2)
    quarter = b1 * 2 + b0
    via_z = (1 - b1) * 2 + b0
    via_x = b1 * 2 + (1 - b0)
    blocks = [(0, 1, F_BLOCK * j, F_BLOCK) for j in range(features // F_BLOCK)] + [
        (1, 2, F_BLOCK * j, F_BLOCK) for j in range(nf)]
    na = features // F_BLOCK
    nb = len(blocks)
    half = features // 2
    tiles = features // F_BLOCK

    def weights_in():
        copies = [pltpu.make_async_copy(qkv_ref, w.at[u, k, 0, pl.ds(0, 3 * width)], l_sem.at[0]),
                  pltpu.make_async_copy(proj_ref, w.at[u, k, 0, pl.ds(3 * width, width)], l_sem.at[1]),
                  pltpu.make_async_copy(down_ref, w.at[u, k, 2], l_sem.at[2])]
        for i in range(tiles):
            for j in range(nf):
                copies.append(pltpu.make_async_copy(
                    up_ref.at[pl.ds(F_BLOCK * i, F_BLOCK), pl.ds(F_BLOCK * j, F_BLOCK)], probs.at[0, i * nf + j],
                    l_sem.at[3 + i * nf + j]))
        return copies

    def row_copies():
        mine = pl.ds(t * here, here)
        cols = pl.ds(t * own_slots, own_slots)
        return [pltpu.make_async_copy(tok_ref.at[mine], tokb.at[:, cols], o_sem.at[0, 2, 0]),
                pltpu.make_async_copy(og_ref.at[mine], ogb.at[:, cols], o_sem.at[0, 2, 1]),
                pltpu.make_async_copy(ext_ref, extb.at[t], o_sem.at[0, 2, 2]),
                pltpu.make_async_copy(qvb_ref, qvb.at[t], o_sem.at[1, 2, 0])]

    own_w = weights_in()
    for copy in own_w + row_copies():
        copy.start()

    barrier = pltpu.get_barrier_semaphore()
    targets = others + peers
    for target in targets:
        pl.semaphore_signal(barrier, inc=1, device_id=target, device_id_type=MESH)
    pl.semaphore_wait(barrier, len(targets))

    def remote(src, dst, sem, index, target):
        return pltpu.make_async_remote_copy(src_ref=src, dst_ref=dst, send_sem=sem.at[(0, *index)],
                                            recv_sem=sem.at[(1, *index)], device_id=target, device_id_type=MESH)

    def rows_copy(n, i):
        target = others[i]
        mine = pl.ds(target[1] * here, here)
        cols = pl.ds(t * own_slots, own_slots)
        src, dst = (lambda: (tok_ref.at[mine], tokb.at[:, cols]), lambda: (ext_ref, extb.at[t]),
                    lambda: (og_ref.at[mine], ogb.at[:, cols]), lambda: (qvb_ref, qvb.at[t]),
                    lambda: (upb.at[t], upb.at[t]))[n]()
        return remote(src, dst, t_sem, (n, i), target)

    def w_copy(kind, i):
        part, parts, base, rows = blocks[i]
        q, h = rows // 4, rows // 8
        su, start, size, sem, index, target = {
            "y": (u, base + quarter * q, q, y_sem, (i,), side),
            "x": (1 - u, base + quarter * q, q, q_sem, (0, i), across),
            "z": (1 - u, base + quarter * q, q, q_sem, (1, i), along),
            "xf": (1 - u, base + via_z * q, h, f_sem, (0, i), across),
            "zf": (1 - u, base + via_x * q + h, h, f_sem, (1, i), along),
            "co": (u, base, rows, c_sem, (0, i), core),
            "cf": (1 - u, base, rows, c_sem, (1, i), core),
        }[kind]
        view = w.at[su, k, pl.ds(part, parts), pl.ds(aligned(start), size)]
        return remote(view, view, sem, index, target)

    def step1(i):
        w_copy("y", i).wait_recv()
        w_copy("x", i).start()
        w_copy("z", i).start()

    def step2(i):
        w_copy("z", i).wait_recv()
        w_copy("xf", i).start()
        w_copy("x", i).wait_recv()
        w_copy("zf", i).start()

    def step3(i):
        w_copy("xf", i).wait_recv()
        w_copy("zf", i).wait_recv()
        w_copy("cf", i).start()

    def step4(i):
        w_copy("cf", i).wait_recv()
        for kind in ("x", "z", "xf", "zf", "cf"):
            w_copy(kind, i).wait_send()

    def step_own(i):
        w_copy("co", i).wait_recv()
        for kind in ("y", "co"):
            w_copy(kind, i).wait_send()

    def start_rows(n):
        for i in range(N_TP - 1):
            rows_copy(n, i).start()

    def wait_rows(n):
        for i in range(N_TP - 1):
            rows_copy(n, i).wait_recv()

    upb[pl.ds(t, 1), :, :] = row(upb_ref).reshape(1, 1, hidden)
    own_w[0].wait()
    for i in range(na):
        if i == na - 1:
            own_w[1].wait()
        w_copy("y", i).start()
    for n in (1, 3, 4):
        start_rows(n)
    for i in range(na):
        w_copy("co", i).start()
    for copy in own_w[2:]:
        copy.wait()
    for i in range(tiles):
        for j in range(nf):
            w[u, k, 1, j * F_BLOCK : (j + 1) * F_BLOCK, i * F_BLOCK : (i + 1) * F_BLOCK] = probs[0, i * nf + j].T
    for copy in row_copies():
        copy.wait()

    step1(0)
    start_rows(0)
    small[...] = jnp.zeros_like(small)
    step1(1)
    step2(0)
    step1(2)
    w_copy("y", na).start()
    ff[...] = jnp.zeros_like(ff)
    sg[...] = jnp.zeros_like(sg)
    step2(1)
    step2(2)
    w_copy("y", na + 1).start()
    for n in (1, 3, 4, 0):
        wait_rows(n)
    start_rows(2)

    per_clip = slots // ROWS
    sources = ROWS // own_slots

    def rows_at(i):
        return lax.div(i, per_clip), pl.ds(pl.multiple_of(lax.rem(i, per_clip) * ROWS, ROWS), ROWS), pl.ds(
            pl.multiple_of(i * ROWS, ROWS), ROWS)

    def first_rows(i, _):
        b, here_rows, rows = rows_at(i)
        line = lax.broadcasted_iota(jnp.int32, (2 * TABLE, own_slots), 0) & (TABLE - 1)
        pos = []
        for n in range(sources):
            place = extb[lax.rem(i, per_clip) * sources + n, pl.ds(t * here + b, 1), :]
            hot = [jnp.where(line == lax.broadcast_in_dim(v, line.shape, (0, 1)), 1.0, 0.0).astype(BF)
                   for v in (lax.shift_right_logical(place, 6), place & (TABLE - 1))]
            hi = dot(hot[0], table_ref[0 : 2 * TABLE, :], TN)
            lo = dot(hot[1], table_ref[2 * TABLE :, :], TN)
            sh, ch, sl, cl = hi[:, :half], hi[:, half:], lo[:, :half], lo[:, half:]
            pos.append(jnp.concatenate([sh * cl + ch * sl, ch * cl - sh * sl], axis=1))
        v = tokb[b, here_rows, :].astype(F32) + jnp.concatenate(pos, axis=0)
        stream[rows, :] = v
        xhat, _ = stats(v)
        first[rows, :] = (xhat * row(gain1_ref) + row(bias1_ref)).astype(BF)
        return 0

    lax.fori_loop(0, n_rows // ROWS, first_rows, 0)
    for i in range(na):
        step_own(i)
    for i in range(na, nb):
        w_copy("co", i).start()

    scale = HD ** -0.5

    def group(n):
        gu, gk = lax.rem(u + lax.div(n, 2), 2), lax.rem(n, 2)
        return gu * 2 + gk, gu, gk

    def qkv_of(n):
        g, gu, gk = group(n)
        out = dot(w[gu, gk, 0, 0 : 3 * width, :], first[...], NT)
        add = jnp.concatenate([qvb[g, :, :], jnp.zeros((6, width), F32)], axis=0)
        add = jnp.concatenate([add, jnp.zeros((8, 64), F32)], axis=1).T
        qkvt[g, 0:width, :] = ((out[0:width] + add[0:width, 0:1]).astype(BF).astype(F32) * scale).astype(BF)
        qkvt[g, width : 2 * width, :] = out[width : 2 * width].astype(BF)
        qkvt[g, 2 * width :, :] = (out[2 * width :] + add[0:width, 1:2]).astype(BF)


    per_group = width // HD

    def attend(n, _):
        @pl.when(n == 1)
        def _():
            for i in range(na):
                step3(i)

        @pl.when(n == 2)
        def _():
            for i in range(na):
                step4(i)

        qkv_of(n)
        g, _, _ = group(n)
        for b in range(here):
            cols = slice(b * slots, (b + 1) * slots)
            visible = count_ref[t * here + b]
            keep = lax.broadcasted_iota(jnp.int32, (slots, slots), 0) < visible
            for r in range(per_group):
                q = qkvt[g, r * HD : (r + 1) * HD, cols]
                key = qkvt[g, width + r * HD : width + (r + 1) * HD, cols]
                value = qkvt[g, 2 * width + r * HD : 2 * width + (r + 1) * HD, cols]
                s = jnp.where(keep, dot(key, q, TN), NEGATIVE)
                e = jnp.exp(s - jnp.max(s, axis=0, keepdims=True))
                p = (e * (1.0 / jnp.sum(e, axis=0, keepdims=True))).astype(BF)
                probs[b, g * per_group + r] = p
                mixed[g, r * HD : (r + 1) * HD, cols] = dot(value, p, NN).astype(BF)

        for at, work in ((0, lambda: (step1(na), w_copy("y", na + 2).start())), (1, lambda: step1(na + 1)),
                         (2, lambda: step2(na))):
            @pl.when(n == at)
            def _():
                work()

        return 0

    lax.fori_loop(0, N_TP, attend, 0)

    def second_rows(i, _):
        _, _, rows = rows_at(i)
        total = stream[rows, :] + row(projb_ref)
        for g in range(N_TP):
            total = total + dot(mixed[g, :, rows], w[g // 2, g % 2, 0, 3 * width :, :], TN)
        middle[rows, :] = total
        xhat, _ = stats(total)
        second[rows, :] = (xhat * row(gain2_ref) + row(bias2_ref)).astype(BF)
        return 0

    lax.fori_loop(0, n_rows // ROWS, second_rows, 0)
    step3(na)
    step_own(na)
    wait_rows(2)

    sums, plan = reduce_plan(n_clips)
    n_all = len(plan)
    f_chunks = nf * 2 * F_BLOCK // CHUNK
    per_f = F_BLOCK // CHUNK

    def place_of(chunk):
        last = div(chunk, f_chunks)
        in_block = mod(chunk, 2 * per_f)
        part = (1 - last) * (1 + mod(in_block, 2))
        row = (1 - last) * (div(chunk, 2 * per_f) * F_BLOCK + div(in_block, 2) * CHUNK)
        return part, row + last * (chunk - f_chunks) * CHUNK

    def kept(stage):
        start = 0
        for kind, bit, rows, halving in sums[:stage]:
            if halving:
                start = start + c_bits[bit] * rows
        return start

    def land_at(stage, chunk):
        return chunk * sum(p[2] for p in sums[2:]) + sum(p[2] for p in sums[2:stage])

    def copy_of(stage, chunk):
        kind, bit, rows, halving = plan[stage]
        base = chunk * CHUNK
        if kind == "core":
            part, row = place_of(chunk)
            src = w.at[:, 1 - k, part, pl.ds(aligned(row), CHUNK)]
            dst, target = core_buf.at[:, pl.ds(aligned(base), CHUNK)], core
        elif kind == "side":
            at = pl.ds(aligned(base), rows)
            src, dst, target = core_buf.at[1 - u, at], side_buf.at[at], side
        elif kind == "reduce":
            start = base + kept(stage)
            if halving:
                start = start + (1 - c_bits[bit]) * rows
            src = side_buf.at[pl.ds(aligned(start), rows)]
            dst, target = land.at[pl.ds(aligned(land_at(stage, chunk)), rows)], peers[bit]
        else:
            part, row = place_of(chunk)
            src = grad_ref.at[part, pl.ds(aligned(row + kept(bit + 3)), rows)]
            dst, target = src, peers[bit]
        send = chunk if kind == "reduce" and not halving else 0
        return pltpu.make_async_remote_copy(
            src_ref=src, dst_ref=dst, send_sem=r_sem.at[0, stage, send], recv_sem=r_sem.at[1, stage, chunk],
            device_id=target, device_id_type=MESH)

    def add(a, b):
        return (a.astype(F32) + b.astype(F32)).astype(BF)

    def finish(stage, chunk):
        copy_of(stage, chunk).wait_recv()
        kind, bit, rows, halving = plan[stage]
        base = chunk * CHUNK
        if kind == "core":
            part, row = place_of(chunk)
            at = pl.ds(aligned(base), CHUNK)
            for n in (0, 1):
                core_buf[n, at] = add(w[n, k, part, pl.ds(aligned(row), CHUNK)], core_buf[n, at])
        elif kind == "side":
            at = pl.ds(aligned(base), rows)
            side_buf[at] = add(core_buf[u, at], side_buf[at])
        elif kind == "reduce":
            at = pl.ds(aligned(base + kept(stage + 1)), rows)
            if not halving:
                copy_of(stage, chunk).wait_send()
            total = add(side_buf[at], land[pl.ds(aligned(land_at(stage, chunk)), rows)])
            if stage == len(sums) - 1:
                part, row = place_of(chunk)
                grad_ref[part, pl.ds(aligned(row + kept(stage + 1)), rows)] = total
            else:
                side_buf[at] = total

    lags = list(LAGS) + [1] * 32
    starts = [sum(lags[:n]) for n in range(n_all + 1)]

    def step(stage, chunk):
        if stage > 0:
            finish(stage - 1, chunk)
        if stage < n_all:
            copy_of(stage, chunk).start()

    def tick(i):
        for stage in range(n_all + 1):
            chunk = i - starts[stage]

            @pl.when((chunk >= 0) & (chunk < n_chunks))
            def _():
                step(stage, chunk)

    def ffn(gu, start, size):
        hid = pl.ds(pl.multiple_of(start, size), size)
        up = w[gu, :, 1, hid, :].reshape(2 * size, features)
        down = w[gu, :, 2, hid, :].reshape(2 * size, features)
        pre = dot(second[...], up, NT) + jnp.concatenate([upb[2 * gu, :, hid], upb[2 * gu + 1, :, hid]], axis=1)
        act, slope = gelu_parts(pre)
        act = act.astype(BF)
        ff[...] += dot(act, down, NN)
        og = ogb[...].reshape(n_rows, features)
        pg = (dot(og, down, NT) * slope).astype(BF)
        sg[...] += dot(pg, up, NN)
        w[gu, :, 2, hid, :] = dot(act, og, TN).astype(BF).reshape(2, size, features)
        w[gu, :, 1, hid, :] = dot(pg, second[...], TN).astype(BF).reshape(2, size, features)
        sums = jnp.sum(pg.astype(F32), axis=0, keepdims=True)
        for gk in (0, 1):
            for m in range(size // 128):
                at = gk * size + m * 128
                upsum[(2 * gu + gk) * (hidden // 128) + lax.div(start, 128) + m] = sums[:, at : at + 128]

    def hooks(i, *work):
        for at, do in work:
            @pl.when(i == at)
            def _():
                do()

    def ffn_block(i, _):
        hooks(i, (0, lambda: step2(na + 1)), (1, lambda: (step4(na), step1(na + 2))),
              (2, lambda: (step_own(na + 1), step3(na + 1), step2(na + 2))),
              (3, lambda: (step4(na + 1), step3(na + 2))), (4, lambda: step_own(na + 2)), (5, lambda: step4(na + 2)))
        ffn(lax.rem(u + i, 2), lax.div(i, 2) * F_BLOCK, F_BLOCK)

        @pl.when(i >= 2)
        def _():
            tick(2 * i - 4)
            tick(2 * i - 3)

        return 0

    lax.fori_loop(0, nf * 2, ffn_block, 0)
    done = (nf - 1) * N_TP
    for g in range(N_TP):
        for m in range(hidden // 128):
            small[8 + g : 9 + g, m * 128 : (m + 1) * 128] = upsum[g * (hidden // 128) + m]

    def middle_rows(i, _):
        b, here_rows, rows = rows_at(i)
        m = middle[rows, :]
        outp[b, here_rows, :] = (m + ff[rows, :] + row(downb_ref)).astype(BF)
        dv, dgain, dbias = norm_back(m, sg[rows, :], row(gain2_ref))
        og = ogb[b, here_rows, :].astype(F32)
        mg = og + dv
        ff[rows, :] = mg
        bg = mg.astype(BF)
        branch[rows, :] = bg
        small[2:3, :] += dgain
        small[3:4, :] += dbias
        small[4:5, :] += jnp.sum(bg.astype(F32), axis=0, keepdims=True)
        small[5:6, :] += jnp.sum(og, axis=0, keepdims=True)
        return 0

    lax.fori_loop(0, n_rows // ROWS, middle_rows, 0)

    def back_copy(n, i, b):
        src, dst = ((outp, res_ref), (inp, ing_ref))[n]
        target = others[i]
        return remote(src.at[b, pl.ds(target[1] * own_slots, own_slots)], dst.at[t * here + b], b_sem, (n, i, b), target)

    def back_own(n):
        src, dst = ((outp, res_ref), (inp, ing_ref))[n]
        return pltpu.make_async_copy(src.at[:, pl.ds(t * own_slots, own_slots)], dst.at[pl.ds(t * here, here)],
                                     l_sem.at[n])

    back_pieces = [(i, b) for i in range(N_TP - 1) for b in range(here)]

    def send_back(n, at):
        if at == 0:
            back_own(n).start()
        for i, b in back_pieces[at::4]:
            back_copy(n, i, b).start()

    sg[...] = jnp.zeros_like(sg)

    def back_group(g, _):
        gu, gk = lax.div(g, 2), lax.rem(g, 2)
        bg = branch[...]
        dmix = dot(w[gu, gk, 0, 3 * width :, :], bg, NT).astype(BF)
        w[gu, gk, 0, 3 * width :, :] = dot(mixed[g], bg, NN).astype(BF)
        for b in range(here):
            cols = slice(b * slots, (b + 1) * slots)
            for r in range(per_group):
                q_rows = slice(r * HD, (r + 1) * HD)
                k_rows = slice(width + r * HD, width + (r + 1) * HD)
                v_rows = slice(2 * width + r * HD, 2 * width + (r + 1) * HD)
                q, key, value = qkvt[g, q_rows, cols], qkvt[g, k_rows, cols], qkvt[g, v_rows, cols]
                dm = dmix[q_rows, cols]
                p = probs[b, g * per_group + r]
                pf = p.astype(F32)
                dp = dot(value, dm, TN)
                ds = (pf * (dp - jnp.sum(pf * dp, axis=0, keepdims=True))).astype(BF)
                qkvt[g, q_rows, cols] = (dot(key, ds, NN) * scale).astype(BF)
                qkvt[g, k_rows, cols] = dot(q, ds, NT).astype(BF)
                qkvt[g, v_rows, cols] = dot(dm, p, NT).astype(BF)
        dqkv = qkvt[g]
        sg[...] += dot(dqkv, w[gu, gk, 0, 0 : 3 * width, :], TN)
        w[gu, gk, 0, 0 : 3 * width, :] = dot(dqkv, first[...], NN).astype(BF)
        small[pl.ds(12 + g, 1), 0 : 3 * width] = dot(jnp.ones((8, n_rows), BF), dqkv, NT)[0:1]
        tick(done + g)
        return 0

    lax.fori_loop(0, N_TP, back_group, 0)

    def last_rows(i, _):
        b, here_rows, rows = rows_at(i)
        dv, dgain, dbias = norm_back(stream[rows, :], sg[rows, :], row(gain1_ref))
        inp[b, here_rows, :] = (ff[rows, :] + dv).astype(BF)
        small[0:1, :] += dgain
        small[1:2, :] += dbias
        return 0

    lax.fori_loop(0, n_rows // ROWS, last_rows, 0)

    small_targets = [core, side] + peers

    def small_copy(i):
        return remote(small, small_buf.at[i], s_sem, (i,), small_targets[i])

    done = done + N_TP

    def small_turn(n):
        if n > len(small_targets):
            return
        if n > 0:
            small_copy(n - 1).wait()
            small[...] += small_buf[n - 1]
        if n < len(small_targets):
            small_copy(n).start()

    def rest_of(i, _):
        tick(i)
        hooks(i, *((done + n, functools.partial(small_turn, n)) for n in range(n_chunks - done)))
        return 0

    lax.fori_loop(done, n_chunks, rest_of, 0)
    state = {}
    for chunk in range(n_chunks):
        stage = max(n for n in range(n_all + 1) if chunk + starts[n] < n_chunks)
        if stage < n_all:
            state[chunk] = stage
    turn = 0
    up_left = True
    small_left = list(range(n_chunks - done, len(small_targets) + 1))
    while state or small_left:
        for n, piece in BACK.get(("t", turn), ()):
            send_back(n, piece)
        if small_left:
            small_turn(small_left.pop(0))
        for chunk in sorted(state):
            state[chunk] += 1
            step(state[chunk], chunk)
            if state[chunk] == n_all:
                del state[chunk]
        if up_left and not [chunk for chunk in state if chunk < f_chunks]:
            up_left = False
            for m in range(tiles):
                for j in range(nf):
                    upg_ref[m * F_BLOCK : (m + 1) * F_BLOCK, j * F_BLOCK : (j + 1) * F_BLOCK] = grad_ref[
                        1, j * F_BLOCK : (j + 1) * F_BLOCK, m * F_BLOCK : (m + 1) * F_BLOCK].T
        turn += 1
    small_ref[0:6, :] = small[0:6, :]
    small_ref[6:7, :] = small[pl.ds(8 + t, 1), :]
    small_ref[7:8, :] = small[pl.ds(12 + t, 1), :]

    for n in (0, 1):
        for i, b in back_pieces:
            back_copy(n, i, b).wait_recv()
            back_copy(n, i, b).wait_send()
        back_own(n).wait()
    for n in range(5):
        for i in range(N_TP - 1):
            rows_copy(n, i).wait_send()

    for stage, (kind, _, rows, halving) in enumerate(plan):
        if kind != "reduce" or halving:
            view = core_buf if kind == "core" else side_buf.at[pl.ds(0, n_chunks * rows)]
            pltpu.make_async_remote_copy(
                src_ref=view, dst_ref=view, send_sem=r_sem.at[0, stage, 0], recv_sem=r_sem.at[1, stage, 0],
                device_id=core, device_id_type=MESH).wait_send()


def layer_call(n_clips, counts, tok, ext, og, proj, qkv, up, down, vectors, qv_bias, table):
    count, own_slots, features = tok.shape
    width = proj.shape[0]
    hidden = up.shape[1]
    here = count // N_TP
    slots = own_slots * N_TP
    n_rows = here * slots
    nf = hidden // F_BLOCK
    n_chunks = 3 * features // CHUNK
    heads = features // HD
    bits = n_clips.bit_length() - 1
    sums, plan = reduce_plan(n_clips)
    n_all = len(plan)
    hbm = pl.BlockSpec(memory_space=pl.ANY)
    vmem = pl.BlockSpec(memory_space=pltpu.VMEM)
    smem = pl.BlockSpec(memory_space=pltpu.SMEM)
    dma = pltpu.SemaphoreType.DMA
    nb = nf + features // F_BLOCK
    return pl.pallas_call(
        functools.partial(layer_kernel, (here, slots, width, hidden, features), n_clips),
        out_shape=(
            jax.ShapeDtypeStruct((3, features, features), BF),
            jax.ShapeDtypeStruct((features, hidden), BF),
            jax.ShapeDtypeStruct((8, features), F32),
            jax.ShapeDtypeStruct((count, own_slots, features), BF),
            jax.ShapeDtypeStruct((count, own_slots, features), BF),
        ),
        in_specs=[smem, hbm, vmem] + [hbm] * 5 + [vmem] * 9,
        out_specs=(vmem, vmem, vmem, hbm, hbm),
        scratch_shapes=[
            pltpu.VMEM((2, 2, 3, features, features), BF),
            pltpu.VMEM((here, slots, features), BF),
            pltpu.VMEM((N_TP, *ext.shape), jnp.int32),
            pltpu.VMEM((here, slots, features), BF),
            pltpu.VMEM((N_TP, *qv_bias.shape), F32),
            pltpu.VMEM((N_TP, 1, hidden), F32),
            pltpu.VMEM((n_rows, features), F32),
            pltpu.VMEM((n_rows, features), BF),
            pltpu.VMEM((N_TP, 3 * width, n_rows), BF),
            pltpu.VMEM((here, heads, slots, slots), BF),
            pltpu.VMEM((N_TP, width, n_rows), BF),
            pltpu.VMEM((n_rows, features), F32),
            pltpu.VMEM((n_rows, features), BF),
            pltpu.VMEM((n_rows, features), F32),
            pltpu.VMEM((n_rows, features), F32),
            pltpu.VMEM((n_rows, features), BF),
            pltpu.VMEM((here, slots, features), BF),
            pltpu.VMEM((here, slots, features), BF),
            pltpu.VMEM((2, 3 * features, features), BF),
            pltpu.VMEM((3 * features, features), BF),
            pltpu.VMEM((n_chunks * sum(p[2] for p in sums[2:]), features), BF),
            pltpu.VMEM((16, features), F32),
            pltpu.VMEM((N_TP * hidden // 128, 1, 128), F32),
            pltpu.VMEM((2 + bits, 16, features), F32),
            dma((3 + nf * features // F_BLOCK,)),
            dma((2, 5, N_TP - 1)),
            dma((2, nb)),
            dma((2, 2, nb)),
            dma((2, 2, nb)),
            dma((2, 2, nb)),
            dma((2, n_all, n_chunks)),
            dma((2, 2 + bits)),
            dma((2, 3, N_TP - 1)),
            dma((2, 2, N_TP - 1, here)),
        ],
        compiler_params=pltpu.CompilerParams(collective_id=0, has_side_effects=True, vmem_limit_bytes=VMEM_LIMIT),
        name="encoder_layer",
    )(counts, tok, ext, og, proj, qkv, up, down, *vectors, qv_bias, table)


def widen_kernel(qkv_ref, proj_ref, down_ref, up_ref, out_ref, in_ref, small_ref, qkvo_ref, projo_ref, downo_ref,
                 upo_ref, outo_ref, ino_ref, qvo_ref, g1_ref, b1_ref, g2_ref, b2_ref, pb_ref, db_ref, ub_ref):
    for src, dst in ((qkv_ref, qkvo_ref), (proj_ref, projo_ref), (down_ref, downo_ref)):
        dst[...] = src[0].astype(F32)
    for src, dst in ((up_ref, upo_ref), (out_ref, outo_ref), (in_ref, ino_ref)):
        dst[...] = src[...].astype(F32)
    width = qvo_ref.shape[1]

    @pl.when(pl.program_id(0) == 0)
    def _():
        for i, ref in enumerate((g1_ref, b1_ref, g2_ref, b2_ref, pb_ref, db_ref, ub_ref)):
            ref[...] = small_ref[i, :]
        qvo_ref[0:1, :] = small_ref[7:8, 0:width]
        qvo_ref[1:2, :] = small_ref[7:8, 2 * width : 3 * width]


def widen_call(grads, up_grad, small, rows_out, rows_in, width):
    _, features, _ = grads.shape
    hidden = up_grad.shape[1]
    count, own_slots, _ = rows_out.shape
    steps = 4
    whole = pl.BlockSpec(memory_space=pltpu.VMEM)

    def rows_of(rows, first):
        return pl.BlockSpec((1, rows // steps, features), lambda i: (first[0], first[1] // (rows // steps) + i, 0))

    def flat(rows, cols):
        return pl.BlockSpec((rows // steps, cols), lambda i: (i, 0))

    clips = pl.BlockSpec((count // steps, own_slots, features), lambda i: (i, 0, 0))
    vector = jax.ShapeDtypeStruct((features,), F32)
    return pl.pallas_call(
        widen_kernel,
        grid=(steps,),
        out_shape=(
            jax.ShapeDtypeStruct((3 * width, features), F32),
            jax.ShapeDtypeStruct((width, features), F32),
            jax.ShapeDtypeStruct((hidden, features), F32),
            jax.ShapeDtypeStruct((features, hidden), F32),
            jax.ShapeDtypeStruct((count, own_slots, features), F32),
            jax.ShapeDtypeStruct((count, own_slots, features), F32),
            jax.ShapeDtypeStruct((2, width), F32),
        ) + (vector,) * 6 + (jax.ShapeDtypeStruct((hidden,), F32),),
        in_specs=[rows_of(3 * width, (0, 0)), rows_of(width, (0, 3 * width)), rows_of(hidden, (2, 0)),
                  flat(features, hidden), clips, clips, whole],
        out_specs=(flat(3 * width, features), flat(width, features), flat(hidden, features), flat(features, hidden),
                   clips, clips) + (whole,) * 8,
        compiler_params=pltpu.CompilerParams(vmem_limit_bytes=VMEM_LIMIT),
        name="widen",
    )(grads, grads, grads, up_grad, rows_out, rows_in, small)


def place_table(features, largest):
    half = features // 2
    freq = np.exp(-math.log(10000.0) * np.arange(half, dtype=np.float64) / half).astype(np.float32).astype(np.float64)
    parts = []
    for step in (TABLE, 1):
        angle = step * np.arange(TABLE, dtype=np.float64)[:, None] * freq
        values = np.concatenate([np.sin(angle), np.cos(angle)], axis=1).astype(np.float32)
        high = values.astype(BF)
        parts += [high, (values - high.astype(np.float32)).astype(BF)]
    return np.concatenate(parts, axis=0)


def per_device(n_clips, tokens, tubelet_index, visible_count, norm1_gain, norm1_bias, qkv_weight, qv_bias,
               proj_weight, proj_bias, norm2_gain, norm2_bias, up_weight, up_bias, down_weight, down_bias, out_grad):
    count, rows, features = tokens.shape
    width = qkv_weight.shape[2]
    hidden = up_weight.shape[1]
    qkv_t = jnp.transpose(qkv_weight, (1, 2, 0)).reshape(3 * width, features)
    vectors = (norm1_gain, norm1_bias, norm2_gain, norm2_bias, proj_bias, down_bias, up_bias)
    table = jnp.asarray(place_table(features, 2560))
    grads, up_grad, small, rows_out, rows_in = layer_call(
        n_clips, visible_count, tokens, tubelet_index, out_grad, proj_weight, qkv_t, up_weight, down_weight, vectors, qv_bias,
        table)
    qkv_grad, proj_grad, down_grad, up_grad, rows_out, rows_in, qv_grad, g1, b1, g2, b2, pb, db, ub = widen_call(
        grads, up_grad, small, rows_out, rows_in, width)
    qkv_grad = jnp.transpose(qkv_grad.reshape(3, width, features), (2, 0, 1))
    return rows_out, rows_in, g1, b1, qkv_grad, qv_grad, proj_grad, pb, g2, b2, up_grad, ub, down_grad, db


def solution(mesh):
    placed = (
        P("clips", "tp", None), P("clips", "tp"), P("clips"), P(), P(), P(None, None, "tp"), P(None, "tp"),
        P("tp", None), P(), P(), P(), P(None, "tp"), P("tp"), P("tp", None), P(), P("clips", "tp", None),
    )
    return jax.shard_map(
        functools.partial(per_device, mesh.shape["clips"]),
        mesh=mesh,
        in_specs=placed,
        out_specs=(
            P("clips", "tp", None), P("clips", "tp", None), P(), P(), P(None, None, "tp"), P(None, "tp"),
            P("tp", None), P(), P(), P(), P(None, "tp"), P("tp"), P("tp", None), P(),
        ),
        check_vma=False,
    )
```

```python
import functools
import math

import jax
import jax.numpy as jnp
import numpy as np
from jax import lax
from jax.experimental import pallas as pl
from jax.experimental.pallas import tpu as pltpu
from jax.sharding import PartitionSpec as P

HD = 64
EPSILON = 1e-06
NEGATIVE = -1000000000.0
BF = jnp.bfloat16
F32 = jnp.float32
MESH = pl.DeviceIdType.MESH
VMEM_LIMIT = 62 * 2**20
CHUNK = 128
F_BLOCK = 256
ROWS = 128
N_TP = 4
TABLE = 64
NN = (((1,), (0,)), ((), ()))
NT = (((1,), (1,)), ((), ()))
TN = (((0,), (0,)), ((), ()))


def dot(a, b, dims):
    return lax.dot_general(a, b, dims, preferred_element_type=F32)


def flip(value, weight):
    return value + weight - 2 * weight * lax.rem(lax.div(value, weight), 2)


def bit_of(value, weight):
    return lax.rem(lax.div(value, weight), 2)


def row(ref):
    return ref[...].reshape(1, ref.shape[0])


def div(value, by):
    return value // by if isinstance(value, int) else lax.div(value, by)


def mod(value, by):
    return value % by if isinstance(value, int) else lax.rem(value, by)


def aligned(value, multiple=16):
    return value if isinstance(value, int) else pl.multiple_of(value, multiple)


def gelu_parts(x):
    e = jnp.exp(-0.5 * x * x)
    z = jnp.abs(x) * (0.3275911 / math.sqrt(2.0))
    r = 1.0 / (1.0 + z)
    poly = r * (0.254829592 + r * (-0.284496736 + r * (1.421413741 + r * (-1.453152027 + r * 1.061405429))))
    tail = 0.5 * poly * e
    cdf = jnp.where(x >= 0, 1.0 - tail, tail)
    return x * cdf, cdf + x * (e * (1.0 / math.sqrt(2.0 * math.pi)))


def stats(v):
    mean = jnp.mean(v, axis=-1, keepdims=True)
    center = v - mean
    rstd = lax.rsqrt(jnp.mean(center * center, axis=-1, keepdims=True) + EPSILON)
    return center * rstd, rstd


def norm_back(v, dy, gain):
    xhat, rstd = stats(v)
    dx = dy * gain
    m1 = jnp.mean(dx, axis=-1, keepdims=True)
    m2 = jnp.mean(dx * xhat, axis=-1, keepdims=True)
    return (dx - m1 - xhat * m2) * rstd, jnp.sum(dy * xhat, axis=0, keepdims=True), jnp.sum(dy, axis=0, keepdims=True)


LAGS = (1, 2, 1, 1, 1, 1, 1, 2)
BACK = {("t", 2): [(n, piece) for n in (0, 1) for piece in range(4)]}


def reduce_plan(n_clips):
    plan = [("core", 0, CHUNK, False), ("side", 0, CHUNK, False)]
    rows = CHUNK
    gathers = []
    for bit in range(n_clips.bit_length() - 1):
        halving = rows >= 32
        if halving:
            rows //= 2
            gathers.append(("gather", bit, rows, True))
        plan.append(("reduce", bit, rows, halving))
    return plan, plan + gathers[::-1]


def layer_kernel(dims, n_clips, count_ref, tok_ref, ext_ref, og_ref, proj_ref, qkv_ref, up_ref, down_ref,
                 gain1_ref, bias1_ref, gain2_ref, bias2_ref, projb_ref, downb_ref, upb_ref, qvb_ref, table_ref,
                 grad_ref, upg_ref, small_ref, res_ref, ing_ref,
                 w, tokb, extb, ogb, qvb, upb, stream, first, qkvt, probs, mixed, middle, second, ff, sg, branch, outp,
                 inp, core_buf, side_buf, land, small, upsum, small_buf, l_sem, t_sem, y_sem, q_sem, f_sem, c_sem,
                 r_sem, s_sem, o_sem, b_sem):
    here, slots, width, hidden, features = dims
    bits = n_clips.bit_length() - 1
    c = lax.axis_index("clips")
    t = lax.axis_index("tp")
    k, u = bit_of(t, 1), bit_of(t, 2)
    core = (c, flip(t, 1))
    side = (c, flip(t, 2))
    across = (flip(c, 1), t)
    along = (flip(c, 2), t)
    others = [(c, lax.rem(t + i, N_TP)) for i in range(1, N_TP)]
    peers = [(flip(c, 2 ** bit), t) for bit in range(bits)]
    c_bits = [bit_of(c, 2 ** bit) for bit in range(bits)]
    own_slots = slots // N_TP
    n_rows = here * slots
    nf = hidden // F_BLOCK
    n_chunks = 3 * features // CHUNK
    b0, b1 = bit_of(c, 1), bit_of(c, 2)
    quarter = b1 * 2 + b0
    via_z = (1 - b1) * 2 + b0
    via_x = b1 * 2 + (1 - b0)
    blocks = [(0, 1, F_BLOCK * j, F_BLOCK) for j in range(features // F_BLOCK)] + [
        (1, 2, F_BLOCK * j, F_BLOCK) for j in range(nf)]
    na = features // F_BLOCK
    nb = len(blocks)
    half = features // 2
    tiles = features // F_BLOCK

    def weights_in():
        copies = [pltpu.make_async_copy(qkv_ref, w.at[u, k, 0, pl.ds(0, 3 * width)], l_sem.at[0]),
                  pltpu.make_async_copy(proj_ref, w.at[u, k, 0, pl.ds(3 * width, width)], l_sem.at[1]),
                  pltpu.make_async_copy(down_ref, w.at[u, k, 2], l_sem.at[2])]
        for i in range(tiles):
            for j in range(nf):
                copies.append(pltpu.make_async_copy(
                    up_ref.at[pl.ds(F_BLOCK * i, F_BLOCK), pl.ds(F_BLOCK * j, F_BLOCK)], probs.at[0, i * nf + j],
                    l_sem.at[3 + i * nf + j]))
        return copies

    def row_copies():
        mine = pl.ds(t * here, here)
        cols = pl.ds(t * own_slots, own_slots)
        return [pltpu.make_async_copy(tok_ref.at[mine], tokb.at[:, cols], o_sem.at[0, 2, 0]),
                pltpu.make_async_copy(og_ref.at[mine], ogb.at[:, cols], o_sem.at[0, 2, 1]),
                pltpu.make_async_copy(ext_ref, extb.at[t], o_sem.at[0, 2, 2]),
                pltpu.make_async_copy(qvb_ref, qvb.at[t], o_sem.at[1, 2, 0])]

    own_w = weights_in()
    for copy in own_w + row_copies():
        copy.start()

    barrier = pltpu.get_barrier_semaphore()
    targets = others + peers
    for target in targets:
        pl.semaphore_signal(barrier, inc=1, device_id=target, device_id_type=MESH)
    pl.semaphore_wait(barrier, len(targets))

    def remote(src, dst, sem, index, target):
        return pltpu.make_async_remote_copy(src_ref=src, dst_ref=dst, send_sem=sem.at[(0, *index)],
                                            recv_sem=sem.at[(1, *index)], device_id=target, device_id_type=MESH)

    def rows_copy(n, i):
        target = others[i]
        mine = pl.ds(target[1] * here, here)
        cols = pl.ds(t * own_slots, own_slots)
        src, dst = (lambda: (tok_ref.at[mine], tokb.at[:, cols]), lambda: (ext_ref, extb.at[t]),
                    lambda: (og_ref.at[mine], ogb.at[:, cols]), lambda: (qvb_ref, qvb.at[t]),
                    lambda: (upb.at[t], upb.at[t]))[n]()
        return remote(src, dst, t_sem, (n, i), target)

    def w_copy(kind, i):
        part, parts, base, rows = blocks[i]
        q, h = rows // 4, rows // 8
        su, start, size, sem, index, target = {
            "y": (u, base + quarter * q, q, y_sem, (i,), side),
            "x": (1 - u, base + quarter * q, q, q_sem, (0, i), across),
            "z": (1 - u, base + quarter * q, q, q_sem, (1, i), along),
            "xf": (1 - u, base + via_z * q, h, f_sem, (0, i), across),
            "zf": (1 - u, base + via_x * q + h, h, f_sem, (1, i), along),
            "co": (u, base, rows, c_sem, (0, i), core),
            "cf": (1 - u, base, rows, c_sem, (1, i), core),
        }[kind]
        view = w.at[su, k, pl.ds(part, parts), pl.ds(aligned(start), size)]
        return remote(view, view, sem, index, target)

    def step1(i):
        w_copy("y", i).wait_recv()
        w_copy("x", i).start()
        w_copy("z", i).start()

    def step2(i):
        w_copy("z", i).wait_recv()
        w_copy("xf", i).start()
        w_copy("x", i).wait_recv()
        w_copy("zf", i).start()

    def step3(i):
        w_copy("xf", i).wait_recv()
        w_copy("zf", i).wait_recv()
        w_copy("cf", i).start()

    def step4(i):
        w_copy("cf", i).wait_recv()
        for kind in ("x", "z", "xf", "zf", "cf"):
            w_copy(kind, i).wait_send()

    def step_own(i):
        w_copy("co", i).wait_recv()
        for kind in ("y", "co"):
            w_copy(kind, i).wait_send()

    def start_rows(n):
        for i in range(N_TP - 1):
            rows_copy(n, i).start()

    def wait_rows(n):
        for i in range(N_TP - 1):
            rows_copy(n, i).wait_recv()

    upb[pl.ds(t, 1), :, :] = row(upb_ref).reshape(1, 1, hidden)
    own_w[0].wait()
    for i in range(na):
        if i == na - 1:
            own_w[1].wait()
        w_copy("y", i).start()
    for n in (1, 3, 4):
        start_rows(n)
    for i in range(na):
        w_copy("co", i).start()
    for copy in own_w[2:]:
        copy.wait()
    for i in range(tiles):
        for j in range(nf):
            w[u, k, 1, j * F_BLOCK : (j + 1) * F_BLOCK, i * F_BLOCK : (i + 1) * F_BLOCK] = probs[0, i * nf + j].T
    for copy in row_copies():
        copy.wait()

    step1(0)
    start_rows(0)
    small[...] = jnp.zeros_like(small)
    step1(1)
    step2(0)
    step1(2)
    w_copy("y", na).start()
    ff[...] = jnp.zeros_like(ff)
    sg[...] = jnp.zeros_like(sg)
    step2(1)
    step2(2)
    for n in (1, 3, 4, 0):
        wait_rows(n)
    start_rows(2)

    per_clip = slots // ROWS
    sources = ROWS // own_slots

    def rows_at(i):
        return lax.div(i, per_clip), pl.ds(pl.multiple_of(lax.rem(i, per_clip) * ROWS, ROWS), ROWS), pl.ds(
            pl.multiple_of(i * ROWS, ROWS), ROWS)

    def first_rows(i, _):
        b, here_rows, rows = rows_at(i)
        line = lax.broadcasted_iota(jnp.int32, (2 * TABLE, own_slots), 0) & (TABLE - 1)
        pos = []
        for n in range(sources):
            place = extb[lax.rem(i, per_clip) * sources + n, pl.ds(t * here + b, 1), :]
            hot = [jnp.where(line == lax.broadcast_in_dim(v, line.shape, (0, 1)), 1.0, 0.0).astype(BF)
                   for v in (lax.shift_right_logical(place, 6), place & (TABLE - 1))]
            hi = dot(hot[0], table_ref[0 : 2 * TABLE, :], TN)
            lo = dot(hot[1], table_ref[2 * TABLE :, :], TN)
            sh, ch, sl, cl = hi[:, :half], hi[:, half:], lo[:, :half], lo[:, half:]
            pos.append(jnp.concatenate([sh * cl + ch * sl, ch * cl - sh * sl], axis=1))
        v = tokb[b, here_rows, :].astype(F32) + jnp.concatenate(pos, axis=0)
        stream[rows, :] = v
        xhat, _ = stats(v)
        first[rows, :] = (xhat * row(gain1_ref) + row(bias1_ref)).astype(BF)
        return 0

    lax.fori_loop(0, n_rows // ROWS, first_rows, 0)
    for i in range(na):
        step_own(i)
    for i in range(na, nb):
        w_copy("co", i).start()

    scale = HD ** -0.5

    def group(n):
        gu, gk = lax.rem(u + lax.div(n, 2), 2), lax.rem(n, 2)
        return gu * 2 + gk, gu, gk

    def qkv_of(n):
        g, gu, gk = group(n)
        out = dot(w[gu, gk, 0, 0 : 3 * width, :], first[...], NT)
        add = jnp.concatenate([qvb[g, :, :], jnp.zeros((6, width), F32)], axis=0)
        add = jnp.concatenate([add, jnp.zeros((8, 64), F32)], axis=1).T
        qkvt[g, 0:width, :] = ((out[0:width] + add[0:width, 0:1]).astype(BF).astype(F32) * scale).astype(BF)
        qkvt[g, width : 2 * width, :] = out[width : 2 * width].astype(BF)
        qkvt[g, 2 * width :, :] = (out[2 * width :] + add[0:width, 1:2]).astype(BF)


    per_group = width // HD

    def attend(n, _):
        @pl.when(n == 1)
        def _():
            for i in range(na):
                step3(i)

        @pl.when(n == 2)
        def _():
            for i in range(na):
                step4(i)

        qkv_of(n)
        g, _, _ = group(n)
        for b in range(here):
            cols = slice(b * slots, (b + 1) * slots)
            visible = count_ref[t * here + b]
            keep = lax.broadcasted_iota(jnp.int32, (slots, slots), 0) < visible
            for r in range(per_group):
                q = qkvt[g, r * HD : (r + 1) * HD, cols]
                key = qkvt[g, width + r * HD : width + (r + 1) * HD, cols]
                value = qkvt[g, 2 * width + r * HD : 2 * width + (r + 1) * HD, cols]
                s = jnp.where(keep, dot(key, q, TN), NEGATIVE)
                e = jnp.exp(s - jnp.max(s, axis=0, keepdims=True))
                p = (e * (1.0 / jnp.sum(e, axis=0, keepdims=True))).astype(BF)
                probs[b, g * per_group + r] = p
                mixed[g, r * HD : (r + 1) * HD, cols] = dot(value, p, NN).astype(BF)

        for at, work in ((0, lambda: (step1(na), w_copy("y", na + 1).start())),
                         (1, lambda: w_copy("y", na + 2).start()), (2, lambda: step2(na))):
            @pl.when(n == at)
            def _():
                work()

        return 0

    lax.fori_loop(0, N_TP, attend, 0)

    def second_rows(i, _):
        _, _, rows = rows_at(i)
        total = stream[rows, :] + row(projb_ref)
        for g in range(N_TP):
            total = total + dot(mixed[g, :, rows], w[g // 2, g % 2, 0, 3 * width :, :], TN)
        middle[rows, :] = total
        xhat, _ = stats(total)
        second[rows, :] = (xhat * row(gain2_ref) + row(bias2_ref)).astype(BF)
        return 0

    lax.fori_loop(0, n_rows // ROWS, second_rows, 0)
    step3(na)
    step_own(na)
    wait_rows(2)

    sums, plan = reduce_plan(n_clips)
    n_all = len(plan)
    f_chunks = nf * 2 * F_BLOCK // CHUNK
    per_f = F_BLOCK // CHUNK

    def place_of(chunk):
        last = div(chunk, f_chunks)
        in_block = mod(chunk, 2 * per_f)
        part = (1 - last) * (1 + mod(in_block, 2))
        row = (1 - last) * (div(chunk, 2 * per_f) * F_BLOCK + div(in_block, 2) * CHUNK)
        return part, row + last * (chunk - f_chunks) * CHUNK

    def kept(stage):
        start = 0
        for kind, bit, rows, halving in sums[:stage]:
            if halving:
                start = start + c_bits[bit] * rows
        return start

    def land_at(stage, chunk):
        return chunk * sum(p[2] for p in sums[2:]) + sum(p[2] for p in sums[2:stage])

    def copy_of(stage, chunk):
        kind, bit, rows, halving = plan[stage]
        base = chunk * CHUNK
        if kind == "core":
            part, row = place_of(chunk)
            src = w.at[:, 1 - k, part, pl.ds(aligned(row), CHUNK)]
            dst, target = core_buf.at[:, pl.ds(aligned(base), CHUNK)], core
        elif kind == "side":
            at = pl.ds(aligned(base), rows)
            src, dst, target = core_buf.at[1 - u, at], side_buf.at[at], side
        elif kind == "reduce":
            start = base + kept(stage)
            if halving:
                start = start + (1 - c_bits[bit]) * rows
            src = side_buf.at[pl.ds(aligned(start), rows)]
            dst, target = land.at[pl.ds(aligned(land_at(stage, chunk)), rows)], peers[bit]
        else:
            part, row = place_of(chunk)
            src = grad_ref.at[part, pl.ds(aligned(row + kept(bit + 3)), rows)]
            dst, target = src, peers[bit]
        send = chunk if kind == "reduce" and not halving else 0
        return pltpu.make_async_remote_copy(
            src_ref=src, dst_ref=dst, send_sem=r_sem.at[0, stage, send], recv_sem=r_sem.at[1, stage, chunk],
            device_id=target, device_id_type=MESH)

    def add(a, b):
        return (a.astype(F32) + b.astype(F32)).astype(BF)

    def finish(stage, chunk):
        copy_of(stage, chunk).wait_recv()
        kind, bit, rows, halving = plan[stage]
        base = chunk * CHUNK
        if kind == "core":
            part, row = place_of(chunk)
            at = pl.ds(aligned(base), CHUNK)
            for n in (0, 1):
                core_buf[n, at] = add(w[n, k, part, pl.ds(aligned(row), CHUNK)], core_buf[n, at])
        elif kind == "side":
            at = pl.ds(aligned(base), rows)
            side_buf[at] = add(core_buf[u, at], side_buf[at])
        elif kind == "reduce":
            at = pl.ds(aligned(base + kept(stage + 1)), rows)
            if not halving:
                copy_of(stage, chunk).wait_send()
            total = add(side_buf[at], land[pl.ds(aligned(land_at(stage, chunk)), rows)])
            if stage == len(sums) - 1:
                part, row = place_of(chunk)
                grad_ref[part, pl.ds(aligned(row + kept(stage + 1)), rows)] = total
            else:
                side_buf[at] = total

    lags = list(LAGS) + [1] * 32
    starts = [sum(lags[:n]) for n in range(n_all + 1)]

    def step(stage, chunk):
        if stage > 0:
            finish(stage - 1, chunk)
        if stage < n_all:
            copy_of(stage, chunk).start()

    def tick(i):
        for stage in range(n_all + 1):
            chunk = i - starts[stage]

            @pl.when((chunk >= 0) & (chunk < n_chunks))
            def _():
                step(stage, chunk)

    def ffn(gu, start, size):
        hid = pl.ds(pl.multiple_of(start, size), size)
        up = w[gu, :, 1, hid, :].reshape(2 * size, features)
        down = w[gu, :, 2, hid, :].reshape(2 * size, features)
        pre = dot(second[...], up, NT) + jnp.concatenate([upb[2 * gu, :, hid], upb[2 * gu + 1, :, hid]], axis=1)
        act, slope = gelu_parts(pre)
        act = act.astype(BF)
        ff[...] += dot(act, down, NN)
        og = ogb[...].reshape(n_rows, features)
        pg = (dot(og, down, NT) * slope).astype(BF)
        sg[...] += dot(pg, up, NN)
        w[gu, :, 2, hid, :] = dot(act, og, TN).astype(BF).reshape(2, size, features)
        w[gu, :, 1, hid, :] = dot(pg, second[...], TN).astype(BF).reshape(2, size, features)
        sums = jnp.sum(pg.astype(F32), axis=0, keepdims=True)
        for gk in (0, 1):
            for m in range(size // 128):
                at = gk * size + m * 128
                upsum[(2 * gu + gk) * (hidden // 128) + lax.div(start, 128) + m] = sums[:, at : at + 128]

    def hooks(i, *work):
        for at, do in work:
            @pl.when(i == at)
            def _():
                do()

    def ffn_block(i, _):
        hooks(i, (0, lambda: step1(na + 1)), (1, lambda: step4(na)),
              (2, lambda: (step_own(na + 1), step2(na + 1), step1(na + 2))),
              (3, lambda: (step3(na + 1), step4(na + 1), step2(na + 2))),
              (4, lambda: (step_own(na + 2), step3(na + 2))), (5, lambda: step4(na + 2)))
        ffn(lax.rem(u + i, 2), lax.div(i, 2) * F_BLOCK, F_BLOCK)

        @pl.when(i >= 1)
        def _():
            tick(2 * i - 2)
            tick(2 * i - 1)

        return 0

    lax.fori_loop(0, nf * 2, ffn_block, 0)
    done = 4 * nf - 2
    for g in range(N_TP):
        for m in range(hidden // 128):
            small[8 + g : 9 + g, m * 128 : (m + 1) * 128] = upsum[g * (hidden // 128) + m]

    def middle_rows(i, _):
        b, here_rows, rows = rows_at(i)
        m = middle[rows, :]
        outp[b, here_rows, :] = (m + ff[rows, :] + row(downb_ref)).astype(BF)
        dv, dgain, dbias = norm_back(m, sg[rows, :], row(gain2_ref))
        og = ogb[b, here_rows, :].astype(F32)
        mg = og + dv
        ff[rows, :] = mg
        bg = mg.astype(BF)
        branch[rows, :] = bg
        small[2:3, :] += dgain
        small[3:4, :] += dbias
        small[4:5, :] += jnp.sum(bg.astype(F32), axis=0, keepdims=True)
        small[5:6, :] += jnp.sum(og, axis=0, keepdims=True)
        return 0

    lax.fori_loop(0, n_rows // ROWS, middle_rows, 0)

    def back_copy(n, i, b):
        src, dst = ((outp, res_ref), (inp, ing_ref))[n]
        target = others[i]
        return remote(src.at[b, pl.ds(target[1] * own_slots, own_slots)], dst.at[t * here + b], b_sem, (n, i, b), target)

    def back_own(n):
        src, dst = ((outp, res_ref), (inp, ing_ref))[n]
        return pltpu.make_async_copy(src.at[:, pl.ds(t * own_slots, own_slots)], dst.at[pl.ds(t * here, here)],
                                     l_sem.at[n])

    back_pieces = [(i, b) for i in range(N_TP - 1) for b in range(here)]

    def send_back(n, at):
        if at == 0:
            back_own(n).start()
        for i, b in back_pieces[at::4]:
            back_copy(n, i, b).start()

    sg[...] = jnp.zeros_like(sg)

    def back_group(g, _):
        gu, gk = lax.div(g, 2), lax.rem(g, 2)
        bg = branch[...]
        dmix = dot(w[gu, gk, 0, 3 * width :, :], bg, NT).astype(BF)
        w[gu, gk, 0, 3 * width :, :] = dot(mixed[g], bg, NN).astype(BF)
        for b in range(here):
            cols = slice(b * slots, (b + 1) * slots)
            for r in range(per_group):
                q_rows = slice(r * HD, (r + 1) * HD)
                k_rows = slice(width + r * HD, width + (r + 1) * HD)
                v_rows = slice(2 * width + r * HD, 2 * width + (r + 1) * HD)
                q, key, value = qkvt[g, q_rows, cols], qkvt[g, k_rows, cols], qkvt[g, v_rows, cols]
                dm = dmix[q_rows, cols]
                p = probs[b, g * per_group + r]
                pf = p.astype(F32)
                dp = dot(value, dm, TN)
                ds = (pf * (dp - jnp.sum(pf * dp, axis=0, keepdims=True))).astype(BF)
                qkvt[g, q_rows, cols] = (dot(key, ds, NN) * scale).astype(BF)
                qkvt[g, k_rows, cols] = dot(q, ds, NT).astype(BF)
                qkvt[g, v_rows, cols] = dot(dm, p, NT).astype(BF)
        dqkv = qkvt[g]
        sg[...] += dot(dqkv, w[gu, gk, 0, 0 : 3 * width, :], TN)
        w[gu, gk, 0, 0 : 3 * width, :] = dot(dqkv, first[...], NN).astype(BF)
        small[pl.ds(12 + g, 1), 0 : 3 * width] = dot(jnp.ones((8, n_rows), BF), dqkv, NT)[0:1]
        @pl.when(lax.rem(g, 2) == 0)
        def _():
            tick(done + lax.div(g, 2))

        return 0

    lax.fori_loop(0, N_TP, back_group, 0)

    def last_rows(i, _):
        b, here_rows, rows = rows_at(i)
        dv, dgain, dbias = norm_back(stream[rows, :], sg[rows, :], row(gain1_ref))
        inp[b, here_rows, :] = (ff[rows, :] + dv).astype(BF)
        small[0:1, :] += dgain
        small[1:2, :] += dbias
        return 0

    lax.fori_loop(0, n_rows // ROWS, last_rows, 0)

    small_targets = [core, side] + peers

    def small_copy(i):
        return remote(small, small_buf.at[i], s_sem, (i,), small_targets[i])

    done = done + N_TP // 2

    def small_turn(n):
        if n > len(small_targets):
            return
        if n > 0:
            small_copy(n - 1).wait()
            small[...] += small_buf[n - 1]
        if n < len(small_targets):
            small_copy(n).start()

    def rest_of(i, _):
        tick(i)
        hooks(i, *((done + n, functools.partial(small_turn, n)) for n in range(n_chunks - done)))
        return 0

    lax.fori_loop(done, n_chunks, rest_of, 0)
    state = {}
    for chunk in range(n_chunks):
        stage = max(n for n in range(n_all + 1) if chunk + starts[n] < n_chunks)
        if stage < n_all:
            state[chunk] = stage
    turn = 0
    up_left = True
    small_left = list(range(n_chunks - done, len(small_targets) + 1))
    while state or small_left:
        for n, piece in BACK.get(("t", turn), ()):
            send_back(n, piece)
        if small_left:
            small_turn(small_left.pop(0))
        for chunk in sorted(state, reverse=True):
            state[chunk] += 1
            step(state[chunk], chunk)
            if state[chunk] == n_all:
                del state[chunk]
        if up_left and not [chunk for chunk in state if chunk < f_chunks]:
            up_left = False
            for m in range(tiles):
                for j in range(nf):
                    upg_ref[m * F_BLOCK : (m + 1) * F_BLOCK, j * F_BLOCK : (j + 1) * F_BLOCK] = grad_ref[
                        1, j * F_BLOCK : (j + 1) * F_BLOCK, m * F_BLOCK : (m + 1) * F_BLOCK].T
        turn += 1
    small_ref[0:6, :] = small[0:6, :]
    small_ref[6:7, :] = small[pl.ds(8 + t, 1), :]
    small_ref[7:8, :] = small[pl.ds(12 + t, 1), :]

    for n in (0, 1):
        for i, b in back_pieces:
            back_copy(n, i, b).wait_recv()
            back_copy(n, i, b).wait_send()
        back_own(n).wait()
    for n in range(5):
        for i in range(N_TP - 1):
            rows_copy(n, i).wait_send()

    for stage, (kind, _, rows, halving) in enumerate(plan):
        if kind != "reduce" or halving:
            view = core_buf if kind == "core" else side_buf.at[pl.ds(0, n_chunks * rows)]
            pltpu.make_async_remote_copy(
                src_ref=view, dst_ref=view, send_sem=r_sem.at[0, stage, 0], recv_sem=r_sem.at[1, stage, 0],
                device_id=core, device_id_type=MESH).wait_send()


def layer_call(n_clips, counts, tok, ext, og, proj, qkv, up, down, vectors, qv_bias, table):
    count, own_slots, features = tok.shape
    width = proj.shape[0]
    hidden = up.shape[1]
    here = count // N_TP
    slots = own_slots * N_TP
    n_rows = here * slots
    nf = hidden // F_BLOCK
    n_chunks = 3 * features // CHUNK
    heads = features // HD
    bits = n_clips.bit_length() - 1
    sums, plan = reduce_plan(n_clips)
    n_all = len(plan)
    hbm = pl.BlockSpec(memory_space=pl.ANY)
    vmem = pl.BlockSpec(memory_space=pltpu.VMEM)
    smem = pl.BlockSpec(memory_space=pltpu.SMEM)
    dma = pltpu.SemaphoreType.DMA
    nb = nf + features // F_BLOCK
    return pl.pallas_call(
        functools.partial(layer_kernel, (here, slots, width, hidden, features), n_clips),
        out_shape=(
            jax.ShapeDtypeStruct((3, features, features), BF),
            jax.ShapeDtypeStruct((features, hidden), BF),
            jax.ShapeDtypeStruct((8, features), F32),
            jax.ShapeDtypeStruct((count, own_slots, features), BF),
            jax.ShapeDtypeStruct((count, own_slots, features), BF),
        ),
        in_specs=[smem, hbm, vmem] + [hbm] * 5 + [vmem] * 9,
        out_specs=(vmem, vmem, vmem, hbm, hbm),
        scratch_shapes=[
            pltpu.VMEM((2, 2, 3, features, features), BF),
            pltpu.VMEM((here, slots, features), BF),
            pltpu.VMEM((N_TP, *ext.shape), jnp.int32),
            pltpu.VMEM((here, slots, features), BF),
            pltpu.VMEM((N_TP, *qv_bias.shape), F32),
            pltpu.VMEM((N_TP, 1, hidden), F32),
            pltpu.VMEM((n_rows, features), F32),
            pltpu.VMEM((n_rows, features), BF),
            pltpu.VMEM((N_TP, 3 * width, n_rows), BF),
            pltpu.VMEM((here, heads, slots, slots), BF),
            pltpu.VMEM((N_TP, width, n_rows), BF),
            pltpu.VMEM((n_rows, features), F32),
            pltpu.VMEM((n_rows, features), BF),
            pltpu.VMEM((n_rows, features), F32),
            pltpu.VMEM((n_rows, features), F32),
            pltpu.VMEM((n_rows, features), BF),
            pltpu.VMEM((here, slots, features), BF),
            pltpu.VMEM((here, slots, features), BF),
            pltpu.VMEM((2, 3 * features, features), BF),
            pltpu.VMEM((3 * features, features), BF),
            pltpu.VMEM((n_chunks * sum(p[2] for p in sums[2:]), features), BF),
            pltpu.VMEM((16, features), F32),
            pltpu.VMEM((N_TP * hidden // 128, 1, 128), F32),
            pltpu.VMEM((2 + bits, 16, features), F32),
            dma((3 + nf * features // F_BLOCK,)),
            dma((2, 5, N_TP - 1)),
            dma((2, nb)),
            dma((2, 2, nb)),
            dma((2, 2, nb)),
            dma((2, 2, nb)),
            dma((2, n_all, n_chunks)),
            dma((2, 2 + bits)),
            dma((2, 3, N_TP - 1)),
            dma((2, 2, N_TP - 1, here)),
        ],
        compiler_params=pltpu.CompilerParams(collective_id=0, has_side_effects=True, vmem_limit_bytes=VMEM_LIMIT),
        name="encoder_layer",
    )(counts, tok, ext, og, proj, qkv, up, down, *vectors, qv_bias, table)


def widen_kernel(qkv_ref, proj_ref, down_ref, up_ref, out_ref, in_ref, small_ref, qkvo_ref, projo_ref, downo_ref,
                 upo_ref, outo_ref, ino_ref, qvo_ref, g1_ref, b1_ref, g2_ref, b2_ref, pb_ref, db_ref, ub_ref):
    for src, dst in ((qkv_ref, qkvo_ref), (proj_ref, projo_ref), (down_ref, downo_ref)):
        dst[...] = src[0].astype(F32)
    for src, dst in ((up_ref, upo_ref), (out_ref, outo_ref), (in_ref, ino_ref)):
        dst[...] = src[...].astype(F32)
    width = qvo_ref.shape[1]

    @pl.when(pl.program_id(0) == 0)
    def _():
        for i, ref in enumerate((g1_ref, b1_ref, g2_ref, b2_ref, pb_ref, db_ref, ub_ref)):
            ref[...] = small_ref[i, :]
        qvo_ref[0:1, :] = small_ref[7:8, 0:width]
        qvo_ref[1:2, :] = small_ref[7:8, 2 * width : 3 * width]


def widen_call(grads, up_grad, small, rows_out, rows_in, width):
    _, features, _ = grads.shape
    hidden = up_grad.shape[1]
    count, own_slots, _ = rows_out.shape
    steps = 2
    whole = pl.BlockSpec(memory_space=pltpu.VMEM)

    def rows_of(rows, first):
        return pl.BlockSpec((1, rows // steps, features), lambda i: (first[0], first[1] // (rows // steps) + i, 0))

    def flat(rows, cols):
        return pl.BlockSpec((rows // steps, cols), lambda i: (i, 0))

    clips = pl.BlockSpec((count // steps, own_slots, features), lambda i: (i, 0, 0))
    vector = jax.ShapeDtypeStruct((features,), F32)
    return pl.pallas_call(
        widen_kernel,
        grid=(steps,),
        out_shape=(
            jax.ShapeDtypeStruct((3 * width, features), F32),
            jax.ShapeDtypeStruct((width, features), F32),
            jax.ShapeDtypeStruct((hidden, features), F32),
            jax.ShapeDtypeStruct((features, hidden), F32),
            jax.ShapeDtypeStruct((count, own_slots, features), F32),
            jax.ShapeDtypeStruct((count, own_slots, features), F32),
            jax.ShapeDtypeStruct((2, width), F32),
        ) + (vector,) * 6 + (jax.ShapeDtypeStruct((hidden,), F32),),
        in_specs=[rows_of(3 * width, (0, 0)), rows_of(width, (0, 3 * width)), rows_of(hidden, (2, 0)),
                  flat(features, hidden), clips, clips, whole],
        out_specs=(flat(3 * width, features), flat(width, features), flat(hidden, features), flat(features, hidden),
                   clips, clips) + (whole,) * 8,
        compiler_params=pltpu.CompilerParams(vmem_limit_bytes=VMEM_LIMIT),
        name="widen",
    )(grads, grads, grads, up_grad, rows_out, rows_in, small)


def place_table(features, largest):
    half = features // 2
    freq = np.exp(-math.log(10000.0) * np.arange(half, dtype=np.float64) / half).astype(np.float32).astype(np.float64)
    parts = []
    for step in (TABLE, 1):
        angle = step * np.arange(TABLE, dtype=np.float64)[:, None] * freq
        values = np.concatenate([np.sin(angle), np.cos(angle)], axis=1).astype(np.float32)
        high = values.astype(BF)
        parts += [high, (values - high.astype(np.float32)).astype(BF)]
    return np.concatenate(parts, axis=0)


def per_device(n_clips, tokens, tubelet_index, visible_count, norm1_gain, norm1_bias, qkv_weight, qv_bias,
               proj_weight, proj_bias, norm2_gain, norm2_bias, up_weight, up_bias, down_weight, down_bias, out_grad):
    count, rows, features = tokens.shape
    width = qkv_weight.shape[2]
    hidden = up_weight.shape[1]
    qkv_t = jnp.transpose(qkv_weight, (1, 2, 0)).reshape(3 * width, features)
    vectors = (norm1_gain, norm1_bias, norm2_gain, norm2_bias, proj_bias, down_bias, up_bias)
    table = jnp.asarray(place_table(features, 2560))
    grads, up_grad, small, rows_out, rows_in = layer_call(
        n_clips, visible_count, tokens, tubelet_index, out_grad, proj_weight, qkv_t, up_weight, down_weight, vectors, qv_bias,
        table)
    qkv_grad, proj_grad, down_grad, up_grad, rows_out, rows_in, qv_grad, g1, b1, g2, b2, pb, db, ub = widen_call(
        grads, up_grad, small, rows_out, rows_in, width)
    qkv_grad = jnp.transpose(qkv_grad.reshape(3, width, features), (2, 0, 1))
    return rows_out, rows_in, g1, b1, qkv_grad, qv_grad, proj_grad, pb, g2, b2, up_grad, ub, down_grad, db


def solution(mesh):
    placed = (
        P("clips", "tp", None), P("clips", "tp"), P("clips"), P(), P(), P(None, None, "tp"), P(None, "tp"),
        P("tp", None), P(), P(), P(), P(None, "tp"), P("tp"), P("tp", None), P(), P("clips", "tp", None),
    )
    return jax.shard_map(
        functools.partial(per_device, mesh.shape["clips"]),
        mesh=mesh,
        in_specs=placed,
        out_specs=(
            P("clips", "tp", None), P("clips", "tp", None), P(), P(), P(None, None, "tp"), P(None, "tp"),
            P("tp", None), P(), P(), P(), P(None, "tp"), P("tp"), P("tp", None), P(),
        ),
        check_vma=False,
    )
```

```python
import functools
import math

import jax
import jax.numpy as jnp
import numpy as np
from jax import lax
from jax.experimental import pallas as pl
from jax.experimental.pallas import tpu as pltpu
from jax.sharding import PartitionSpec as P

HD = 64
EPSILON = 1e-06
NEGATIVE = -1000000000.0
BF = jnp.bfloat16
F32 = jnp.float32
MESH = pl.DeviceIdType.MESH
VMEM_LIMIT = 62 * 2**20
CHUNK = 128
F_BLOCK = 256
ROWS = 128
N_TP = 4
TABLE = 64
NN = (((1,), (0,)), ((), ()))
NT = (((1,), (1,)), ((), ()))
TN = (((0,), (0,)), ((), ()))


def dot(a, b, dims):
    return lax.dot_general(a, b, dims, preferred_element_type=F32)


def flip(value, weight):
    return value + weight - 2 * weight * lax.rem(lax.div(value, weight), 2)


def bit_of(value, weight):
    return lax.rem(lax.div(value, weight), 2)


def row(ref):
    return ref[...].reshape(1, ref.shape[0])


def div(value, by):
    return value // by if isinstance(value, int) else lax.div(value, by)


def mod(value, by):
    return value % by if isinstance(value, int) else lax.rem(value, by)


def aligned(value, multiple=16):
    return value if isinstance(value, int) else pl.multiple_of(value, multiple)


def gelu_parts(x):
    e = jnp.exp(-0.5 * x * x)
    z = jnp.abs(x) * (0.3275911 / math.sqrt(2.0))
    r = 1.0 / (1.0 + z)
    poly = r * (0.254829592 + r * (-0.284496736 + r * (1.421413741 + r * (-1.453152027 + r * 1.061405429))))
    tail = 0.5 * poly * e
    cdf = jnp.where(x >= 0, 1.0 - tail, tail)
    return x * cdf, cdf + x * (e * (1.0 / math.sqrt(2.0 * math.pi)))


def stats(v):
    mean = jnp.mean(v, axis=-1, keepdims=True)
    center = v - mean
    rstd = lax.rsqrt(jnp.mean(center * center, axis=-1, keepdims=True) + EPSILON)
    return center * rstd, rstd


def norm_back(v, dy, gain):
    xhat, rstd = stats(v)
    dx = dy * gain
    m1 = jnp.mean(dx, axis=-1, keepdims=True)
    m2 = jnp.mean(dx * xhat, axis=-1, keepdims=True)
    return (dx - m1 - xhat * m2) * rstd, jnp.sum(dy * xhat, axis=0, keepdims=True), jnp.sum(dy, axis=0, keepdims=True)


LAGS = (1, 2, 1, 1, 1, 1, 1, 2)
BACK = {("t", 2): [(n, piece) for n in (0, 1) for piece in range(4)]}


def reduce_plan(n_clips):
    plan = [("core", 0, CHUNK, False), ("side", 0, CHUNK, False)]
    rows = CHUNK
    gathers = []
    for bit in range(n_clips.bit_length() - 1):
        halving = rows >= 32
        if halving:
            rows //= 2
            gathers.append(("gather", bit, rows, True))
        plan.append(("reduce", bit, rows, halving))
    return plan, plan + gathers[::-1]


def layer_kernel(dims, n_clips, count_ref, tok_ref, ext_ref, og_ref, proj_ref, qkv_ref, up_ref, down_ref,
                 gain1_ref, bias1_ref, gain2_ref, bias2_ref, projb_ref, downb_ref, upb_ref, qvb_ref, table_ref,
                 grad_ref, upg_ref, small_ref, res_ref, ing_ref,
                 w, tokb, extb, ogb, qvb, upb, stream, first, qkvt, probs, mixed, middle, second, ff, sg, branch, outp,
                 inp, core_buf, side_buf, land, small, upsum, small_buf, l_sem, t_sem, y_sem, q_sem, f_sem, c_sem,
                 r_sem, s_sem, o_sem, b_sem):
    here, slots, width, hidden, features = dims
    bits = n_clips.bit_length() - 1
    c = lax.axis_index("clips")
    t = lax.axis_index("tp")
    k, u = bit_of(t, 1), bit_of(t, 2)
    core = (c, flip(t, 1))
    side = (c, flip(t, 2))
    across = (flip(c, 1), t)
    along = (flip(c, 2), t)
    others = [(c, lax.rem(t + i, N_TP)) for i in range(1, N_TP)]
    peers = [(flip(c, 2 ** bit), t) for bit in range(bits)]
    c_bits = [bit_of(c, 2 ** bit) for bit in range(bits)]
    own_slots = slots // N_TP
    n_rows = here * slots
    nf = hidden // F_BLOCK
    n_chunks = 3 * features // CHUNK
    b0, b1 = bit_of(c, 1), bit_of(c, 2)
    quarter = b1 * 2 + b0
    via_z = (1 - b1) * 2 + b0
    via_x = b1 * 2 + (1 - b0)
    blocks = [(0, 1, F_BLOCK * j, F_BLOCK) for j in range(features // F_BLOCK)] + [
        (1, 2, F_BLOCK * j, F_BLOCK) for j in range(nf)]
    na = features // F_BLOCK
    nb = len(blocks)
    half = features // 2
    tiles = features // F_BLOCK

    def weights_in():
        copies = [pltpu.make_async_copy(qkv_ref, w.at[u, k, 0, pl.ds(0, 3 * width)], l_sem.at[0]),
                  pltpu.make_async_copy(proj_ref, w.at[u, k, 0, pl.ds(3 * width, width)], l_sem.at[1]),
                  pltpu.make_async_copy(down_ref, w.at[u, k, 2], l_sem.at[2])]
        for i in range(tiles):
            for j in range(nf):
                copies.append(pltpu.make_async_copy(
                    up_ref.at[pl.ds(F_BLOCK * i, F_BLOCK), pl.ds(F_BLOCK * j, F_BLOCK)], probs.at[0, i * nf + j],
                    l_sem.at[3 + i * nf + j]))
        return copies

    def row_copies():
        mine = pl.ds(t * here, here)
        cols = pl.ds(t * own_slots, own_slots)
        return [pltpu.make_async_copy(tok_ref.at[mine], tokb.at[:, cols], o_sem.at[0, 2, 0]),
                pltpu.make_async_copy(og_ref.at[mine], ogb.at[:, cols], o_sem.at[0, 2, 1]),
                pltpu.make_async_copy(ext_ref, extb.at[t], o_sem.at[0, 2, 2]),
                pltpu.make_async_copy(qvb_ref, qvb.at[t], o_sem.at[1, 2, 0])]

    own_w = weights_in()
    for copy in own_w + row_copies():
        copy.start()

    barrier = pltpu.get_barrier_semaphore()
    targets = others + peers
    for target in targets:
        pl.semaphore_signal(barrier, inc=1, device_id=target, device_id_type=MESH)
    pl.semaphore_wait(barrier, len(targets))

    def remote(src, dst, sem, index, target):
        return pltpu.make_async_remote_copy(src_ref=src, dst_ref=dst, send_sem=sem.at[(0, *index)],
                                            recv_sem=sem.at[(1, *index)], device_id=target, device_id_type=MESH)

    def rows_copy(n, i):
        target = others[i]
        mine = pl.ds(target[1] * here, here)
        cols = pl.ds(t * own_slots, own_slots)
        src, dst = (lambda: (tok_ref.at[mine], tokb.at[:, cols]), lambda: (ext_ref, extb.at[t]),
                    lambda: (og_ref.at[mine], ogb.at[:, cols]), lambda: (qvb_ref, qvb.at[t]),
                    lambda: (upb.at[t], upb.at[t]))[n]()
        return remote(src, dst, t_sem, (n, i), target)

    def w_copy(kind, i):
        part, parts, base, rows = blocks[i]
        q, h = rows // 4, rows // 8
        su, start, size, sem, index, target = {
            "y": (u, base + quarter * q, q, y_sem, (i,), side),
            "x": (1 - u, base + quarter * q, q, q_sem, (0, i), across),
            "z": (1 - u, base + quarter * q, q, q_sem, (1, i), along),
            "xf": (1 - u, base + via_z * q, h, f_sem, (0, i), across),
            "zf": (1 - u, base + via_x * q + h, h, f_sem, (1, i), along),
            "co": (u, base, rows, c_sem, (0, i), core),
            "cf": (1 - u, base, rows, c_sem, (1, i), core),
        }[kind]
        view = w.at[su, k, pl.ds(part, parts), pl.ds(aligned(start), size)]
        return remote(view, view, sem, index, target)

    def step1(i):
        w_copy("y", i).wait_recv()
        w_copy("x", i).start()
        w_copy("z", i).start()

    def step2(i):
        w_copy("z", i).wait_recv()
        w_copy("xf", i).start()
        w_copy("x", i).wait_recv()
        w_copy("zf", i).start()

    def step3(i):
        w_copy("xf", i).wait_recv()
        w_copy("zf", i).wait_recv()
        w_copy("cf", i).start()

    def step4(i):
        w_copy("cf", i).wait_recv()
        for kind in ("x", "z", "xf", "zf", "cf"):
            w_copy(kind, i).wait_send()

    def step_own(i):
        w_copy("co", i).wait_recv()
        for kind in ("y", "co"):
            w_copy(kind, i).wait_send()

    def start_rows(n):
        for i in range(N_TP - 1):
            rows_copy(n, i).start()

    def wait_rows(n):
        for i in range(N_TP - 1):
            rows_copy(n, i).wait_recv()

    upb[pl.ds(t, 1), :, :] = row(upb_ref).reshape(1, 1, hidden)
    own_w[0].wait()
    for i in range(na):
        if i == na - 1:
            own_w[1].wait()
        w_copy("y", i).start()
    for n in (1, 3, 4):
        start_rows(n)
    for i in range(na):
        w_copy("co", i).start()
    for copy in own_w[2:]:
        copy.wait()
    for i in range(tiles):
        for j in range(nf):
            w[u, k, 1, j * F_BLOCK : (j + 1) * F_BLOCK, i * F_BLOCK : (i + 1) * F_BLOCK] = probs[0, i * nf + j].T
    for copy in row_copies():
        copy.wait()

    per_clip = slots // ROWS
    sources = ROWS // own_slots

    def rows_at(i):
        return lax.div(i, per_clip), pl.ds(pl.multiple_of(lax.rem(i, per_clip) * ROWS, ROWS), ROWS), pl.ds(
            pl.multiple_of(i * ROWS, ROWS), ROWS)

    def place_rows(i, _):
        b, here_rows, rows = rows_at(i)
        line = lax.broadcasted_iota(jnp.int32, (2 * TABLE, own_slots), 0) & (TABLE - 1)
        pos = []
        for n in range(sources):
            place = extb[lax.rem(i, per_clip) * sources + n, pl.ds(t * here + b, 1), :]
            hot = [jnp.where(line == lax.broadcast_in_dim(v, line.shape, (0, 1)), 1.0, 0.0).astype(BF)
                   for v in (lax.shift_right_logical(place, 6), place & (TABLE - 1))]
            hi = dot(hot[0], table_ref[0 : 2 * TABLE, :], TN)
            lo = dot(hot[1], table_ref[2 * TABLE :, :], TN)
            sh, ch, sl, cl = hi[:, :half], hi[:, half:], lo[:, :half], lo[:, half:]
            pos.append(jnp.concatenate([sh * cl + ch * sl, ch * cl - sh * sl], axis=1))
        stream[rows, :] = jnp.concatenate(pos, axis=0)
        return 0

    def first_rows(i, _):
        b, here_rows, rows = rows_at(i)
        v = tokb[b, here_rows, :].astype(F32) + stream[rows, :]
        stream[rows, :] = v
        xhat, _ = stats(v)
        first[rows, :] = (xhat * row(gain1_ref) + row(bias1_ref)).astype(BF)
        return 0

    step1(0)
    small[...] = jnp.zeros_like(small)
    step1(1)
    start_rows(0)
    step2(0)
    step1(2)
    ff[...] = jnp.zeros_like(ff)
    sg[...] = jnp.zeros_like(sg)
    step2(1)
    step2(2)
    w_copy("y", na).start()
    for n in (1, 3, 4):
        wait_rows(n)
    lax.fori_loop(0, n_rows // ROWS, place_rows, 0)
    wait_rows(0)
    start_rows(2)
    lax.fori_loop(0, n_rows // ROWS, first_rows, 0)
    for i in range(na):
        step_own(i)
    for i in range(na, nb):
        w_copy("co", i).start()

    scale = HD ** -0.5

    def group(n):
        gu, gk = lax.rem(u + lax.div(n, 2), 2), lax.rem(n, 2)
        return gu * 2 + gk, gu, gk

    def qkv_of(n):
        g, gu, gk = group(n)
        out = dot(w[gu, gk, 0, 0 : 3 * width, :], first[...], NT)
        add = jnp.concatenate([qvb[g, :, :], jnp.zeros((6, width), F32)], axis=0)
        add = jnp.concatenate([add, jnp.zeros((8, 64), F32)], axis=1).T
        qkvt[g, 0:width, :] = ((out[0:width] + add[0:width, 0:1]).astype(BF).astype(F32) * scale).astype(BF)
        qkvt[g, width : 2 * width, :] = out[width : 2 * width].astype(BF)
        qkvt[g, 2 * width :, :] = (out[2 * width :] + add[0:width, 1:2]).astype(BF)


    per_group = width // HD

    def attend(n, _):
        @pl.when(n == 1)
        def _():
            for i in range(na):
                step3(i)

        @pl.when(n == 2)
        def _():
            for i in range(na):
                step4(i)

        qkv_of(n)
        g, _, _ = group(n)
        for b in range(here):
            cols = slice(b * slots, (b + 1) * slots)
            visible = count_ref[t * here + b]
            keep = lax.broadcasted_iota(jnp.int32, (slots, slots), 0) < visible
            for r in range(per_group):
                q = qkvt[g, r * HD : (r + 1) * HD, cols]
                key = qkvt[g, width + r * HD : width + (r + 1) * HD, cols]
                value = qkvt[g, 2 * width + r * HD : 2 * width + (r + 1) * HD, cols]
                s = jnp.where(keep, dot(key, q, TN), NEGATIVE)
                e = jnp.exp(s - jnp.max(s, axis=0, keepdims=True))
                p = (e * (1.0 / jnp.sum(e, axis=0, keepdims=True))).astype(BF)
                probs[b, g * per_group + r] = p
                mixed[g, r * HD : (r + 1) * HD, cols] = dot(value, p, NN).astype(BF)

        for at, work in ((0, lambda: (step1(na), w_copy("y", na + 1).start())),
                         (1, lambda: w_copy("y", na + 2).start()), (2, lambda: step2(na))):
            @pl.when(n == at)
            def _():
                work()

        return 0

    lax.fori_loop(0, N_TP, attend, 0)

    def second_rows(i, _):
        _, _, rows = rows_at(i)
        total = stream[rows, :] + row(projb_ref)
        for g in range(N_TP):
            total = total + dot(mixed[g, :, rows], w[g // 2, g % 2, 0, 3 * width :, :], TN)
        middle[rows, :] = total
        xhat, _ = stats(total)
        second[rows, :] = (xhat * row(gain2_ref) + row(bias2_ref)).astype(BF)
        return 0

    lax.fori_loop(0, n_rows // ROWS, second_rows, 0)
    step3(na)
    step_own(na)
    wait_rows(2)

    sums, plan = reduce_plan(n_clips)
    n_all = len(plan)
    f_chunks = nf * 2 * F_BLOCK // CHUNK
    per_f = F_BLOCK // CHUNK

    def place_of(chunk):
        last = div(chunk, f_chunks)
        in_block = mod(chunk, 2 * per_f)
        part = (1 - last) * (1 + mod(in_block, 2))
        row = (1 - last) * (div(chunk, 2 * per_f) * F_BLOCK + div(in_block, 2) * CHUNK)
        return part, row + last * (chunk - f_chunks) * CHUNK

    def kept(stage):
        start = 0
        for kind, bit, rows, halving in sums[:stage]:
            if halving:
                start = start + c_bits[bit] * rows
        return start

    def land_at(stage, chunk):
        return chunk * sum(p[2] for p in sums[2:]) + sum(p[2] for p in sums[2:stage])

    def copy_of(stage, chunk):
        kind, bit, rows, halving = plan[stage]
        base = chunk * CHUNK
        if kind == "core":
            part, row = place_of(chunk)
            src = w.at[:, 1 - k, part, pl.ds(aligned(row), CHUNK)]
            dst, target = core_buf.at[:, pl.ds(aligned(base), CHUNK)], core
        elif kind == "side":
            at = pl.ds(aligned(base), rows)
            src, dst, target = core_buf.at[1 - u, at], side_buf.at[at], side
        elif kind == "reduce":
            start = base + kept(stage)
            if halving:
                start = start + (1 - c_bits[bit]) * rows
            src = side_buf.at[pl.ds(aligned(start), rows)]
            dst, target = land.at[pl.ds(aligned(land_at(stage, chunk)), rows)], peers[bit]
        else:
            part, row = place_of(chunk)
            src = grad_ref.at[part, pl.ds(aligned(row + kept(bit + 3)), rows)]
            dst, target = src, peers[bit]
        send = chunk if kind == "reduce" and not halving else 0
        return pltpu.make_async_remote_copy(
            src_ref=src, dst_ref=dst, send_sem=r_sem.at[0, stage, send], recv_sem=r_sem.at[1, stage, chunk],
            device_id=target, device_id_type=MESH)

    def add(a, b):
        return (a.astype(F32) + b.astype(F32)).astype(BF)

    def finish(stage, chunk):
        copy_of(stage, chunk).wait_recv()
        kind, bit, rows, halving = plan[stage]
        base = chunk * CHUNK
        if kind == "core":
            part, row = place_of(chunk)
            at = pl.ds(aligned(base), CHUNK)
            for n in (0, 1):
                core_buf[n, at] = add(w[n, k, part, pl.ds(aligned(row), CHUNK)], core_buf[n, at])
        elif kind == "side":
            at = pl.ds(aligned(base), rows)
            side_buf[at] = add(core_buf[u, at], side_buf[at])
        elif kind == "reduce":
            at = pl.ds(aligned(base + kept(stage + 1)), rows)
            if not halving:
                copy_of(stage, chunk).wait_send()
            total = add(side_buf[at], land[pl.ds(aligned(land_at(stage, chunk)), rows)])
            if stage == len(sums) - 1:
                part, row = place_of(chunk)
                grad_ref[part, pl.ds(aligned(row + kept(stage + 1)), rows)] = total
            else:
                side_buf[at] = total

    lags = list(LAGS) + [1] * 32
    starts = [sum(lags[:n]) for n in range(n_all + 1)]

    def step(stage, chunk):
        if stage > 0:
            finish(stage - 1, chunk)
        if stage < n_all:
            copy_of(stage, chunk).start()

    def tick(i):
        for stage in range(n_all + 1):
            chunk = i - starts[stage]

            @pl.when((chunk >= 0) & (chunk < n_chunks))
            def _():
                step(stage, chunk)

    def ffn(gu, start, size):
        hid = pl.ds(pl.multiple_of(start, size), size)
        up = w[gu, :, 1, hid, :].reshape(2 * size, features)
        down = w[gu, :, 2, hid, :].reshape(2 * size, features)
        pre = dot(second[...], up, NT) + jnp.concatenate([upb[2 * gu, :, hid], upb[2 * gu + 1, :, hid]], axis=1)
        act, slope = gelu_parts(pre)
        act = act.astype(BF)
        ff[...] += dot(act, down, NN)
        og = ogb[...].reshape(n_rows, features)
        pg = (dot(og, down, NT) * slope).astype(BF)
        sg[...] += dot(pg, up, NN)
        w[gu, :, 2, hid, :] = dot(act, og, TN).astype(BF).reshape(2, size, features)
        w[gu, :, 1, hid, :] = dot(pg, second[...], TN).astype(BF).reshape(2, size, features)
        sums = jnp.sum(pg.astype(F32), axis=0, keepdims=True)
        for gk in (0, 1):
            for m in range(size // 128):
                at = gk * size + m * 128
                upsum[(2 * gu + gk) * (hidden // 128) + lax.div(start, 128) + m] = sums[:, at : at + 128]

    def hooks(i, *work):
        for at, do in work:
            @pl.when(i == at)
            def _():
                do()

    def ffn_block(i, _):
        hooks(i, (0, lambda: step1(na + 1)), (1, lambda: step4(na)),
              (2, lambda: (step_own(na + 1), step2(na + 1), step1(na + 2))),
              (3, lambda: (step3(na + 1), step4(na + 1), step2(na + 2))),
              (4, lambda: (step_own(na + 2), step3(na + 2))), (5, lambda: step4(na + 2)))
        ffn(lax.rem(u + i, 2), lax.div(i, 2) * F_BLOCK, F_BLOCK)

        @pl.when(i >= 1)
        def _():
            tick(2 * i - 2)
            tick(2 * i - 1)

        return 0

    lax.fori_loop(0, nf * 2, ffn_block, 0)
    done = 4 * nf - 2
    for g in range(N_TP):
        for m in range(hidden // 128):
            small[8 + g : 9 + g, m * 128 : (m + 1) * 128] = upsum[g * (hidden // 128) + m]

    def middle_rows(i, _):
        b, here_rows, rows = rows_at(i)
        m = middle[rows, :]
        outp[b, here_rows, :] = (m + ff[rows, :] + row(downb_ref)).astype(BF)
        dv, dgain, dbias = norm_back(m, sg[rows, :], row(gain2_ref))
        og = ogb[b, here_rows, :].astype(F32)
        mg = og + dv
        ff[rows, :] = mg
        bg = mg.astype(BF)
        branch[rows, :] = bg
        small[2:3, :] += dgain
        small[3:4, :] += dbias
        small[4:5, :] += jnp.sum(bg.astype(F32), axis=0, keepdims=True)
        small[5:6, :] += jnp.sum(og, axis=0, keepdims=True)
        return 0

    lax.fori_loop(0, n_rows // ROWS, middle_rows, 0)

    def back_copy(n, i, b):
        src, dst = ((outp, res_ref), (inp, ing_ref))[n]
        target = others[i]
        return remote(src.at[b, pl.ds(target[1] * own_slots, own_slots)], dst.at[t * here + b], b_sem, (n, i, b), target)

    def back_own(n):
        src, dst = ((outp, res_ref), (inp, ing_ref))[n]
        return pltpu.make_async_copy(src.at[:, pl.ds(t * own_slots, own_slots)], dst.at[pl.ds(t * here, here)],
                                     l_sem.at[n])

    back_pieces = [(i, b) for i in range(N_TP - 1) for b in range(here)]

    def send_back(n, at):
        if at == 0:
            back_own(n).start()
        for i, b in back_pieces[at::4]:
            back_copy(n, i, b).start()

    sg[...] = jnp.zeros_like(sg)

    def back_group(g, _):
        gu, gk = lax.div(g, 2), lax.rem(g, 2)
        bg = branch[...]
        dmix = dot(w[gu, gk, 0, 3 * width :, :], bg, NT).astype(BF)
        w[gu, gk, 0, 3 * width :, :] = dot(mixed[g], bg, NN).astype(BF)
        for b in range(here):
            cols = slice(b * slots, (b + 1) * slots)
            for r in range(per_group):
                q_rows = slice(r * HD, (r + 1) * HD)
                k_rows = slice(width + r * HD, width + (r + 1) * HD)
                v_rows = slice(2 * width + r * HD, 2 * width + (r + 1) * HD)
                q, key, value = qkvt[g, q_rows, cols], qkvt[g, k_rows, cols], qkvt[g, v_rows, cols]
                dm = dmix[q_rows, cols]
                p = probs[b, g * per_group + r]
                pf = p.astype(F32)
                dp = dot(value, dm, TN)
                ds = (pf * (dp - jnp.sum(pf * dp, axis=0, keepdims=True))).astype(BF)
                qkvt[g, q_rows, cols] = (dot(key, ds, NN) * scale).astype(BF)
                qkvt[g, k_rows, cols] = dot(q, ds, NT).astype(BF)
                qkvt[g, v_rows, cols] = dot(dm, p, NT).astype(BF)
        dqkv = qkvt[g]
        sg[...] += dot(dqkv, w[gu, gk, 0, 0 : 3 * width, :], TN)
        w[gu, gk, 0, 0 : 3 * width, :] = dot(dqkv, first[...], NN).astype(BF)
        small[pl.ds(12 + g, 1), 0 : 3 * width] = dot(jnp.ones((8, n_rows), BF), dqkv, NT)[0:1]
        @pl.when(lax.rem(g, 2) == 0)
        def _():
            tick(done + lax.div(g, 2))

        return 0

    lax.fori_loop(0, N_TP, back_group, 0)

    def last_rows(i, _):
        b, here_rows, rows = rows_at(i)
        dv, dgain, dbias = norm_back(stream[rows, :], sg[rows, :], row(gain1_ref))
        inp[b, here_rows, :] = (ff[rows, :] + dv).astype(BF)
        small[0:1, :] += dgain
        small[1:2, :] += dbias
        return 0


    small_targets = [core, side] + peers

    def small_copy(i):
        return remote(small, small_buf.at[i], s_sem, (i,), small_targets[i])

    done = done + N_TP // 2

    def small_turn(n):
        if n > len(small_targets):
            return
        if n > 0:
            small_copy(n - 1).wait()
            small[...] += small_buf[n - 1]
        if n < len(small_targets):
            small_copy(n).start()

    def rest_of(i, _):
        tick(i)
        hooks(i, (done, lambda: lax.fori_loop(0, n_rows // ROWS, last_rows, 0)))
        hooks(i, *((done + n, functools.partial(small_turn, n)) for n in range(n_chunks - done)))
        return 0

    lax.fori_loop(done, n_chunks, rest_of, 0)
    state = {}
    for chunk in range(n_chunks):
        stage = max(n for n in range(n_all + 1) if chunk + starts[n] < n_chunks)
        if stage < n_all:
            state[chunk] = stage
    turn = 0
    up_left = True
    small_left = list(range(n_chunks - done, len(small_targets) + 1))
    while state or small_left:
        for n, piece in BACK.get(("t", turn), ()):
            send_back(n, piece)
        if small_left:
            small_turn(small_left.pop(0))
        for chunk in sorted(state, reverse=True):
            state[chunk] += 1
            step(state[chunk], chunk)
            if state[chunk] == n_all:
                del state[chunk]
        if up_left and not [chunk for chunk in state if chunk < f_chunks]:
            up_left = False
            for m in range(tiles):
                for j in range(nf):
                    upg_ref[m * F_BLOCK : (m + 1) * F_BLOCK, j * F_BLOCK : (j + 1) * F_BLOCK] = grad_ref[
                        1, j * F_BLOCK : (j + 1) * F_BLOCK, m * F_BLOCK : (m + 1) * F_BLOCK].T
        turn += 1
    small_ref[0:6, :] = small[0:6, :]
    small_ref[6:7, :] = small[pl.ds(8 + t, 1), :]
    small_ref[7:8, :] = small[pl.ds(12 + t, 1), :]

    for n in (0, 1):
        for i, b in back_pieces:
            back_copy(n, i, b).wait_recv()
            back_copy(n, i, b).wait_send()
        back_own(n).wait()
    for n in range(5):
        for i in range(N_TP - 1):
            rows_copy(n, i).wait_send()

    for stage, (kind, _, rows, halving) in enumerate(plan):
        if kind != "reduce" or halving:
            view = core_buf if kind == "core" else side_buf.at[pl.ds(0, n_chunks * rows)]
            pltpu.make_async_remote_copy(
                src_ref=view, dst_ref=view, send_sem=r_sem.at[0, stage, 0], recv_sem=r_sem.at[1, stage, 0],
                device_id=core, device_id_type=MESH).wait_send()


def layer_call(n_clips, counts, tok, ext, og, proj, qkv, up, down, vectors, qv_bias, table):
    count, own_slots, features = tok.shape
    width = proj.shape[0]
    hidden = up.shape[1]
    here = count // N_TP
    slots = own_slots * N_TP
    n_rows = here * slots
    nf = hidden // F_BLOCK
    n_chunks = 3 * features // CHUNK
    heads = features // HD
    bits = n_clips.bit_length() - 1
    sums, plan = reduce_plan(n_clips)
    n_all = len(plan)
    hbm = pl.BlockSpec(memory_space=pl.ANY)
    vmem = pl.BlockSpec(memory_space=pltpu.VMEM)
    smem = pl.BlockSpec(memory_space=pltpu.SMEM)
    dma = pltpu.SemaphoreType.DMA
    nb = nf + features // F_BLOCK
    return pl.pallas_call(
        functools.partial(layer_kernel, (here, slots, width, hidden, features), n_clips),
        out_shape=(
            jax.ShapeDtypeStruct((3, features, features), BF),
            jax.ShapeDtypeStruct((features, hidden), BF),
            jax.ShapeDtypeStruct((8, features), F32),
            jax.ShapeDtypeStruct((count, own_slots, features), BF),
            jax.ShapeDtypeStruct((count, own_slots, features), BF),
        ),
        in_specs=[smem, hbm, vmem] + [hbm] * 5 + [vmem] * 9,
        out_specs=(vmem, vmem, vmem, hbm, hbm),
        scratch_shapes=[
            pltpu.VMEM((2, 2, 3, features, features), BF),
            pltpu.VMEM((here, slots, features), BF),
            pltpu.VMEM((N_TP, *ext.shape), jnp.int32),
            pltpu.VMEM((here, slots, features), BF),
            pltpu.VMEM((N_TP, *qv_bias.shape), F32),
            pltpu.VMEM((N_TP, 1, hidden), F32),
            pltpu.VMEM((n_rows, features), F32),
            pltpu.VMEM((n_rows, features), BF),
            pltpu.VMEM((N_TP, 3 * width, n_rows), BF),
            pltpu.VMEM((here, heads, slots, slots), BF),
            pltpu.VMEM((N_TP, width, n_rows), BF),
            pltpu.VMEM((n_rows, features), F32),
            pltpu.VMEM((n_rows, features), BF),
            pltpu.VMEM((n_rows, features), F32),
            pltpu.VMEM((n_rows, features), F32),
            pltpu.VMEM((n_rows, features), BF),
            pltpu.VMEM((here, slots, features), BF),
            pltpu.VMEM((here, slots, features), BF),
            pltpu.VMEM((2, 3 * features, features), BF),
            pltpu.VMEM((3 * features, features), BF),
            pltpu.VMEM((n_chunks * sum(p[2] for p in sums[2:]), features), BF),
            pltpu.VMEM((16, features), F32),
            pltpu.VMEM((N_TP * hidden // 128, 1, 128), F32),
            pltpu.VMEM((2 + bits, 16, features), F32),
            dma((3 + nf * features // F_BLOCK,)),
            dma((2, 5, N_TP - 1)),
            dma((2, nb)),
            dma((2, 2, nb)),
            dma((2, 2, nb)),
            dma((2, 2, nb)),
            dma((2, n_all, n_chunks)),
            dma((2, 2 + bits)),
            dma((2, 3, N_TP - 1)),
            dma((2, 2, N_TP - 1, here)),
        ],
        compiler_params=pltpu.CompilerParams(collective_id=0, has_side_effects=True, vmem_limit_bytes=VMEM_LIMIT),
        name="encoder_layer",
    )(counts, tok, ext, og, proj, qkv, up, down, *vectors, qv_bias, table)


def widen_kernel(qkv_ref, proj_ref, down_ref, up_ref, out_ref, in_ref, small_ref, qkvo_ref, projo_ref, downo_ref,
                 upo_ref, outo_ref, ino_ref, qvo_ref, g1_ref, b1_ref, g2_ref, b2_ref, pb_ref, db_ref, ub_ref):
    for src, dst in ((qkv_ref, qkvo_ref), (proj_ref, projo_ref), (down_ref, downo_ref)):
        dst[...] = src[0].astype(F32)
    for src, dst in ((up_ref, upo_ref), (out_ref, outo_ref), (in_ref, ino_ref)):
        dst[...] = src[...].astype(F32)
    width = qvo_ref.shape[1]

    @pl.when(pl.program_id(0) == 0)
    def _():
        for i, ref in enumerate((g1_ref, b1_ref, g2_ref, b2_ref, pb_ref, db_ref, ub_ref)):
            ref[...] = small_ref[i, :]
        qvo_ref[0:1, :] = small_ref[7:8, 0:width]
        qvo_ref[1:2, :] = small_ref[7:8, 2 * width : 3 * width]


def widen_call(grads, up_grad, small, rows_out, rows_in, width):
    _, features, _ = grads.shape
    hidden = up_grad.shape[1]
    count, own_slots, _ = rows_out.shape
    steps = 2
    whole = pl.BlockSpec(memory_space=pltpu.VMEM)

    def rows_of(rows, first):
        return pl.BlockSpec((1, rows // steps, features), lambda i: (first[0], first[1] // (rows // steps) + i, 0))

    def flat(rows, cols):
        return pl.BlockSpec((rows // steps, cols), lambda i: (i, 0))

    clips = pl.BlockSpec((count // steps, own_slots, features), lambda i: (i, 0, 0))
    vector = jax.ShapeDtypeStruct((features,), F32)
    return pl.pallas_call(
        widen_kernel,
        grid=(steps,),
        out_shape=(
            jax.ShapeDtypeStruct((3 * width, features), F32),
            jax.ShapeDtypeStruct((width, features), F32),
            jax.ShapeDtypeStruct((hidden, features), F32),
            jax.ShapeDtypeStruct((features, hidden), F32),
            jax.ShapeDtypeStruct((count, own_slots, features), F32),
            jax.ShapeDtypeStruct((count, own_slots, features), F32),
            jax.ShapeDtypeStruct((2, width), F32),
        ) + (vector,) * 6 + (jax.ShapeDtypeStruct((hidden,), F32),),
        in_specs=[rows_of(3 * width, (0, 0)), rows_of(width, (0, 3 * width)), rows_of(hidden, (2, 0)),
                  flat(features, hidden), clips, clips, whole],
        out_specs=(flat(3 * width, features), flat(width, features), flat(hidden, features), flat(features, hidden),
                   clips, clips) + (whole,) * 8,
        compiler_params=pltpu.CompilerParams(vmem_limit_bytes=VMEM_LIMIT),
        name="widen",
    )(grads, grads, grads, up_grad, rows_out, rows_in, small)


def place_table(features, largest):
    half = features // 2
    freq = np.exp(-math.log(10000.0) * np.arange(half, dtype=np.float64) / half).astype(np.float32).astype(np.float64)
    parts = []
    for step in (TABLE, 1):
        angle = step * np.arange(TABLE, dtype=np.float64)[:, None] * freq
        values = np.concatenate([np.sin(angle), np.cos(angle)], axis=1).astype(np.float32)
        high = values.astype(BF)
        parts += [high, (values - high.astype(np.float32)).astype(BF)]
    return np.concatenate(parts, axis=0)


def per_device(n_clips, tokens, tubelet_index, visible_count, norm1_gain, norm1_bias, qkv_weight, qv_bias,
               proj_weight, proj_bias, norm2_gain, norm2_bias, up_weight, up_bias, down_weight, down_bias, out_grad):
    count, rows, features = tokens.shape
    width = qkv_weight.shape[2]
    hidden = up_weight.shape[1]
    qkv_t = jnp.transpose(qkv_weight, (1, 2, 0)).reshape(3 * width, features)
    vectors = (norm1_gain, norm1_bias, norm2_gain, norm2_bias, proj_bias, down_bias, up_bias)
    table = jnp.asarray(place_table(features, 2560))
    grads, up_grad, small, rows_out, rows_in = layer_call(
        n_clips, visible_count, tokens, tubelet_index, out_grad, proj_weight, qkv_t, up_weight, down_weight, vectors, qv_bias,
        table)
    qkv_grad, proj_grad, down_grad, up_grad, rows_out, rows_in, qv_grad, g1, b1, g2, b2, pb, db, ub = widen_call(
        grads, up_grad, small, rows_out, rows_in, width)
    qkv_grad = jnp.transpose(qkv_grad.reshape(3, width, features), (2, 0, 1))
    return rows_out, rows_in, g1, b1, qkv_grad, qv_grad, proj_grad, pb, g2, b2, up_grad, ub, down_grad, db


def solution(mesh):
    placed = (
        P("clips", "tp", None), P("clips", "tp"), P("clips"), P(), P(), P(None, None, "tp"), P(None, "tp"),
        P("tp", None), P(), P(), P(), P(None, "tp"), P("tp"), P("tp", None), P(), P("clips", "tp", None),
    )
    return jax.shard_map(
        functools.partial(per_device, mesh.shape["clips"]),
        mesh=mesh,
        in_specs=placed,
        out_specs=(
            P("clips", "tp", None), P("clips", "tp", None), P(), P(), P(None, None, "tp"), P(None, "tp"),
            P("tp", None), P(), P(), P(), P(None, "tp"), P("tp"), P("tp", None), P(),
        ),
        check_vma=False,
    )
```

```python
import functools
import math

import jax
import jax.numpy as jnp
import numpy as np
from jax import lax
from jax.experimental import pallas as pl
from jax.experimental.pallas import tpu as pltpu
from jax.sharding import PartitionSpec as P

HD = 64
EPSILON = 1e-06
NEGATIVE = -1000000000.0
BF = jnp.bfloat16
F32 = jnp.float32
MESH = pl.DeviceIdType.MESH
VMEM_LIMIT = 62 * 2**20
CHUNK = 128
F_BLOCK = 256
ROWS = 128
N_TP = 4
TABLE = 64
NN = (((1,), (0,)), ((), ()))
NT = (((1,), (1,)), ((), ()))
TN = (((0,), (0,)), ((), ()))


def dot(a, b, dims):
    return lax.dot_general(a, b, dims, preferred_element_type=F32)


def flip(value, weight):
    return value + weight - 2 * weight * lax.rem(lax.div(value, weight), 2)


def bit_of(value, weight):
    return lax.rem(lax.div(value, weight), 2)


def row(ref):
    return ref[...].reshape(1, ref.shape[0])


def div(value, by):
    return value // by if isinstance(value, int) else lax.div(value, by)


def mod(value, by):
    return value % by if isinstance(value, int) else lax.rem(value, by)


def aligned(value, multiple=16):
    return value if isinstance(value, int) else pl.multiple_of(value, multiple)


def gelu_parts(x):
    e = jnp.exp(-0.5 * x * x)
    z = jnp.abs(x) * (0.3275911 / math.sqrt(2.0))
    r = 1.0 / (1.0 + z)
    poly = r * (0.254829592 + r * (-0.284496736 + r * (1.421413741 + r * (-1.453152027 + r * 1.061405429))))
    tail = 0.5 * poly * e
    cdf = jnp.where(x >= 0, 1.0 - tail, tail)
    return x * cdf, cdf + x * (e * (1.0 / math.sqrt(2.0 * math.pi)))


def stats(v):
    mean = jnp.mean(v, axis=-1, keepdims=True)
    center = v - mean
    rstd = lax.rsqrt(jnp.mean(center * center, axis=-1, keepdims=True) + EPSILON)
    return center * rstd, rstd


def norm_back(v, dy, gain):
    xhat, rstd = stats(v)
    dx = dy * gain
    m1 = jnp.mean(dx, axis=-1, keepdims=True)
    m2 = jnp.mean(dx * xhat, axis=-1, keepdims=True)
    return (dx - m1 - xhat * m2) * rstd, jnp.sum(dy * xhat, axis=0, keepdims=True), jnp.sum(dy, axis=0, keepdims=True)


LAGS = (1, 2, 1, 1, 1, 1, 1, 2)
BACK = {("t", 2): [(n, piece) for n in (0, 1) for piece in range(4)]}


def reduce_plan(n_clips):
    plan = [("core", 0, CHUNK, False), ("side", 0, CHUNK, False)]
    rows = CHUNK
    gathers = []
    for bit in range(n_clips.bit_length() - 1):
        halving = rows >= 32
        if halving:
            rows //= 2
            gathers.append(("gather", bit, rows, True))
        plan.append(("reduce", bit, rows, halving))
    return plan, plan + gathers[::-1]


def layer_kernel(dims, n_clips, count_ref, tok_ref, ext_ref, og_ref, proj_ref, qkv_ref, up_ref, down_ref,
                 gain1_ref, bias1_ref, gain2_ref, bias2_ref, projb_ref, downb_ref, upb_ref, qvb_ref, table_ref,
                 grad_out, up_out, small_ref, res_ref, ing_ref,
                 w, tokb, extb, ogb, qvb, upb, stream, first, qkvt, probs, mixed, middle, second, ff, sg, branch, outp,
                 inp, core_buf, side_buf, land, grad_ref, upg_ref, small, upsum, small_buf, l_sem, t_sem, y_sem, q_sem, f_sem, c_sem,
                 r_sem, s_sem, o_sem, b_sem):
    here, slots, width, hidden, features = dims
    bits = n_clips.bit_length() - 1
    c = lax.axis_index("clips")
    t = lax.axis_index("tp")
    k, u = bit_of(t, 1), bit_of(t, 2)
    core = (c, flip(t, 1))
    side = (c, flip(t, 2))
    across = (flip(c, 1), t)
    along = (flip(c, 2), t)
    others = [(c, lax.rem(t + i, N_TP)) for i in range(1, N_TP)]
    peers = [(flip(c, 2 ** bit), t) for bit in range(bits)]
    c_bits = [bit_of(c, 2 ** bit) for bit in range(bits)]
    own_slots = slots // N_TP
    n_rows = here * slots
    nf = hidden // F_BLOCK
    n_chunks = 3 * features // CHUNK
    b0, b1 = bit_of(c, 1), bit_of(c, 2)
    quarter = b1 * 2 + b0
    via_z = (1 - b1) * 2 + b0
    via_x = b1 * 2 + (1 - b0)
    blocks = [(0, 1, F_BLOCK * j, F_BLOCK) for j in range(features // F_BLOCK)] + [
        (1, 2, F_BLOCK * j, F_BLOCK) for j in range(nf)]
    na = features // F_BLOCK
    nb = len(blocks)
    half = features // 2
    tiles = features // F_BLOCK

    def weights_in():
        copies = [pltpu.make_async_copy(qkv_ref, w.at[u, k, 0, pl.ds(0, 3 * width)], l_sem.at[0]),
                  pltpu.make_async_copy(proj_ref, w.at[u, k, 0, pl.ds(3 * width, width)], l_sem.at[1]),
                  pltpu.make_async_copy(down_ref, w.at[u, k, 2], l_sem.at[2])]
        for i in range(tiles):
            for j in range(nf):
                copies.append(pltpu.make_async_copy(
                    up_ref.at[pl.ds(F_BLOCK * i, F_BLOCK), pl.ds(F_BLOCK * j, F_BLOCK)], probs.at[0, i * nf + j],
                    l_sem.at[3 + i * nf + j]))
        return copies

    def row_copies():
        mine = pl.ds(t * here, here)
        cols = pl.ds(t * own_slots, own_slots)
        return [pltpu.make_async_copy(tok_ref.at[mine], tokb.at[:, cols], o_sem.at[0, 2, 0]),
                pltpu.make_async_copy(og_ref.at[mine], ogb.at[:, cols], o_sem.at[0, 2, 1]),
                pltpu.make_async_copy(ext_ref, extb.at[t], o_sem.at[0, 2, 2]),
                pltpu.make_async_copy(qvb_ref, qvb.at[t], o_sem.at[1, 2, 0])]

    own_w = weights_in()
    for copy in own_w + row_copies():
        copy.start()

    barrier = pltpu.get_barrier_semaphore()
    targets = others + peers
    for target in targets:
        pl.semaphore_signal(barrier, inc=1, device_id=target, device_id_type=MESH)
    pl.semaphore_wait(barrier, len(targets))

    def remote(src, dst, sem, index, target):
        return pltpu.make_async_remote_copy(src_ref=src, dst_ref=dst, send_sem=sem.at[(0, *index)],
                                            recv_sem=sem.at[(1, *index)], device_id=target, device_id_type=MESH)

    def rows_copy(n, i):
        target = others[i]
        mine = pl.ds(target[1] * here, here)
        cols = pl.ds(t * own_slots, own_slots)
        src, dst = (lambda: (tok_ref.at[mine], tokb.at[:, cols]), lambda: (ext_ref, extb.at[t]),
                    lambda: (og_ref.at[mine], ogb.at[:, cols]), lambda: (qvb_ref, qvb.at[t]),
                    lambda: (upb.at[t], upb.at[t]))[n]()
        return remote(src, dst, t_sem, (n, i), target)

    def w_copy(kind, i):
        part, parts, base, rows = blocks[i]
        q, h = rows // 4, rows // 8
        su, start, size, sem, index, target = {
            "y": (u, base + quarter * q, q, y_sem, (i,), side),
            "x": (1 - u, base + quarter * q, q, q_sem, (0, i), across),
            "z": (1 - u, base + quarter * q, q, q_sem, (1, i), along),
            "xf": (1 - u, base + via_z * q, h, f_sem, (0, i), across),
            "zf": (1 - u, base + via_x * q + h, h, f_sem, (1, i), along),
            "co": (u, base, rows, c_sem, (0, i), core),
            "cf": (1 - u, base, rows, c_sem, (1, i), core),
        }[kind]
        view = w.at[su, k, pl.ds(part, parts), pl.ds(aligned(start), size)]
        return remote(view, view, sem, index, target)

    def step1(i):
        w_copy("y", i).wait_recv()
        w_copy("x", i).start()
        w_copy("z", i).start()

    def step2(i):
        w_copy("z", i).wait_recv()
        w_copy("xf", i).start()
        w_copy("x", i).wait_recv()
        w_copy("zf", i).start()

    def step3(i):
        w_copy("xf", i).wait_recv()
        w_copy("zf", i).wait_recv()
        w_copy("cf", i).start()

    def step4(i):
        w_copy("cf", i).wait_recv()
        for kind in ("x", "z", "xf", "zf", "cf"):
            w_copy(kind, i).wait_send()

    def step_own(i):
        w_copy("co", i).wait_recv()
        for kind in ("y", "co"):
            w_copy(kind, i).wait_send()

    def start_rows(n):
        for i in range(N_TP - 1):
            rows_copy(n, i).start()

    def wait_rows(n):
        for i in range(N_TP - 1):
            rows_copy(n, i).wait_recv()

    upb[pl.ds(t, 1), :, :] = row(upb_ref).reshape(1, 1, hidden)
    own_w[0].wait()
    for i in range(na):
        if i == na - 1:
            own_w[1].wait()
        w_copy("y", i).start()
    for n in (1, 3, 4):
        start_rows(n)
    for i in range(na):
        w_copy("co", i).start()
    for copy in own_w[2:]:
        copy.wait()
    for i in range(tiles):
        for j in range(nf):
            w[u, k, 1, j * F_BLOCK : (j + 1) * F_BLOCK, i * F_BLOCK : (i + 1) * F_BLOCK] = probs[0, i * nf + j].T
    for copy in row_copies():
        copy.wait()

    per_clip = slots // ROWS
    sources = ROWS // own_slots

    def rows_at(i):
        return lax.div(i, per_clip), pl.ds(pl.multiple_of(lax.rem(i, per_clip) * ROWS, ROWS), ROWS), pl.ds(
            pl.multiple_of(i * ROWS, ROWS), ROWS)

    def place_rows(i, _):
        b, here_rows, rows = rows_at(i)
        line = lax.broadcasted_iota(jnp.int32, (2 * TABLE, own_slots), 0) & (TABLE - 1)
        pos = []
        for n in range(sources):
            place = extb[lax.rem(i, per_clip) * sources + n, pl.ds(t * here + b, 1), :]
            hot = [jnp.where(line == lax.broadcast_in_dim(v, line.shape, (0, 1)), 1.0, 0.0).astype(BF)
                   for v in (lax.shift_right_logical(place, 6), place & (TABLE - 1))]
            hi = dot(hot[0], table_ref[0 : 2 * TABLE, :], TN)
            lo = dot(hot[1], table_ref[2 * TABLE :, :], TN)
            sh, ch, sl, cl = hi[:, :half], hi[:, half:], lo[:, :half], lo[:, half:]
            pos.append(jnp.concatenate([sh * cl + ch * sl, ch * cl - sh * sl], axis=1))
        stream[rows, :] = jnp.concatenate(pos, axis=0)
        return 0

    def first_rows(i, _):
        b, here_rows, rows = rows_at(i)
        v = tokb[b, here_rows, :].astype(F32) + stream[rows, :]
        stream[rows, :] = v
        xhat, _ = stats(v)
        first[rows, :] = (xhat * row(gain1_ref) + row(bias1_ref)).astype(BF)
        return 0

    step1(0)
    small[...] = jnp.zeros_like(small)
    step1(1)
    start_rows(0)
    step2(0)
    step1(2)
    ff[...] = jnp.zeros_like(ff)
    sg[...] = jnp.zeros_like(sg)
    step2(1)
    step2(2)
    w_copy("y", na).start()
    for n in (1, 3, 4):
        wait_rows(n)
    lax.fori_loop(0, n_rows // ROWS, place_rows, 0)
    wait_rows(0)
    start_rows(2)
    lax.fori_loop(0, n_rows // ROWS, first_rows, 0)
    for i in range(na):
        step_own(i)
    for i in range(na, nb):
        w_copy("co", i).start()

    scale = HD ** -0.5

    def group(n):
        gu, gk = lax.rem(u + lax.div(n, 2), 2), lax.rem(n, 2)
        return gu * 2 + gk, gu, gk

    def qkv_of(n):
        g, gu, gk = group(n)
        out = dot(w[gu, gk, 0, 0 : 3 * width, :], first[...], NT)
        add = jnp.concatenate([qvb[g, :, :], jnp.zeros((6, width), F32)], axis=0)
        add = jnp.concatenate([add, jnp.zeros((8, 64), F32)], axis=1).T
        qkvt[g, 0:width, :] = ((out[0:width] + add[0:width, 0:1]).astype(BF).astype(F32) * scale).astype(BF)
        qkvt[g, width : 2 * width, :] = out[width : 2 * width].astype(BF)
        qkvt[g, 2 * width :, :] = (out[2 * width :] + add[0:width, 1:2]).astype(BF)


    per_group = width // HD

    def attend(n, _):
        @pl.when(n == 1)
        def _():
            for i in range(na):
                step3(i)

        @pl.when(n == 2)
        def _():
            for i in range(na):
                step4(i)

        qkv_of(n)
        g, _, _ = group(n)
        for b in range(here):
            cols = slice(b * slots, (b + 1) * slots)
            visible = count_ref[t * here + b]
            keep = lax.broadcasted_iota(jnp.int32, (slots, slots), 0) < visible
            for r in range(per_group):
                q = qkvt[g, r * HD : (r + 1) * HD, cols]
                key = qkvt[g, width + r * HD : width + (r + 1) * HD, cols]
                value = qkvt[g, 2 * width + r * HD : 2 * width + (r + 1) * HD, cols]
                s = jnp.where(keep, dot(key, q, TN), NEGATIVE)
                e = jnp.exp(s - jnp.max(s, axis=0, keepdims=True))
                p = (e * (1.0 / jnp.sum(e, axis=0, keepdims=True))).astype(BF)
                probs[b, g * per_group + r] = p
                mixed[g, r * HD : (r + 1) * HD, cols] = dot(value, p, NN).astype(BF)

        for at, work in ((0, lambda: (step1(na), w_copy("y", na + 1).start())),
                         (1, lambda: w_copy("y", na + 2).start()), (2, lambda: step2(na))):
            @pl.when(n == at)
            def _():
                work()

        return 0

    lax.fori_loop(0, N_TP, attend, 0)

    def second_rows(i, _):
        _, _, rows = rows_at(i)
        total = stream[rows, :] + row(projb_ref)
        for g in range(N_TP):
            total = total + dot(mixed[g, :, rows], w[g // 2, g % 2, 0, 3 * width :, :], TN)
        middle[rows, :] = total
        xhat, _ = stats(total)
        second[rows, :] = (xhat * row(gain2_ref) + row(bias2_ref)).astype(BF)
        return 0

    lax.fori_loop(0, n_rows // ROWS, second_rows, 0)
    step3(na)
    step_own(na)
    wait_rows(2)

    sums, plan = reduce_plan(n_clips)
    n_all = len(plan)
    f_chunks = nf * 2 * F_BLOCK // CHUNK
    per_f = F_BLOCK // CHUNK

    def place_of(chunk):
        last = div(chunk, f_chunks)
        in_block = mod(chunk, 2 * per_f)
        part = (1 - last) * (1 + mod(in_block, 2))
        row = (1 - last) * (div(chunk, 2 * per_f) * F_BLOCK + div(in_block, 2) * CHUNK)
        return part, row + last * (chunk - f_chunks) * CHUNK

    def kept(stage):
        start = 0
        for kind, bit, rows, halving in sums[:stage]:
            if halving:
                start = start + c_bits[bit] * rows
        return start

    def land_at(stage, chunk):
        return chunk * sum(p[2] for p in sums[2:]) + sum(p[2] for p in sums[2:stage])

    def copy_of(stage, chunk):
        kind, bit, rows, halving = plan[stage]
        base = chunk * CHUNK
        if kind == "core":
            part, row = place_of(chunk)
            src = w.at[:, 1 - k, part, pl.ds(aligned(row), CHUNK)]
            dst, target = core_buf.at[:, pl.ds(aligned(base), CHUNK)], core
        elif kind == "side":
            at = pl.ds(aligned(base), rows)
            src, dst, target = core_buf.at[1 - u, at], side_buf.at[at], side
        elif kind == "reduce":
            start = base + kept(stage)
            if halving:
                start = start + (1 - c_bits[bit]) * rows
            src = side_buf.at[pl.ds(aligned(start), rows)]
            dst, target = land.at[pl.ds(aligned(land_at(stage, chunk)), rows)], peers[bit]
        else:
            part, row = place_of(chunk)
            src = grad_ref.at[part, pl.ds(aligned(row + kept(bit + 3)), rows)]
            dst, target = src, peers[bit]
        send = chunk if kind == "reduce" and not halving else 0
        return pltpu.make_async_remote_copy(
            src_ref=src, dst_ref=dst, send_sem=r_sem.at[0, stage, send], recv_sem=r_sem.at[1, stage, chunk],
            device_id=target, device_id_type=MESH)

    def add(a, b):
        return (a.astype(F32) + b.astype(F32)).astype(BF)

    def finish(stage, chunk):
        copy_of(stage, chunk).wait_recv()
        kind, bit, rows, halving = plan[stage]
        base = chunk * CHUNK
        if kind == "core":
            part, row = place_of(chunk)
            at = pl.ds(aligned(base), CHUNK)
            for n in (0, 1):
                core_buf[n, at] = add(w[n, k, part, pl.ds(aligned(row), CHUNK)], core_buf[n, at])
        elif kind == "side":
            at = pl.ds(aligned(base), rows)
            side_buf[at] = add(core_buf[u, at], side_buf[at])
        elif kind == "reduce":
            at = pl.ds(aligned(base + kept(stage + 1)), rows)
            if not halving:
                copy_of(stage, chunk).wait_send()
            total = add(side_buf[at], land[pl.ds(aligned(land_at(stage, chunk)), rows)])
            if stage == len(sums) - 1:
                part, row = place_of(chunk)
                grad_ref[part, pl.ds(aligned(row + kept(stage + 1)), rows)] = total
            else:
                side_buf[at] = total

    lags = list(LAGS) + [1] * 32
    starts = [sum(lags[:n]) for n in range(n_all + 1)]

    def step(stage, chunk):
        if stage > 0:
            finish(stage - 1, chunk)
        if stage < n_all:
            copy_of(stage, chunk).start()

    def tick(i):
        for stage in range(n_all + 1):
            chunk = i - starts[stage]

            @pl.when((chunk >= 0) & (chunk < n_chunks))
            def _():
                step(stage, chunk)

    def ffn(gu, start, size):
        hid = pl.ds(pl.multiple_of(start, size), size)
        up = w[gu, :, 1, hid, :].reshape(2 * size, features)
        down = w[gu, :, 2, hid, :].reshape(2 * size, features)
        pre = dot(second[...], up, NT) + jnp.concatenate([upb[2 * gu, :, hid], upb[2 * gu + 1, :, hid]], axis=1)
        act, slope = gelu_parts(pre)
        act = act.astype(BF)
        ff[...] += dot(act, down, NN)
        og = ogb[...].reshape(n_rows, features)
        pg = (dot(og, down, NT) * slope).astype(BF)
        sg[...] += dot(pg, up, NN)
        w[gu, :, 2, hid, :] = dot(act, og, TN).astype(BF).reshape(2, size, features)
        w[gu, :, 1, hid, :] = dot(pg, second[...], TN).astype(BF).reshape(2, size, features)
        sums = jnp.sum(pg.astype(F32), axis=0, keepdims=True)
        for gk in (0, 1):
            for m in range(size // 128):
                at = gk * size + m * 128
                upsum[(2 * gu + gk) * (hidden // 128) + lax.div(start, 128) + m] = sums[:, at : at + 128]

    def hooks(i, *work):
        for at, do in work:
            @pl.when(i == at)
            def _():
                do()

    def ffn_block(i, _):
        hooks(i, (0, lambda: step1(na + 1)), (1, lambda: step4(na)),
              (2, lambda: (step_own(na + 1), step2(na + 1), step1(na + 2))),
              (3, lambda: (step3(na + 1), step4(na + 1), step2(na + 2))),
              (4, lambda: (step_own(na + 2), step3(na + 2))), (5, lambda: step4(na + 2)))
        ffn(lax.rem(u + i, 2), lax.div(i, 2) * F_BLOCK, F_BLOCK)

        @pl.when(i >= 1)
        def _():
            tick(2 * i - 2)
            tick(2 * i - 1)

        return 0

    lax.fori_loop(0, nf * 2, ffn_block, 0)
    done = 4 * nf - 2
    for g in range(N_TP):
        for m in range(hidden // 128):
            small[8 + g : 9 + g, m * 128 : (m + 1) * 128] = upsum[g * (hidden // 128) + m]

    def middle_rows(i, _):
        b, here_rows, rows = rows_at(i)
        m = middle[rows, :]
        outp[b, here_rows, :] = (m + ff[rows, :] + row(downb_ref)).astype(BF)
        dv, dgain, dbias = norm_back(m, sg[rows, :], row(gain2_ref))
        og = ogb[b, here_rows, :].astype(F32)
        mg = og + dv
        ff[rows, :] = mg
        bg = mg.astype(BF)
        branch[rows, :] = bg
        small[2:3, :] += dgain
        small[3:4, :] += dbias
        small[4:5, :] += jnp.sum(bg.astype(F32), axis=0, keepdims=True)
        small[5:6, :] += jnp.sum(og, axis=0, keepdims=True)
        return 0

    lax.fori_loop(0, n_rows // ROWS, middle_rows, 0)

    def back_copy(n, i, b):
        src, dst = ((outp, res_ref), (inp, ing_ref))[n]
        target = others[i]
        return remote(src.at[b, pl.ds(target[1] * own_slots, own_slots)], dst.at[t * here + b], b_sem, (n, i, b), target)

    def back_own(n):
        src, dst = ((outp, res_ref), (inp, ing_ref))[n]
        return pltpu.make_async_copy(src.at[:, pl.ds(t * own_slots, own_slots)], dst.at[pl.ds(t * here, here)],
                                     l_sem.at[n])

    back_pieces = [(i, b) for i in range(N_TP - 1) for b in range(here)]

    def send_back(n, at):
        if at == 0:
            back_own(n).start()
        for i, b in back_pieces[at::4]:
            back_copy(n, i, b).start()

    sg[...] = jnp.zeros_like(sg)

    def back_group(g, _):
        gu, gk = lax.div(g, 2), lax.rem(g, 2)
        bg = branch[...]
        dmix = dot(w[gu, gk, 0, 3 * width :, :], bg, NT).astype(BF)
        w[gu, gk, 0, 3 * width :, :] = dot(mixed[g], bg, NN).astype(BF)
        for b in range(here):
            cols = slice(b * slots, (b + 1) * slots)
            for r in range(per_group):
                q_rows = slice(r * HD, (r + 1) * HD)
                k_rows = slice(width + r * HD, width + (r + 1) * HD)
                v_rows = slice(2 * width + r * HD, 2 * width + (r + 1) * HD)
                q, key, value = qkvt[g, q_rows, cols], qkvt[g, k_rows, cols], qkvt[g, v_rows, cols]
                dm = dmix[q_rows, cols]
                p = probs[b, g * per_group + r]
                pf = p.astype(F32)
                dp = dot(value, dm, TN)
                ds = (pf * (dp - jnp.sum(pf * dp, axis=0, keepdims=True))).astype(BF)
                qkvt[g, q_rows, cols] = (dot(key, ds, NN) * scale).astype(BF)
                qkvt[g, k_rows, cols] = dot(q, ds, NT).astype(BF)
                qkvt[g, v_rows, cols] = dot(dm, p, NT).astype(BF)
        dqkv = qkvt[g]
        sg[...] += dot(dqkv, w[gu, gk, 0, 0 : 3 * width, :], TN)
        w[gu, gk, 0, 0 : 3 * width, :] = dot(dqkv, first[...], NN).astype(BF)
        small[pl.ds(12 + g, 1), 0 : 3 * width] = dot(jnp.ones((8, n_rows), BF), dqkv, NT)[0:1]
        @pl.when(lax.rem(g, 2) == 0)
        def _():
            tick(done + lax.div(g, 2))

        return 0

    lax.fori_loop(0, N_TP, back_group, 0)

    def last_rows(i, _):
        b, here_rows, rows = rows_at(i)
        dv, dgain, dbias = norm_back(stream[rows, :], sg[rows, :], row(gain1_ref))
        inp[b, here_rows, :] = (ff[rows, :] + dv).astype(BF)
        small[0:1, :] += dgain
        small[1:2, :] += dbias
        return 0


    small_targets = [core, side] + peers

    def small_copy(i):
        return remote(small, small_buf.at[i], s_sem, (i,), small_targets[i])

    done = done + N_TP // 2

    def small_turn(n):
        if n > len(small_targets):
            return
        if n > 0:
            small_copy(n - 1).wait()
            small[...] += small_buf[n - 1]
        if n < len(small_targets):
            small_copy(n).start()

    def rest_of(i, _):
        tick(i)
        hooks(i, (done, lambda: lax.fori_loop(0, n_rows // ROWS, last_rows, 0)))
        hooks(i, *((done + n, functools.partial(small_turn, n)) for n in range(n_chunks - done)))
        return 0

    lax.fori_loop(done, n_chunks, rest_of, 0)
    state = {}
    for chunk in range(n_chunks):
        stage = max(n for n in range(n_all + 1) if chunk + starts[n] < n_chunks)
        if stage < n_all:
            state[chunk] = stage
    turn = 0
    up_left = True
    out_copies = [pltpu.make_async_copy(grad_ref.at[2], grad_out.at[2], l_sem.at[2]),
                  pltpu.make_async_copy(upg_ref, up_out, l_sem.at[3]),
                  pltpu.make_async_copy(grad_ref.at[0], grad_out.at[0], l_sem.at[4])]
    small_left = list(range(n_chunks - done, len(small_targets) + 1))
    while state or small_left:
        for n, piece in BACK.get(("t", turn), ()):
            send_back(n, piece)
        if small_left:
            small_turn(small_left.pop(0))
        for chunk in sorted(state, reverse=True):
            state[chunk] += 1
            step(state[chunk], chunk)
            if state[chunk] == n_all:
                del state[chunk]
        if up_left and not [chunk for chunk in state if chunk < f_chunks]:
            up_left = False
            for m in range(tiles):
                for j in range(nf):
                    upg_ref[m * F_BLOCK : (m + 1) * F_BLOCK, j * F_BLOCK : (j + 1) * F_BLOCK] = grad_ref[
                        1, j * F_BLOCK : (j + 1) * F_BLOCK, m * F_BLOCK : (m + 1) * F_BLOCK].T
            out_copies[0].start()
            out_copies[1].start()
        turn += 1
    out_copies[2].start()
    small_ref[0:6, :] = small[0:6, :]
    small_ref[6:7, :] = small[pl.ds(8 + t, 1), :]
    small_ref[7:8, :] = small[pl.ds(12 + t, 1), :]

    for n in (0, 1):
        for i, b in back_pieces:
            back_copy(n, i, b).wait_recv()
            back_copy(n, i, b).wait_send()
        back_own(n).wait()
    for n in range(5):
        for i in range(N_TP - 1):
            rows_copy(n, i).wait_send()

    for copy in out_copies:
        copy.wait()
    for stage, (kind, _, rows, halving) in enumerate(plan):
        if kind != "reduce" or halving:
            view = core_buf if kind == "core" else side_buf.at[pl.ds(0, n_chunks * rows)]
            pltpu.make_async_remote_copy(
                src_ref=view, dst_ref=view, send_sem=r_sem.at[0, stage, 0], recv_sem=r_sem.at[1, stage, 0],
                device_id=core, device_id_type=MESH).wait_send()


def layer_call(n_clips, counts, tok, ext, og, proj, qkv, up, down, vectors, qv_bias, table):
    count, own_slots, features = tok.shape
    width = proj.shape[0]
    hidden = up.shape[1]
    here = count // N_TP
    slots = own_slots * N_TP
    n_rows = here * slots
    nf = hidden // F_BLOCK
    n_chunks = 3 * features // CHUNK
    heads = features // HD
    bits = n_clips.bit_length() - 1
    sums, plan = reduce_plan(n_clips)
    n_all = len(plan)
    hbm = pl.BlockSpec(memory_space=pl.ANY)
    vmem = pl.BlockSpec(memory_space=pltpu.VMEM)
    smem = pl.BlockSpec(memory_space=pltpu.SMEM)
    dma = pltpu.SemaphoreType.DMA
    nb = nf + features // F_BLOCK
    return pl.pallas_call(
        functools.partial(layer_kernel, (here, slots, width, hidden, features), n_clips),
        out_shape=(
            jax.ShapeDtypeStruct((3, features, features), BF),
            jax.ShapeDtypeStruct((features, hidden), BF),
            jax.ShapeDtypeStruct((8, features), F32),
            jax.ShapeDtypeStruct((count, own_slots, features), BF),
            jax.ShapeDtypeStruct((count, own_slots, features), BF),
        ),
        in_specs=[smem, hbm, vmem] + [hbm] * 5 + [vmem] * 9,
        out_specs=(hbm, hbm, vmem, hbm, hbm),
        scratch_shapes=[
            pltpu.VMEM((2, 2, 3, features, features), BF),
            pltpu.VMEM((here, slots, features), BF),
            pltpu.VMEM((N_TP, *ext.shape), jnp.int32),
            pltpu.VMEM((here, slots, features), BF),
            pltpu.VMEM((N_TP, *qv_bias.shape), F32),
            pltpu.VMEM((N_TP, 1, hidden), F32),
            pltpu.VMEM((n_rows, features), F32),
            pltpu.VMEM((n_rows, features), BF),
            pltpu.VMEM((N_TP, 3 * width, n_rows), BF),
            pltpu.VMEM((here, heads, slots, slots), BF),
            pltpu.VMEM((N_TP, width, n_rows), BF),
            pltpu.VMEM((n_rows, features), F32),
            pltpu.VMEM((n_rows, features), BF),
            pltpu.VMEM((n_rows, features), F32),
            pltpu.VMEM((n_rows, features), F32),
            pltpu.VMEM((n_rows, features), BF),
            pltpu.VMEM((here, slots, features), BF),
            pltpu.VMEM((here, slots, features), BF),
            pltpu.VMEM((2, 3 * features, features), BF),
            pltpu.VMEM((3 * features, features), BF),
            pltpu.VMEM((n_chunks * sum(p[2] for p in sums[2:]), features), BF),
            pltpu.VMEM((3, features, features), BF),
            pltpu.VMEM((features, hidden), BF),
            pltpu.VMEM((16, features), F32),
            pltpu.VMEM((N_TP * hidden // 128, 1, 128), F32),
            pltpu.VMEM((2 + bits, 16, features), F32),
            dma((3 + nf * features // F_BLOCK,)),
            dma((2, 5, N_TP - 1)),
            dma((2, nb)),
            dma((2, 2, nb)),
            dma((2, 2, nb)),
            dma((2, 2, nb)),
            dma((2, n_all, n_chunks)),
            dma((2, 2 + bits)),
            dma((2, 3, N_TP - 1)),
            dma((2, 2, N_TP - 1, here)),
        ],
        compiler_params=pltpu.CompilerParams(collective_id=0, has_side_effects=True, vmem_limit_bytes=VMEM_LIMIT),
        name="encoder_layer",
    )(counts, tok, ext, og, proj, qkv, up, down, *vectors, qv_bias, table)


def widen_kernel(qkv_ref, proj_ref, down_ref, up_ref, out_ref, in_ref, small_ref, qkvo_ref, projo_ref, downo_ref,
                 upo_ref, outo_ref, ino_ref, qvo_ref, g1_ref, b1_ref, g2_ref, b2_ref, pb_ref, db_ref, ub_ref):
    for src, dst in ((qkv_ref, qkvo_ref), (proj_ref, projo_ref), (down_ref, downo_ref)):
        dst[...] = src[0].astype(F32)
    for src, dst in ((up_ref, upo_ref), (out_ref, outo_ref), (in_ref, ino_ref)):
        dst[...] = src[...].astype(F32)
    width = qvo_ref.shape[1]

    @pl.when(pl.program_id(0) == 0)
    def _():
        for i, ref in enumerate((g1_ref, b1_ref, g2_ref, b2_ref, pb_ref, db_ref, ub_ref)):
            ref[...] = small_ref[i, :]
        qvo_ref[0:1, :] = small_ref[7:8, 0:width]
        qvo_ref[1:2, :] = small_ref[7:8, 2 * width : 3 * width]


def widen_call(grads, up_grad, small, rows_out, rows_in, width):
    _, features, _ = grads.shape
    hidden = up_grad.shape[1]
    count, own_slots, _ = rows_out.shape
    steps = 2
    whole = pl.BlockSpec(memory_space=pltpu.VMEM)

    def rows_of(rows, first):
        return pl.BlockSpec((1, rows // steps, features), lambda i: (first[0], first[1] // (rows // steps) + i, 0))

    def flat(rows, cols):
        return pl.BlockSpec((rows // steps, cols), lambda i: (i, 0))

    clips = pl.BlockSpec((count // steps, own_slots, features), lambda i: (i, 0, 0))
    vector = jax.ShapeDtypeStruct((features,), F32)
    return pl.pallas_call(
        widen_kernel,
        grid=(steps,),
        out_shape=(
            jax.ShapeDtypeStruct((3 * width, features), F32),
            jax.ShapeDtypeStruct((width, features), F32),
            jax.ShapeDtypeStruct((hidden, features), F32),
            jax.ShapeDtypeStruct((features, hidden), F32),
            jax.ShapeDtypeStruct((count, own_slots, features), F32),
            jax.ShapeDtypeStruct((count, own_slots, features), F32),
            jax.ShapeDtypeStruct((2, width), F32),
        ) + (vector,) * 6 + (jax.ShapeDtypeStruct((hidden,), F32),),
        in_specs=[rows_of(3 * width, (0, 0)), rows_of(width, (0, 3 * width)), rows_of(hidden, (2, 0)),
                  flat(features, hidden), clips, clips, whole],
        out_specs=(flat(3 * width, features), flat(width, features), flat(hidden, features), flat(features, hidden),
                   clips, clips) + (whole,) * 8,
        compiler_params=pltpu.CompilerParams(vmem_limit_bytes=VMEM_LIMIT),
        name="widen",
    )(grads, grads, grads, up_grad, rows_out, rows_in, small)


def place_table(features, largest):
    half = features // 2
    freq = np.exp(-math.log(10000.0) * np.arange(half, dtype=np.float64) / half).astype(np.float32).astype(np.float64)
    parts = []
    for step in (TABLE, 1):
        angle = step * np.arange(TABLE, dtype=np.float64)[:, None] * freq
        values = np.concatenate([np.sin(angle), np.cos(angle)], axis=1).astype(np.float32)
        high = values.astype(BF)
        parts += [high, (values - high.astype(np.float32)).astype(BF)]
    return np.concatenate(parts, axis=0)


def per_device(n_clips, tokens, tubelet_index, visible_count, norm1_gain, norm1_bias, qkv_weight, qv_bias,
               proj_weight, proj_bias, norm2_gain, norm2_bias, up_weight, up_bias, down_weight, down_bias, out_grad):
    count, rows, features = tokens.shape
    width = qkv_weight.shape[2]
    hidden = up_weight.shape[1]
    qkv_t = jnp.transpose(qkv_weight, (1, 2, 0)).reshape(3 * width, features)
    vectors = (norm1_gain, norm1_bias, norm2_gain, norm2_bias, proj_bias, down_bias, up_bias)
    table = jnp.asarray(place_table(features, 2560))
    grads, up_grad, small, rows_out, rows_in = layer_call(
        n_clips, visible_count, tokens, tubelet_index, out_grad, proj_weight, qkv_t, up_weight, down_weight, vectors, qv_bias,
        table)
    qkv_grad, proj_grad, down_grad, up_grad, rows_out, rows_in, qv_grad, g1, b1, g2, b2, pb, db, ub = widen_call(
        grads, up_grad, small, rows_out, rows_in, width)
    qkv_grad = jnp.transpose(qkv_grad.reshape(3, width, features), (2, 0, 1))
    return rows_out, rows_in, g1, b1, qkv_grad, qv_grad, proj_grad, pb, g2, b2, up_grad, ub, down_grad, db


def solution(mesh):
    placed = (
        P("clips", "tp", None), P("clips", "tp"), P("clips"), P(), P(), P(None, None, "tp"), P(None, "tp"),
        P("tp", None), P(), P(), P(), P(None, "tp"), P("tp"), P("tp", None), P(), P("clips", "tp", None),
    )
    return jax.shard_map(
        functools.partial(per_device, mesh.shape["clips"]),
        mesh=mesh,
        in_specs=placed,
        out_specs=(
            P("clips", "tp", None), P("clips", "tp", None), P(), P(), P(None, None, "tp"), P(None, "tp"),
            P("tp", None), P(), P(), P(), P(None, "tp"), P("tp"), P("tp", None), P(),
        ),
        check_vma=False,
    )
```
